128 devices in a mesh: ctx: 32 (over y, x_lo, z), fsdp: 4 (over x_hi, core).
Axes of the slice: x: 4 (x_hi: 2, x_lo: 2; x = x_hi * 2 + x_lo), y: 4, z: 4, core: 2. Of those that a mesh axis runs over, the one named last changes fastest.
Arguments:
- tokens: bfloat16 [4, 4096, 768], P('fsdp', 'ctx'), may hold values from -6 to 6
- cotangent: bfloat16 [4, 4096, 768], P('fsdp', 'ctx'), may hold values from -6 to 6
- positions: int32 [4, 4096], P('fsdp'), may hold values from 0 to 4095, as said below
- vectors: float32 [13, 768], replicated, may hold values from -1.2 to 1.6, as said below
- vectors_moment: float32 [13, 768], replicated, may hold values from -64 to 64
- vectors_second: float32 [13, 768], replicated, may hold values from 425.984 to 1638.4
- qkv_weight: float32 [768, 2304], P('fsdp'), may hold values from -0.3125 to 0.3125
- qkv_moment: float32 [768, 2304], P('fsdp'), may hold values from -40 to 40
- qkv_second: float32 [768, 2304], P('fsdp'), may hold values from 212.992 to 868.352
- dense_weight: float32 [768, 768], P('fsdp'), may hold values from -1.25 to 1.25
- dense_moment: float32 [768, 768], P('fsdp'), may hold values from -14 to 14
- dense_second: float32 [768, 768], P('fsdp'), may hold values from 19.6608 to 78.6432
- up_weight: float32 [768, 3072], P('fsdp'), may hold values from -0.21875 to 0.21875
- up_moment: float32 [768, 3072], P('fsdp'), may hold values from -24 to 24
- up_second: float32 [768, 3072], P('fsdp'), may hold values from 78.6432 to 311.296
- down_weight: float32 [3072, 768], P('fsdp'), may hold values from -0.109375 to 0.109375
- down_moment: float32 [3072, 768], P('fsdp'), may hold values from -56 to 56
- down_second: float32 [3072, 768], P('fsdp'), may hold values from 360.448 to 1474.56
Outputs:
- block_out: bfloat16 [4, 4096, 768], P('fsdp', 'ctx')
- input_grad: float32 [4, 4096, 768], P('fsdp', 'ctx')
- vectors_new: float32 [13, 768], replicated
- vectors_moment_new: float32 [13, 768], replicated
- vectors_second_new: float32 [13, 768], replicated
- qkv_new: float32 [768, 2304], P('fsdp')
- qkv_moment_new: float32 [768, 2304], P('fsdp')
- qkv_second_new: float32 [768, 2304], P('fsdp')
- dense_new: float32 [768, 768], P('fsdp')
- dense_moment_new: float32 [768, 768], P('fsdp')
- dense_second_new: float32 [768, 768], P('fsdp')
- up_new: float32 [768, 3072], P('fsdp')
- up_moment_new: float32 [768, 3072], P('fsdp')
- up_second_new: float32 [768, 3072], P('fsdp')
- down_new: float32 [3072, 768], P('fsdp')
- down_moment_new: float32 [3072, 768], P('fsdp')
- down_second_new: float32 [3072, 768], P('fsdp')
The draws below stay inside these ranges and needn't reach their ends.
Inputs may be any that keep to these rules, and one draw needn't show every extreme that they name: Each row is a permutation of the positions of one sequence, made of blocks of 64 consecutive positions; each run of 128 stored tokens holds block j and block 63 - j for some j, in either order. `vectors`: rows 0 and 2 are gains near 1; the other rows are biases of both signs.
All inputs are finite; a program needn't handle non-finite values.
Results may differ from the reference program's by a relative error of at most 0.01.
The reference program's roundings to bfloat16 on the way count: a program that leaves them out, or rounds other values in their place, can miss the bound.
Values may be sent and summed in bfloat16 or wider, within the bound.
A program may use at most 256 MiB of HBM per device.

```python
import math
import jax
import jax.numpy as jnp
from jax import lax

D = 768
HEADS = 12
HEAD = 64
FF = 3072
ROT = 16
VECS = 13
STEP = 10
LENGTH = 4096
SEQS = 4
BLOCK = 64
TOKENS = 16384


def draw_positions(key, part):
    key = jax.random.fold_in(key, 5)
    pair_count = LENGTH // (2 * BLOCK)

    def one_sequence(seq_key):
        order_key, flip_key = jax.random.split(seq_key)
        pair_order = jax.random.permutation(order_key, pair_count)
        flip_bits = jax.random.randint(flip_key, (pair_count,), 0, 2)
        mirror = 2 * pair_count - 1 - pair_order
        lead_block = jnp.where(flip_bits == 1, mirror, pair_order)
        second = pair_order + mirror - lead_block
        blocks = jnp.stack([lead_block, second], 1).reshape(-1)
        offset = jnp.arange(LENGTH)
        return (blocks[offset // BLOCK] * BLOCK + offset % BLOCK).astype(jnp.int32)
    return jax.vmap(one_sequence)(jax.random.split(key, SEQS))


def draw_vectors(key, part):
    key = jax.random.fold_in(key, 11)
    noise = jnp.clip(jax.random.normal(key, (VECS, D), jnp.float32), -4.0, 4.0)
    row_index = jnp.arange(VECS)[:, None]
    gain_rows = (row_index == 0) | (row_index == 2)
    return jnp.where(gain_rows, 1.0 + 0.15 * noise, 0.3 * noise)


def shard_levels(rng, extent, shards, smallest, high):
    def one(axis_at, shards_of):
        draws = jax.random.uniform(jax.random.fold_in(jax.random.fold_in(rng, 6), axis_at), (shards_of,), jnp.float32, smallest / len(shards), high / len(shards))
        return jnp.repeat(jnp.exp(draws), extent[axis_at] // shards_of).reshape((-1,) + (1,) * (len(extent) - axis_at - 1))

    gain = one(*shards[0])
    for cut in shards[1:]:
        gain = gain * one(*cut)
    return gain


def normal_values(stream_key, dims, scale, reach, cuts=(), kind=jnp.bfloat16):
    gain = shard_levels(stream_key, dims, cuts, -0.22, 0.18) if cuts else 1.0
    entries = jax.random.normal(stream_key, dims, jnp.float32) * scale * gain
    return jnp.minimum(jnp.maximum(entries, -reach), reach).astype(kind)


def setup_inputs(seed: int = 0) -> dict:
    seeds = jax.random.split(jax.random.key(seed), 19)
    tokens = normal_values(seeds[0], (SEQS, LENGTH, D), 1.0, 6.0, ((0, 4), (1, 32)))
    cotangent = normal_values(seeds[1], (SEQS, LENGTH, D), 1.0, 6.0, ((0, 4), (1, 32)))
    positions = draw_positions(jax.random.fold_in(seeds[18], 71), 0)
    vectors = draw_vectors(jax.random.fold_in(seeds[18], 71), 0)
    vectors_moment = normal_values(seeds[4], (VECS, D), (0.077 * TOKENS ** 0.5), 64.0, (), jnp.float32)
    vectors_second = jnp.clip(jnp.exp(jax.random.uniform(seeds[5], (VECS, D), jnp.float32, math.log(425.984), math.log(1638.4))), 425.984, 1638.4)
    qkv_weight = normal_values(seeds[6], (D, 3 * D), (D // 2) ** -0.5, 0.3125, ((0, 4),), jnp.float32)
    qkv_moment = normal_values(seeds[7], (D, 3 * D), (0.055 * TOKENS ** 0.5), 40.0, ((0, 4),), jnp.float32)
    qkv_second = jnp.clip(jnp.exp(math.log(868.352) - 1.40534252 * jax.random.uniform(seeds[8], (D, 3 * D), jnp.float32) ** shard_levels(seeds[8], (D, 3 * D), ((0, 4),), -0.2, 0.2)), 212.992, 868.352)
    dense_weight = normal_values(seeds[9], (D, D), (D // 32) ** -0.5, 1.25, ((0, 4),), jnp.float32)
    dense_moment = normal_values(seeds[10], (D, D), (0.017 * TOKENS ** 0.5), 14.0, ((0, 4),), jnp.float32)
    dense_second = jnp.clip(jnp.exp(math.log(78.6432) - 1.3862944 * jax.random.uniform(seeds[11], (D, D), jnp.float32) ** shard_levels(seeds[11], (D, D), ((0, 4),), -0.2, 0.2)), 19.6608, 78.6432)
    up_weight = normal_values(seeds[12], (D, FF), D ** -0.5, 0.21875, ((0, 4),), jnp.float32)
    up_moment = normal_values(seeds[13], (D, FF), (0.033 * TOKENS ** 0.5), 24.0, ((0, 4),), jnp.float32)
    up_second = jnp.clip(jnp.exp(math.log(311.296) - 1.375823 * jax.random.uniform(seeds[14], (D, FF), jnp.float32) ** shard_levels(seeds[14], (D, FF), ((0, 4),), -0.2, 0.2)), 78.6432, 311.296)
    down_weight = normal_values(seeds[15], (FF, D), FF ** -0.5, 0.109375, ((0, 4),), jnp.float32)
    down_moment = normal_values(seeds[16], (FF, D), (0.072 * TOKENS ** 0.5), 56.0, ((0, 4),), jnp.float32)
    down_second = jnp.clip(jnp.exp(math.log(1474.56) - 1.40876726 * jax.random.uniform(seeds[17], (FF, D), jnp.float32) ** shard_levels(seeds[17], (FF, D), ((0, 4),), -0.2, 0.2)), 360.448, 1474.56)
    return dict(tokens=tokens, cotangent=cotangent, positions=positions, vectors=vectors, vectors_moment=vectors_moment, vectors_second=vectors_second, qkv_weight=qkv_weight, qkv_moment=qkv_moment, qkv_second=qkv_second, dense_weight=dense_weight, dense_moment=dense_moment, dense_second=dense_second, up_weight=up_weight, up_moment=up_moment, up_second=up_second, down_weight=down_weight, down_moment=down_moment, down_second=down_second)


@jax.custom_vjp
def low(v):
    return lax.optimization_barrier(v.astype(jnp.bfloat16)).astype(jnp.float32)

@jax.custom_vjp
def low_back(v):
    return v

def low_keep(v):
    return (low(v), None)

def low_pass(kept, grad):
    return (grad,)

def back_keep(v):
    return (v, None)

def back_low(kept, grad):
    return (low(grad),)
low.defvjp(low_keep, low_pass)
low_back.defvjp(back_keep, back_low)
masked = -1e+30
norm_eps = 1e-05
adam_eps = 1e-08
beta_first = 0.9
beta_second = 0.95

def product(left, right):
    return jnp.dot(left, right, precision=lax.Precision.HIGHEST)

def angle_tables(places):
    half_rot = ROT // 2
    frequency = 10000.0 ** (-(jnp.arange(half_rot, dtype=jnp.float32) * 2.0 / ROT))
    angles = places.astype(jnp.float32)[:, None] * frequency[None, :]
    return (jnp.cos(angles), jnp.sin(angles))

def rotate(values, cos_part, sin_part):
    half_rot = cos_part.shape[-1]
    cos_wide = cos_part[:, None, :]
    sin_wide = sin_part[:, None, :]
    low_half = values[..., :half_rot]
    high_half = values[..., half_rot:2 * half_rot]
    rest_part = values[..., 2 * half_rot:]
    return jnp.concatenate([low_half * cos_wide - high_half * sin_wide, high_half * cos_wide + low_half * sin_wide, rest_part], -1)

def layer_norm(inputs, gain_row, shift_row):
    centered = inputs - lax.optimization_barrier(jnp.mean(inputs, -1, keepdims=True))
    inv_scale = lax.rsqrt(lax.optimization_barrier(jnp.mean(centered * centered, -1, keepdims=True)) + norm_eps)
    return centered * inv_scale * gain_row + shift_row

def attention(queries, keys, values, places):
    seq_length = queries.shape[0]
    block_rows = math.gcd(512, seq_length)
    block_count = seq_length // block_rows

    def one_block(sliced):
        query_block, place_block = sliced
        scores = low_back(jnp.einsum('qhd,khd->hqk', query_block, keys, precision=lax.Precision.HIGHEST) * 0.125)
        visible = places[None, None, :] <= place_block[None, :, None]
        scores = jnp.where(visible, scores, masked)
        log_total = jax.nn.logsumexp(scores, -1, keepdims=True)
        soft_weights = low(jnp.exp(scores - log_total))
        return jnp.einsum('hqk,khd->qhd', soft_weights, values, precision=lax.Precision.HIGHEST)
    result = lax.map(jax.checkpoint(one_block), (queries.reshape(block_count, block_rows, HEADS, HEAD), places.reshape(block_count, block_rows)))
    return result.reshape(seq_length, HEADS, HEAD)

def one_layer(params, inputs, places):
    vectors, qkv_weight, dense_weight, up_weight, down_weight = params
    seq_length = inputs.shape[0]
    cos_part, sin_part = angle_tables(places)
    ln_a = low(layer_norm(inputs, vectors[0], vectors[1]))
    ln_b = low(layer_norm(inputs, vectors[2], vectors[3]))
    linear = low_back(product(ln_a, low(qkv_weight)) + vectors[4:7].reshape(-1))
    query_pre = linear[:, :D].reshape(seq_length, HEADS, HEAD)
    key_pre = linear[:, D:2 * D].reshape(seq_length, HEADS, HEAD)
    value_pre = linear[:, 2 * D:].reshape(seq_length, HEADS, HEAD)
    queries = low(rotate(query_pre, cos_part, sin_part))
    keys = low(rotate(key_pre, cos_part, sin_part))
    values = low(value_pre)
    attended = low(low_back(attention(queries, keys, values, places).reshape(seq_length, D)))
    attn_out = product(attended, low(dense_weight)) + vectors[7]
    hidden = low_back(product(ln_b, low(up_weight)) + vectors[8:12].reshape(-1))
    gelu_low = low(jax.nn.gelu(hidden, approximate=False))
    mlp_out = product(gelu_low, low(down_weight)) + vectors[12]
    return inputs + attn_out + mlp_out

def adamw(weight, moment, second, gradient, step_rate, decay_rate):
    moment_new = beta_first * moment + (1.0 - beta_first) * gradient
    second_new = beta_second * second + (1.0 - beta_second) * gradient * gradient
    corrected_first = moment_new / (1.0 - beta_first ** STEP)
    corrected_second = second_new / (1.0 - beta_second ** STEP)
    weight_new = weight - step_rate * (corrected_first / (jnp.sqrt(corrected_second) + adam_eps) + decay_rate * weight)
    return (weight_new, moment_new, second_new)

def reference(tokens, cotangent, positions, vectors, vectors_moment, vectors_second, qkv_weight, qkv_moment, qkv_second, dense_weight, dense_moment, dense_second, up_weight, up_moment, up_second, down_weight, down_moment, down_second):
    params = (vectors, qkv_weight, dense_weight, up_weight, down_weight)
    zeros_tree = jax.tree.map(jnp.zeros_like, params)

    def per_sequence(totals, sliced):
        seq_tokens, seq_cotangent, seq_places = sliced
        result, pull_back = jax.vjp(lambda weights, inputs: one_layer(weights, inputs, seq_places), params, seq_tokens.astype(jnp.float32))
        grad_params, grad_inputs = pull_back(seq_cotangent.astype(jnp.float32))
        return (jax.tree.map(jnp.add, totals, grad_params), (result.astype(jnp.bfloat16), grad_inputs))
    totals, (block_out, input_grad) = lax.scan(per_sequence, zeros_tree, (tokens, cotangent, positions))
    grad_vectors, grad_qkv, grad_dense, grad_up, grad_down = totals
    vec_new = adamw(vectors, vectors_moment, vectors_second, grad_vectors, 0.2, 0.0)
    qkv_out = adamw(qkv_weight, qkv_moment, qkv_second, grad_qkv, 0.03, 0.1)
    dense_out = adamw(dense_weight, dense_moment, dense_second, grad_dense, 0.1, 0.1)
    up_out = adamw(up_weight, up_moment, up_second, grad_up, 0.03, 0.1)
    down_out = adamw(down_weight, down_moment, down_second, grad_down, 0.02, 0.1)
    return (block_out, input_grad, vec_new[0], vec_new[1], vec_new[2], qkv_out[0], qkv_out[1], qkv_out[2], dense_out[0], dense_out[1], dense_out[2], up_out[0], up_out[1], up_out[2], down_out[0], down_out[1], down_out[2])
```

```python
import jax
import jax.numpy as jnp
from jax import lax
from jax.experimental import pallas as pl
from jax.experimental.pallas import tpu as pltpu
from jax.sharding import PartitionSpec as P

HEADS = 12
ROT = 16
STEP = 10
MESH = pl.DeviceIdType.MESH
F32 = jnp.float32
LOW = jnp.bfloat16
VMEM_LIMIT = 56 * 1024 * 1024

masked = -1e30
norm_eps = 1e-05
adam_eps = 1e-08
beta_first = 0.9
beta_second = 0.95
log2e = 1.4426950408889634


def ctx_of(y, xl, z):
    return (lax.rem(y, 4) * 2 + lax.rem(xl, 2)) * 4 + lax.rem(z, 4)


def place():
    ctx = lax.axis_index("ctx")
    fs = lax.axis_index("fsdp")
    c = lax.div(ctx, 4)
    return ctx, fs, lax.div(c, 2), lax.rem(c, 2), lax.rem(ctx, 4)


def greet(devices):
    barrier = pltpu.get_barrier_semaphore()
    for device in devices:
        pl.semaphore_signal(barrier, inc=1, device_id=device, device_id_type=MESH)
    pl.semaphore_wait(barrier, len(devices))


class Wire:
    def __init__(self, send_sem, recv_sem, local_sem):
        self.send_sem, self.recv_sem, self.local_sem = send_sem, recv_sem, local_sem
        self.sent, self.kept, self.local, self.count = [], [], 0, 0

    def send(self, src, dst, device):
        at = self.count
        self.count += 1
        copy = pltpu.make_async_remote_copy(
            src_ref=src,
            dst_ref=dst,
            send_sem=self.send_sem.at[at],
            recv_sem=self.recv_sem.at[at],
            device_id=device,
            device_id_type=MESH,
        )
        copy.start()
        self.sent.append(copy)
        return copy

    def left(self, *copies):
        for copy in copies:
            copy.wait_send()
        self.sent = [s for s in self.sent if not any(s is c for c in copies)]

    def keep(self, src, dst):
        copy = pltpu.make_async_copy(src, dst, self.local_sem.at[self.local])
        self.local += 1
        copy.start()
        self.kept.append(copy)
        return copy

    def finish(self):
        for copy in self.sent:
            copy.wait_send()
        for copy in self.kept:
            copy.wait()


def eight_peers(y, xl, z, fs):
    return [
        (ctx_of(lax.rem(y + 1, 4), xl, z), fs),
        (ctx_of(lax.rem(y + 3, 4), xl, z), fs),
        (ctx_of(y, 1 - xl, z), fs),
    ]


def erf(x):
    x = jnp.clip(x, -3.832506856900711, 3.832506856900711)
    s = x * x
    top = jnp.full_like(x, 0.00022905065861350646)
    for k in (0.0034082910107109506, 0.050955695062380861, 0.18520832239976145, 1.128379143519084):
        top = top * s + k
    low = jnp.full_like(x, -1.1791602954361697e-7)
    for k in (0.000023547966471313185, 0.0010179625278914885, 0.014070470171167667, 0.11098505178285362, 0.49746925110067538, 1.0):
        low = low * s + k
    return x * top / low


def lanes(rows, width=128):
    return lax.broadcasted_iota(jnp.int32, (rows, width), 1)


def turn(u, cos_wide, sin_wide):
    lane = lanes(u.shape[0])
    up = pltpu.roll(u, 120, 1) * jnp.where(lane < 8, -sin_wide, 0.0)
    down = pltpu.roll(u, 8, 1) * jnp.where(lane < 8, 0.0, sin_wide)
    return u * cos_wide + up + down


def angle_lanes(start, rows):
    lane = lanes(rows)
    row = lax.broadcasted_iota(jnp.int32, (rows, 128), 0)
    spot = lax.rem(row, 64)
    for i, first in enumerate(start):
        spot = spot + jnp.where(lax.div(row, 64) == i, first, 0)
    power = lax.rem(lane, 8).astype(F32) * (2.0 / ROT)
    frequency = jnp.where(lane < ROT, jnp.exp(power * -9.210340371976184), 0.0)
    angle = spot.astype(F32) * frequency
    return jnp.cos(angle), jnp.sin(angle)


class Spread:
    def __init__(self, wire, piece, out, where):
        self.wire, self.piece, self.out, self.w = wire, piece, out, where

    def around(self, slab, halves):
        w, wire = self.w, self.wire
        me = slab(w.c)
        a, b = wire.send(me, me, w.north), wire.send(me, me, w.south)
        x = wire.send(me, me, w.side)
        yield
        x.wait_recv()
        mate = slab(w.c_mate)
        p1, p2 = wire.send(mate, mate, w.north), wire.send(mate, mate, w.south)
        a.wait_recv()
        part = halves(slab(w.c_south), 0)
        h1 = wire.send(part, part, w.north)
        b.wait_recv()
        part = halves(slab(w.c_north), 1)
        h2 = wire.send(part, part, w.south)
        yield
        h1.wait_recv()
        h2.wait_recv()
        far = slab(w.c_far)
        last = wire.send(far, far, w.side)
        yield
        for copy in (p1, p2, last):
            copy.wait_recv()

    def eight_first(self):
        w, wire, out = self.w, self.wire, self.out
        width = out.shape[-1]
        own = wire.keep(self.piece, out.at[w.z, w.c])
        own.wait()
        wire.kept = [k for k in wire.kept if k is not own]
        for _ in self.around(lambda c: out.at[w.z, c], lambda r, h: r.at[:, pl.ds(h * width // 2, width // 2)]):
            yield
        mine = out.at[w.z]
        a, b = wire.send(mine, mine, w.up), wire.send(mine, mine, w.down)
        yield
        a.wait_recv()
        part = out.at[w.zm, pl.ds(0, 4)]
        h1 = wire.send(part, part, w.up)
        b.wait_recv()
        part = out.at[w.zp, pl.ds(4, 4)]
        h2 = wire.send(part, part, w.down)
        yield
        h1.wait_recv()
        h2.wait_recv()

    def ring_first(self):
        w, wire, out = self.w, self.wire, self.out
        own = wire.keep(self.piece, out.at[w.c, w.z])
        copies = [wire.send(self.piece, out.at[w.c, w.z], d) for d in (w.opposite, w.up, w.down)]
        yield
        own.wait()
        wire.kept = [k for k in wire.kept if k is not own]
        for copy in copies:
            copy.wait_recv()
        for _ in self.around(lambda c: out.at[c], lambda r, h: r.at[pl.ds(2 * h, 2)]):
            yield


class Where:
    def __init__(self):
        ctx, fs, y, xl, z = place()
        self.ctx, self.fs, self.y, self.xl, self.z = ctx, fs, y, xl, z
        self.core, self.xh = lax.rem(fs, 2), lax.div(fs, 2)
        yp, ym, yo = lax.rem(y + 1, 4), lax.rem(y + 3, 4), lax.rem(y + 2, 4)
        self.zp, self.zm, self.zo = lax.rem(z + 1, 4), lax.rem(z + 3, 4), lax.rem(z + 2, 4)
        self.c, self.c_mate = y * 2 + xl, y * 2 + 1 - xl
        self.c_north, self.c_south, self.c_far = yp * 2 + xl, ym * 2 + xl, yo * 2 + xl
        self.c_north_mate, self.c_south_mate = yp * 2 + 1 - xl, ym * 2 + 1 - xl
        self.c_far_mate = yo * 2 + 1 - xl
        self.north, self.south, self.side = eight_peers(y, xl, z, fs)
        self.up, self.down = (ctx_of(y, xl, self.zp), fs), (ctx_of(y, xl, self.zm), fs)
        self.opposite = (ctx_of(y, xl, self.zo), fs)
        self.twin = (ctx, fs + 1 - 2 * self.core)
        self.near = (ctx_of(y, 1 - xl, z), lax.rem(fs + 2, 4))
        self.plane = []
        for dh in (1, 0):
            for dy in (2, 1, 3, 0):
                for dx in (1, 0):
                    if dh or dy or dx:
                        hh = lax.rem(self.xh + dh, 2)
                        c = lax.rem(y + dy, 4) * 2 + lax.rem(xl + dx, 2)
                        self.plane.append((hh, c, (c * 4 + z, hh * 2 + self.core)))
        self.row = []
        for dh, dx in ((1, 0), (1, 1), (0, 1)):
            hh, xx = lax.rem(self.xh + dh, 2), lax.rem(xl + dx, 2)
            self.row.append((hh, xx, ((y * 2 + xx) * 4 + z, hh * 2 + self.core)))
        self.column = [(yy, (ctx_of(yy, xl, z), fs)) for yy in (yo, yp, ym)]
        self.eight = [(c, device) for hh, c, device in self.plane[8:]]


def layer_kernel(
    places, tok, cot, wqkv, wup, wdown, wdense, vec,
    or_o, ir_o, fa_o, qa_o, qb_o,
    X, G, WQ, WU, WD, WE, sq, su, sd, se, LA, LB, N, R, CS, bias,
    KVA, QGA, EC, GE, GH, SL, GU, GD, IB, SU,
    FT, FQ, FY, FX, FR, FPS,
    KP, QP0, LL, LT, raw, gap, TOP, SUM, MIX, ACC, DKV, OUT,
    F1, MA, MB, H1, H2, MF, NF, SF,
    AT, OPB, IPB, GL, GQ, VS, EP, ET, EQ, EY, EX, ER, QP, QT, QB, QR, QPS_A, QPS_B,
    ssem, rsem, lsem, wsem,
):
    w = Where()
    wire = Wire(ssem, rsem, lsem)
    ctx, fs, y, xl, z, core = w.ctx, w.fs, w.y, w.xl, w.z, w.core
    zp, zm, zo, up, down, twin, near = w.zp, w.zm, w.zo, w.up, w.down, w.twin, w.near
    other = lax.rem(fs + 2, 4)
    parity = lax.rem(z, 2)

    load_x = pltpu.make_async_copy(tok, X.at[z], wsem.at[0])
    load_x.start()
    loads_q = []
    for t in range(3):
        for i in range(3):
            at = pl.multiple_of(t * 768 + 256 * i + 128 * lax.div(z, 2), 128)
            loads_q.append(
                pltpu.make_async_copy(
                    wqkv.at[:, pl.ds(at, 128)], sq.at[:, pl.ds((3 * t + i) * 128, 128)], wsem.at[1 + 3 * t + i]
                )
            )
    for copy in loads_q:
        copy.start()
    load_g = pltpu.make_async_copy(cot, G.at[z], wsem.at[10])
    load_g.start()
    spare = jnp.minimum(lax.rem(z + fs, 4), 2)
    load_e = pltpu.make_async_copy(wdense.at[pl.ds(pl.multiple_of(spare * 64, 64), 64)], se, wsem.at[11])
    load_e.start()
    loads_u = []
    for i in range(4):
        at = pl.multiple_of(768 * i + 192 * z - 64 * parity, 128)
        loads_u.append(
            pltpu.make_async_copy(wup.at[:, pl.ds(at, 256)], su.at[:, pl.ds(256 * i, 256)], wsem.at[12 + i])
        )
    for copy in loads_u:
        copy.start()
    load_d = pltpu.make_async_copy(wdown.at[pl.ds(pl.multiple_of(z * 192, 64), 192)], sd, wsem.at[16])
    load_d.start()

    greet([up, down, w.opposite, twin] + [device for _, _, device in w.plane])

    load_x.wait()
    x_up, x_down = wire.send(X.at[z], X.at[z], up), wire.send(X.at[z], X.at[z], down)
    for copy in loads_q:
        copy.wait()

    def piece(stage, at, odd):
        return stage[:, 128 * at + 64 * odd : 128 * at + 64 * odd + 64]

    for odd in range(2):

        @pl.when(parity == odd)
        def _():
            parts = []
            for i in range(3):
                parts += [piece(sq, 3 + i, odd), piece(sq, 6 + i, odd)]
            parts += [piece(sq, i, odd) for i in range(3)] + [jnp.zeros((192, 64), F32)]
            WQ[fs] = jnp.concatenate(parts, 1).astype(LOW)

    q_near = wire.send(WQ.at[fs], WQ.at[fs], near)
    q_twin = wire.send(WQ.at[fs], WQ.at[fs], twin)
    first = lax.div(ctx, 4) * 512
    CS[0], CS[1] = angle_lanes([places[0, first + 64 * i] for i in range(8)], 512)

    def low_block(start):
        block = lax.div(places[0, start], 64)
        return block < 32, jnp.where(block < 32, block, 63 - block)

    runs = [low_block(first + 128 * i) for i in range(4)]
    row = lax.broadcasted_iota(jnp.int32, (128, 128), 0)
    for b in range(2):
        spot = jnp.where(row < 64, runs[2 * b][1], runs[2 * b + 1][1])
        QP0[b] = spot * 64 + lax.rem(row, 64)
        QP0[2 + b] = (63 - spot) * 64 + lax.rem(row, 64)
    lane = lax.broadcasted_iota(jnp.int32, (8, 256), 1)
    line = lax.broadcasted_iota(jnp.int32, (8, 256), 0)
    for c in range(8):
        spot = jnp.zeros((8, 256), jnp.int32)
        for i in range(4):
            spot = jnp.where(lax.div(lane, 64) == i, low_block(512 * c + 128 * i)[1], spot)
        KP[c] = jnp.where(line == 0, spot, 63 - spot) * 64 + lax.rem(lane, 64)

    gain_a, shift_a, gain_b, shift_b = (vec[i : i + 1, :] for i in range(4))

    def norms(zz):
        rows = pl.ds(pl.multiple_of(128 * zz, 128), 128)
        x = X[zz].astype(F32)
        centered = x - jnp.mean(x, -1, keepdims=True)
        inv = lax.rsqrt(jnp.mean(centered * centered, -1, keepdims=True) + norm_eps)
        normed = centered * inv
        N[rows, :] = normed
        R[rows, :] = jnp.broadcast_to(inv, (128, 128))
        LA[rows, :] = (normed * gain_a + shift_a).astype(LOW)
        LB[rows, :] = (normed * gain_b + shift_b).astype(LOW)

    norms(z)
    load_e.wait()
    WE[fs] = se[...].astype(LOW)
    for copy in loads_u:
        copy.wait()
    for odd in range(2):

        @pl.when(parity == odd)
        def _():
            parts = [su[:, 256 * i + 64 * odd : 256 * i + 64 * odd + 192] for i in range(4)]
            WU[fs] = jnp.concatenate(parts, 1).astype(LOW)

    load_d.wait()
    WD[fs] = sd[...].astype(LOW)
    load_g.wait()

    for zz in range(4):

        @pl.when(z == zz)
        def _():
            def head(row, i):
                return vec[row : row + 1, 64 * (zz + 4 * i) : 64 * (zz + 4 * i) + 64]

            parts = []
            for i in range(3):
                parts += [head(5, i), head(6, i)]
            parts += [head(4, i) for i in range(3)] + [jnp.zeros((1, 64), F32)]
            bias[0:1, 0:640] = jnp.concatenate(parts, 1)
            bias[1:2, :] = jnp.concatenate(
                [vec[8 + i : 9 + i, 192 * zz : 192 * zz + 192] for i in range(4)], 1
            )

    def relay(slab, from_down, from_up):
        from_down.wait_recv()
        part = slab.at[zm, pl.ds(0, 64)]
        a = wire.send(part, part, up)
        from_up.wait_recv()
        part = slab.at[zp, pl.ds(64, 64)]
        return [a, wire.send(part, part, down)]

    def forward(slab, copy):
        copy.wait_recv()
        return wire.send(slab.at[other], slab.at[other], twin)

    wire.left(x_up, x_down)
    g_up, g_down = wire.send(G.at[z], G.at[z], up), wire.send(G.at[z], G.at[z], down)
    x_far = relay(X, x_up, x_down)
    norms(zm)
    norms(zp)
    wire.left(q_near)
    e_near, e_twin = wire.send(WE.at[fs], WE.at[fs], near), wire.send(WE.at[fs], WE.at[fs], twin)
    u_near, u_twin = wire.send(WU.at[fs], WU.at[fs], near), wire.send(WU.at[fs], WU.at[fs], twin)
    q_far = forward(WQ, q_near)
    for copy in x_far:
        copy.wait_recv()
    norms(zo)
    g_far = relay(G, g_up, g_down)
    q_twin.wait_recv()
    q_far.wait_recv()
    low256 = lanes(256) < 64

    def arrange(value, i):
        a, b = value[:64], value[64:]
        return jnp.where(runs[i][0], a, b), jnp.where(runs[i][0], b, a)

    for t in range(2):
        rows = slice(256 * t, 256 * t + 256)
        linear = dot(LA[rows, :], WQ[...].reshape(768, 640)) + bias[0:1, 0:640]
        cos_wide, sin_wide = CS[0, rows, :], CS[1, rows, :]
        ab, last = linear[:, 384:512], linear[:, 512:640]
        for h, u in enumerate((ab, pltpu.roll(ab, 64, 1), last)):
            keys = turn(linear[:, 128 * h : 128 * h + 128], cos_wide, sin_wide)
            asks = jnp.where(low256, turn(u, cos_wide, sin_wide), 0.0)
            for i in (2 * t, 2 * t + 1):
                part = slice(128 * (i - 2 * t), 128 * (i - 2 * t) + 128)
                for half, value in enumerate(arrange(keys[part], i)):
                    at = 256 * half + 64 * i
                    KVA[w.c, h, at : at + 64, :] = value.astype(LOW)
                for half, value in enumerate(arrange(asks[part], i)):
                    at = 256 * half + 64 * i
                    QGA[at : at + 64, 128 * h : 128 * h + 128] = value.astype(LOW)

    spread = Spread(wire, None, None, w)

    def gather(h):
        return spread.around(lambda c: KVA.at[c, h], lambda r, half: r.at[pl.ds(256 * half, 256)])

    kv = [gather(h) for h in range(3)]
    next(kv[0])
    next(kv[2])
    e_far = forward(WE, e_near)
    for copy in g_far + [e_twin, e_far]:
        copy.wait_recv()
    EC[192:, :] = jnp.zeros((64, 768), LOW)
    for i in range(3):
        EC[64 * i : 64 * i + 64, :] = WE[i + jnp.where(i >= 3 - z, 1, 0)]
    for t in range(2):
        grad = dot_rows(G[pl.ds(2 * t, 2)].reshape(256, 768), EC[...])
        ab, last = grad[:, :128], grad[:, 128:]
        for h, u in enumerate((pltpu.roll(ab, 64, 1), ab, pltpu.roll(last, 64, 1))):
            for i in (2 * t, 2 * t + 1):
                part = slice(128 * (i - 2 * t), 128 * (i - 2 * t) + 128)
                for half, value in enumerate(arrange(u[part], i)):
                    at = slice(256 * half + 64 * i, 256 * half + 64 * i + 64)
                    col = slice(128 * h, 128 * h + 128)
                    QGA[at, col] = jnp.where(low256[:64], QGA[at, col], value.astype(LOW))

    wire.left(u_near)
    d_near, d_twin = wire.send(WD.at[fs], WD.at[fs], near), wire.send(WD.at[fs], WD.at[fs], twin)
    u_far = forward(WU, u_near)
    for copy in (u_twin, u_far):
        copy.wait_recv()

    def feed_up(t):
        rows = pl.ds(256 * t, 256)
        hidden = dot(LB[rows, :], WU[...].reshape(768, 768)) + bias[1:2, :]
        half = 0.5 + 0.5 * erf(hidden * 0.7071067811865476)
        GE[rows, :] = (hidden * half).astype(LOW)
        SL[rows, :] = half + hidden * (jnp.exp(hidden * hidden * -0.5) * 0.3989422804014327)

    down_parts = ((GD, 1, 0, 64, 64, 768), (GD, 1, 64, 128, 0, 1536))
    up_parts = ((GU, 0, 0, 128, 0, 0), (GU, 0, 128, 64, 0, 768))

    def exchange(slab, k):
        copies = []
        for h in range(2):
            at = pl.multiple_of(192 * (2 * h + 1 - core), 64)
            copies.append(wire.send(slab.at[pl.ds(at, 192)], FT.at[k, h], twin))
        return copies

    def add_pair(copies, parts):
        for copy in copies:
            copy.wait_recv()
        for slab, k, row, size, to, col in parts:
            for h in range(2):
                at = pl.multiple_of(192 * (2 * h + core) + row, 64)
                for r in range(0, size, 16):
                    total = slab[pl.ds(pl.multiple_of(at + r, 16), 16), :].astype(F32) + FT[
                        k, h, row + r : row + r + 16, :
                    ].astype(F32)
                    FQ[(to + r) // 32, h, (to + r) // 16 % 2, :, col : col + 768] = total.astype(LOW)

    feed_up(0)
    next(kv[0])
    feed_up(1)
    next(kv[1])
    d_far = forward(WD, d_near)
    for copy in (d_twin, d_far):
        copy.wait_recv()
    for t in range(2):
        rows = pl.ds(256 * t, 256)
        grad = G[2 * t : 2 * t + 2].reshape(256, 768)
        GH[rows, :] = (dot_rows(grad, WD[...].reshape(768, 768)) * SL[rows, :]).astype(LOW)
    next(kv[0])

    @pl.loop(0, 3)
    def _(j):
        at = pl.ds(pl.multiple_of(256 * j, 256), 256)
        GD[at, :] = dot_down(GE[:, at], G[...].reshape(512, 768)).astype(LOW)

    paired_down = exchange(GD, 1)
    next(kv[2])

    @pl.loop(0, 3)
    def _(j):
        at = pl.ds(pl.multiple_of(256 * j, 256), 256)
        GU[at, :] = dot_down(LB[:, at], GH[...]).astype(LOW)

    paired_up = exchange(GU, 0)
    next(kv[1])

    low = lanes(512) < 64
    same = (
        lax.broadcasted_iota(jnp.int32, (256, 256), 0) == lax.broadcasted_iota(jnp.int32, (256, 256), 1)
    )
    same = jnp.where(same, 1.0, 0.0).astype(LOW)
    deep = lax.broadcasted_iota(jnp.int32, (128, 256), 0) < 64

    meets = ((0,), (0,), (0, 1), (0, 1))
    spots = {}
    for b in range(4):
        for side in meets[b]:
            spots[b, side] = len(spots)

    def keys_of(c, h, side):
        return KVA[c, h, 256 * side : 256 * side + 256, :]

    def twice(value):
        return jnp.concatenate([value, value], 1)

    def score(h):
        for b in range(4):
            part = QGA[128 * b : 128 * b + 128, 128 * h : 128 * h + 128]
            none = jnp.zeros_like(part)
            pile = jnp.concatenate(
                [jnp.where(low256[:128], part, none), jnp.where(low256[:128], none, part)], 0
            )
            LL[b] = pile
            LT[b] = dot_rows(same[:128, :128], pile).astype(LOW)
        TOP[...] = jnp.full_like(TOP, masked)

        @pl.loop(0, 8)
        def _(c):
            for b in range(4):
                top = TOP[b]
                for side in meets[b]:
                    pair = dot_rows(LL[b], keys_of(c, h, side))
                    scores = pair[:128]
                    if b < 2 or side:
                        seen = KP[c, side : side + 1, :] <= twice(QP0[b])
                        scores = jnp.where(seen, scores, masked)
                    raw[c, spots[b, side]] = scores
                    gap[c, spots[b, side]] = pair[128:]
                    top = jnp.maximum(top, jnp.maximum(scores[:, :128], scores[:, 128:]))
                TOP[b] = top

    def weigh():
        for b in range(4):
            TOP[b] = jnp.broadcast_to(jnp.max(TOP[b], -1, keepdims=True), (128, 128))
        SUM[...] = jnp.zeros_like(SUM)
        MIX[...] = jnp.zeros_like(MIX)

        @pl.loop(0, 8)
        def _(c):
            for b in range(4):
                total, blend = SUM[b], MIX[b]
                for side in meets[b]:
                    i = spots[b, side]
                    e = jnp.exp((raw[c, i] - twice(TOP[b])) * 0.125)
                    raw[c, i] = e
                    mix = e * gap[c, i]
                    total = total + (e[:, :128] + e[:, 128:])
                    blend = blend + (mix[:, :128] + mix[:, 128:])
                SUM[b] = total
                MIX[b] = blend

    def settle(h):
        for b in range(4):
            inverse = 1.0 / jnp.sum(SUM[b], -1, keepdims=True)
            shared = jnp.sum(MIX[b], -1, keepdims=True) * inverse
            SUM[b] = jnp.broadcast_to(inverse, (128, 128))
            MIX[b] = jnp.broadcast_to(shared, (128, 128))
        ACC[...] = jnp.zeros_like(ACC)

        @pl.loop(0, 8)
        def _(c):
            grown = [None, None]
            for b in range(4):
                total = ACC[b]
                for side in meets[b]:
                    i = spots[b, side]
                    probs = raw[c, i] * twice(SUM[b])
                    slope = probs * (gap[c, i] - twice(MIX[b]))
                    pile = jnp.concatenate([slope.astype(LOW), probs.astype(LOW)], 0)
                    total = total + dot(pile, keys_of(c, h, side))
                    part = dot(LT[b], pile)
                    grown[side] = part if grown[side] is None else grown[side] + part
                ACC[b] = total
            for side, g in enumerate(grown):
                g = jnp.where(deep, g * 0.125, g).astype(LOW)
                DKV[c, h, 256 * side : 256 * side + 256, :] = dot_rows(same, g).astype(LOW)

        done = [jnp.where(low256[:128], ACC[b, :128] * 0.125, ACC[b, 128:]) for b in range(4)]
        for i in range(4):
            at = slice(64 * (i % 2), 64 * (i % 2) + 64)
            a, b = done[i // 2][at], done[2 + i // 2][at]
            at = slice(128 * h, 128 * h + 128)
            OUT[128 * i : 128 * i + 64, at] = jnp.where(runs[i][0], a, b)
            OUT[128 * i + 64 : 128 * i + 128, at] = jnp.where(runs[i][0], b, a)

    def tree(h):
        t1 = wire.send(DKV.at[w.c_far_mate, h], F1.at[h], w.side)
        t2 = wire.send(DKV.at[w.c_north_mate, h], MA.at[h], w.north)
        t3 = wire.send(DKV.at[w.c_south_mate, h], MB.at[h], w.south)
        yield
        t1.wait_recv()
        DKV[w.c_far, h] = (DKV[w.c_far, h].astype(F32) + F1[h].astype(F32)).astype(LOW)
        t4 = wire.send(DKV.at[w.c_far, h, pl.ds(0, 256)], H1.at[h], w.south)
        t5 = wire.send(DKV.at[w.c_far, h, pl.ds(256, 256)], H2.at[h], w.north)
        t2.wait_recv()
        t3.wait_recv()
        total = DKV[w.c_mate, h].astype(F32) + MA[h].astype(F32) + MB[h].astype(F32)
        DKV[w.c_mate, h] = total.astype(LOW)
        t6 = wire.send(DKV.at[w.c_mate, h], MF.at[h], w.side)
        yield
        t4.wait_recv()
        total = DKV[w.c_south, h, 0:256, :].astype(F32) + H1[h].astype(F32)
        DKV[w.c_south, h, 0:256, :] = total.astype(LOW)
        t7 = wire.send(DKV.at[w.c_south, h], NF.at[h], w.south)
        t5.wait_recv()
        total = DKV[w.c_north, h, 256:512, :].astype(F32) + H2[h].astype(F32)
        DKV[w.c_north, h, 256:512, :] = total.astype(LOW)
        t8 = wire.send(DKV.at[w.c_north, h], SF.at[h], w.north)
        yield
        for copy in (t6, t7, t8):
            copy.wait_recv()

    def add_up(parts):
        total = parts[0].astype(F32)
        for part in parts[1:]:
            total = total + part.astype(F32)
        return total.astype(LOW)

    def ladder(packet, fy, fx, fr, out):
        copies = [wire.send(packet.at[yy], fy.at[y], device) for yy, device in w.column]
        fy[y] = packet[y]
        yield
        for copy in copies:
            copy.wait_recv()
        for h in range(2):
            for i in range(2):
                fx[h, i] = add_up([fy[j, h, i] for j in range(4)])
        me = w.xh * 2 + xl
        copies = [wire.send(fx.at[hh, xx], fr.at[me], device) for hh, xx, device in w.row]
        fr[me] = fx[w.xh, xl]
        yield
        for copy in copies:
            copy.wait_recv()
        out(add_up([fr[j] for j in range(4)]))

    def drain(steps):
        for _ in steps:
            pass

    def keep_piece(total):
        FPS[...] = total

    def keep_dense(total):
        QPS_B[:, 384:768] = total

    def arrived(copies):
        for copy in copies:
            copy.wait_recv()

    def arrived(copies):
        for copy in copies:
            copy.wait_recv()

    fl = ladder(FQ, FY, FX, FR, keep_piece)
    fa = Spread(wire, FPS, fa_o, w).eight_first()
    trees = [tree(h) for h in range(3)]
    drain(kv[0])
    score(0)
    add_pair(paired_down, down_parts)
    add_pair(paired_up, up_parts)
    next(fl)
    weigh()
    next(kv[1])
    settle(0)
    next(kv[2])
    drain(kv[1])
    score(1)
    next(trees[0])
    weigh()
    next(fl)
    settle(1)
    next(trees[0])
    drain(fl)
    next(fa)
    drain(kv[2])
    score(2)
    next(fa)
    weigh()
    next(trees[1])
    next(fa)
    settle(2)
    next(trees[2])
    next(fa)

    o0, o1, o2 = (OUT[:, 128 * i : 128 * i + 128] for i in range(3))
    AT[:, :128] = jnp.where(low, pltpu.roll(o0, 64, 1), o1).astype(LOW)
    AT[:, 128:] = jnp.where(low, pltpu.roll(o2, 64, 1), 0.0).astype(LOW)
    ge = dot_down(AT[...], G[...].reshape(512, 768))
    for i in range(4):
        empty = 3 - z
        after = ge[64 * i - 64 : 64 * i] if i else ge[0:64]
        before = ge[64 * i : 64 * i + 64] if i < 3 else ge[128:192]
        slot = jnp.where(i > empty, after, before)
        slot = jnp.where(i == empty, 0.0, slot).astype(LOW)
        EP[i, 0:64, :] = slot[:, :384]
        EP[i, 64:128, :] = slot[:, 384:]
    paired_e = [wire.send(EP.at[2 * h + 1 - core], ET.at[h], twin) for h in range(2)]
    next(trees[1])
    next(trees[0])
    SU[...] = jnp.zeros_like(SU)
    for t in range(2):
        rows = pl.ds(256 * t, 256)
        back = GH[rows, :]
        grad_ln = dot_rows(back, WU[...].reshape(768, 768))
        normed = N[rows, :]
        SU[0:1, :] += jnp.sum(grad_ln * normed, 0, keepdims=True)
        SU[1:2, :] += jnp.sum(grad_ln, 0, keepdims=True)
        SU[2:3, :] += jnp.sum(back.astype(F32), 0, keepdims=True)
        IB[rows, :] = norm_back(grad_ln, normed, R[rows, 0:1], gain_b)
    next(trees[2])
    next(trees[1])
    arrived(paired_e)
    for h in range(2):
        for c in range(8):
            at = slice(16 * c, 16 * c + 16)
            EQ[c // 2, h, c % 2] = add_up([EP[2 * h + core, at, :], ET[h, at, :]])
    el = ladder(EQ, EY, EX, ER, keep_dense)
    next(el)
    for i in range(4):
        rows = slice(128 * i, 128 * i + 128)
        total = dot(GE[rows, :], WD[...].reshape(768, 768)) + dot(AT[rows, :], EC[...])
        OPB[i] = total.astype(LOW)
    ring = ((zo, w.opposite), (zp, up), (zm, down))
    o_sent = [wire.send(OPB.at[zz], or_o.at[z], device) for zz, device in ring]
    wire.keep(OPB.at[z], or_o.at[z])
    next(trees[2])

    cos_wide, sin_wide = CS[0], -CS[1]
    u0, u1, u2 = (turn(u, cos_wide, sin_wide) for u in (o0, o1, o2))
    GL[:, 384:512] = jnp.where(low, u0, pltpu.roll(u1, 64, 1)).astype(LOW)
    GL[:, 512:640] = jnp.where(low, u2, 0.0).astype(LOW)

    def own_sum(h):
        drain(trees[h])
        total = DKV[w.c, h].astype(F32) + MF[h].astype(F32) + NF[h].astype(F32) + SF[h].astype(F32)
        for i in range(4):
            a, b = total[64 * i : 64 * i + 64], total[256 + 64 * i : 320 + 64 * i]
            rows = slice(128 * i, 128 * i + 128)
            value = jnp.concatenate([jnp.where(runs[i][0], a, b), jnp.where(runs[i][0], b, a)], 0)
            value = turn(value, CS[0, rows, :], -CS[1, rows, :])
            GL[rows, 128 * h : 128 * h + 128] = value.astype(LOW)

    def project(cols):
        for t in range(2):
            rows = slice(256 * t, 256 * t + 256)
            yield rows, dot_rows(GL[rows, cols], WQ[:, :, cols].reshape(768, -1))

    def weight_part(cols):
        @pl.loop(0, 3)
        def _(j):
            at = pl.ds(pl.multiple_of(256 * j, 256), 256)
            GQ[at, cols] = dot_down(LA[:, at], GL[:, cols]).astype(LOW)

    own_sum(0)
    own_sum(1)
    for rows, value in project(slice(0, 256)):
        SL[rows, :] = value
    for rows, value in project(slice(384, 640)):
        SL[rows, :] = SL[rows, :] + value
    weight_part(slice(0, 256))
    weight_part(slice(384, 640))
    VS[...] = jnp.zeros_like(VS)

    def note(row, values):
        for j in range(values.shape[1] // 128):
            VS[6 * row + j : 6 * row + j + 1, :] = values[:, 128 * j : 128 * j + 128]

    note(2, SU[0:1, :])
    note(3, SU[1:2, :])
    note(5, SU[2:3, :])
    note(6, jnp.sum(G[z].astype(F32), 0, keepdims=True))
    next(el)
    own_sum(2)
    dots = jnp.zeros((1, 768), F32)
    plain = jnp.zeros((1, 768), F32)
    for rows, value in project(slice(256, 384)):
        grad_ln = SL[rows, :] + value
        SL[rows, :] = grad_ln
        dots = dots + jnp.sum(grad_ln * N[rows, :], 0, keepdims=True)
        plain = plain + jnp.sum(grad_ln, 0, keepdims=True)
    note(0, dots)
    note(1, plain)
    note(4, jnp.sum(GL[...].astype(F32), 0, keepdims=True))
    weight_part(slice(256, 384))
    for i in range(4):
        QP[i, :, 0:640] = GQ[192 * i : 192 * i + 128, :]
        QP[i, 0:64, 640:1024] = GQ[192 * i + 128 : 192 * i + 192, 0:384]
        QP[i, 64:128, 640:896] = GQ[192 * i + 128 : 192 * i + 192, 384:640]
        QP[i, 64:128, 896:1024] = VS[...].astype(LOW)
    paired_q = [wire.send(QP.at[2 * h + 1 - core], QT.at[h], twin) for h in range(2)]
    next(fa)
    drain(el)
    arrived(paired_q)
    for h in range(2):
        for c in range(8):
            at = slice(16 * c, 16 * c + 16)
            QB[h, c] = add_up([QP[2 * h + core, at, :], QT[h, at, :]])
    me = w.xh * 8 + w.c
    q_plane = [wire.send(QB.at[hh, c], QR.at[me], device) for hh, c, device in w.plane]
    QR[me] = QB[w.xh, w.c]
    for t in range(4):
        rows = slice(128 * t, 128 * t + 128)
        total = norm_back(SL[rows, :], N[rows, :], R[rows, 0:1], gain_a) + IB[rows, :]
        IPB[t] = total.astype(LOW)
    i_sent = [wire.send(IPB.at[zz], ir_o.at[z], device) for zz, device in ring]
    wire.keep(IPB.at[z], ir_o.at[z])
    for copy in q_plane:
        copy.wait_recv()
    total = add_up([QR[j] for j in range(16)])
    QPS_A[...] = total[:, :640]
    QPS_B[:, :384] = total[:, 640:]
    first_a = [wire.send(QPS_A, qa_o.at[z, w.c], device) for _, device in w.eight]
    first_b = [wire.send(QPS_B, qb_o.at[w.c, z], device) for _, device in ring]
    own = wire.keep(QPS_B, qb_o.at[w.c, z]), wire.keep(QPS_A, qa_o.at[z, w.c])
    for copy in own:
        copy.wait()
    wire.kept = [k for k in wire.kept if not any(k is o for o in own)]
    arrived(first_b)
    last_b = [wire.send(qb_o.at[w.c], qb_o.at[w.c], device) for _, device in w.eight]
    arrived(first_a)
    last_a = [wire.send(qa_o.at[z], qa_o.at[z], device) for _, device in ring]
    drain(fa)
    arrived(last_b + last_a)
    for copy in o_sent + i_sent:
        copy.wait_recv()
    wire.finish()


def layer(places, tok, cot, wqkv, wup, wdown, wdense, vec):
    outs = [
        ((4, 128, 768), LOW),
        ((4, 128, 768), LOW),
        ((4, 8, 16, 2304), LOW),
        ((4, 8, 16, 640), LOW),
        ((8, 4, 16, 768), LOW),
    ]
    scratch = [
        *[((4, 128, 768), LOW)] * 2,
        ((4, 192, 640), LOW),
        *[((4, 192, 768), LOW)] * 2,
        ((4, 64, 768), LOW),
        ((192, 1152), F32),
        ((192, 1024), F32),
        ((192, 768), F32),
        ((64, 768), F32),
        *[((512, 768), LOW)] * 2,
        ((512, 768), F32),
        ((512, 128), F32),
        ((2, 512, 128), F32),
        ((8, 768), F32),
        ((8, 3, 512, 128), LOW),
        ((512, 384), LOW),
        ((256, 768), LOW),
        *[((512, 768), LOW)] * 2,
        ((512, 768), F32),
        *[((768, 768), LOW)] * 2,
        ((512, 768), F32),
        ((8, 768), F32),
        ((2, 2, 192, 768), LOW),
        ((4, 2, 2, 16, 2304), LOW),
        ((4, 2, 2, 16, 2304), LOW),
        ((2, 2, 16, 2304), LOW),
        ((4, 16, 2304), LOW),
        ((16, 2304), LOW),
        ((8, 8, 256), jnp.int32),
        ((4, 128, 128), jnp.int32),
        ((4, 256, 128), LOW),
        ((4, 128, 256), LOW),
        *[((8, 6, 128, 256), F32)] * 2,
        *[((4, 128, 128), F32)] * 3,
        ((4, 256, 128), F32),
        ((8, 3, 512, 128), LOW),
        ((512, 384), F32),
        *[((3, 512, 128), LOW)] * 3,
        *[((3, 256, 128), LOW)] * 2,
        *[((3, 512, 128), LOW)] * 3,
        ((512, 256), LOW),
        *[((4, 128, 768), LOW)] * 2,
        ((512, 640), LOW),
        ((768, 640), LOW),
        ((64, 128), F32),
        ((4, 128, 384), LOW),
        ((2, 128, 384), LOW),
        ((4, 2, 2, 16, 384), LOW),
        ((4, 2, 2, 16, 384), LOW),
        ((2, 2, 16, 384), LOW),
        ((4, 16, 384), LOW),
        ((4, 128, 1024), LOW),
        ((2, 128, 1024), LOW),
        ((2, 8, 16, 1024), LOW),
        ((16, 16, 1024), LOW),
        ((16, 640), LOW),
        ((16, 768), LOW),
    ]
    anywhere = pl.BlockSpec(memory_space=pl.ANY)
    sends = 168
    return pl.pallas_call(
        layer_kernel,
        out_shape=[jax.ShapeDtypeStruct(s, d) for s, d in outs],
        in_specs=[pl.BlockSpec(memory_space=pltpu.SMEM)]
        + [anywhere] * 6
        + [pl.BlockSpec(memory_space=pltpu.VMEM)],
        out_specs=[anywhere] * len(outs),
        scratch_shapes=[pltpu.VMEM(s, d) for s, d in scratch]
        + [
            pltpu.SemaphoreType.DMA((sends,)),
            pltpu.SemaphoreType.DMA((sends,)),
            pltpu.SemaphoreType.DMA((16,)),
            pltpu.SemaphoreType.DMA((17,)),
        ],
        compiler_params=pltpu.CompilerParams(
            collective_id=0, has_side_effects=True, vmem_limit_bytes=60 * 1024 * 1024
        ),
    )(places, tok, cot, wqkv, wup, wdown, wdense, vec)


def step_kernel(
    spot, tok, cot, ors, irs, fa, qa, qb, vec, vec_m, vec_s,
    qw, qm, qs, ew, em, es, uw, um, us, dw, dm, ds,
    blk_o, inp_o, vw_o, vm_o, vs_o,
    qw_o, qm_o, qs_o, ew_o, em_o, es_o, uw_o, um_o, us_o, dw_o, dm_o, ds_o,
    TO, CO, OR, IR, FA, QA, QB, VW, VM, VS, QW, QM, QS, EW, EM, ES, UW, UM, US, DW, DM, DS,
    BL, IN, isem, osem,
):
    count = [0, 0]

    def start(src, dst, sem, which):
        copy = pltpu.make_async_copy(src, dst, sem.at[count[which]])
        count[which] += 1
        copy.start()
        return copy

    def arrive(pairs):
        return [start(a, b, isem, 0) for a, b in pairs]

    def cut_rows(pairs, at, size):
        return [(a.at[pl.ds(at, size)], b.at[pl.ds(at, size)]) for a, b in pairs]

    up, down = ((uw, UW), (um, UM), (us, US)), ((dw, DW), (dm, DM), (ds, DS))
    dense, qkv = ((ew, EW), (em, EM), (es, ES)), ((qw, QW), (qm, QM), (qs, QS))
    load_v = arrive(((vec, VW), (vec_m, VM), (vec_s, VS)))
    load_e = arrive(((qb, QB),) + dense)
    load_small = arrive(((tok, TO), (cot, CO), (ors, OR), (irs, IR)))
    load_u1 = arrive(((fa, FA), *cut_rows(up, 0, 128)))
    load_u2 = arrive(cut_rows(up, 128, 64))
    load_d1 = arrive(cut_rows(down, 0, 384))
    load_d2 = arrive(cut_rows(down, 384, 384))
    load_q = arrive(((qa, QA),) + tuple(cut_rows(qkv, 0, 128)))
    load_q2 = arrive(cut_rows(qkv, 128, 64))
    leaving = []

    def leave(pairs):
        leaving.extend(start(a, b, osem, 1) for a, b in pairs)

    def back_rows(pairs, at, size):
        leave((b.at[pl.ds(at, size)], a.at[pl.ds(at, size)]) for a, b in pairs)

    def wait(copies):
        for copy in copies:
            copy.wait()

    def update(slabs, rows, gradient, rate, decay):
        new = adamw(slabs[0][rows, :], slabs[1][rows, :], slabs[2][rows, :], gradient, rate, decay)
        for slab, value in zip(slabs, new):
            slab[rows, :] = value

    def rows_of(start_at, size=16):
        return pl.ds(pl.multiple_of(start_at, 16), size)

    def spread_up(parts):
        parts = [p.astype(F32) for p in parts]
        return jnp.concatenate([parts[z][:, 192 * i : 192 * i + 192] for i in range(4) for z in range(4)], 1)

    wait(load_v)
    wait(load_e)

    @pl.loop(0, 4)
    def _(c):
        for o in range(3):
            z = lax.rem(o + 4 - spot[0], 4)
            gradient = jnp.concatenate([QB[c, z, :, 384:768], QB[4 + c, z, :, 384:768]], 1).astype(F32)
            update((EW, EM, ES), rows_of(64 * o + 16 * c), gradient, 0.1, 0.1)

    leave(((EW, ew_o), (EM, em_o), (ES, es_o)))
    wait(load_small)
    BL[...] = (
        TO[...].astype(F32) + jnp.sum(OR[...].astype(F32), 0) + VW[7:8, :] + VW[12:13, :]
    ).astype(LOW)
    IN[...] = CO[...].astype(F32) + jnp.sum(IR[...].astype(F32), 0)
    leave(((BL, blk_o), (IN, inp_o)))
    wait(load_u1)

    @pl.loop(0, 8)
    def _(c):
        update((UW, UM, US), rows_of(16 * c), spread_up([FA[z, c, :, 0:768] for z in range(4)]), 0.03, 0.1)

    back_rows(((uw_o, UW), (um_o, UM), (us_o, US)), 0, 128)
    wait(load_u2)

    @pl.loop(0, 4)
    def _(c):
        gradient = spread_up([FA[z, c, :, 768:1536] for z in range(4)])
        update((UW, UM, US), rows_of(128 + 16 * c), gradient, 0.03, 0.1)

    back_rows(((uw_o, UW), (um_o, UM), (us_o, US)), 128, 64)

    for half, load in enumerate((load_d1, load_d2)):
        wait(load)

        @pl.loop(0, 8)
        def _(c):
            for z in (2 * half, 2 * half + 1):
                rows = rows_of(192 * z + 64 + 16 * c)
                update((DW, DM, DS), rows, FA[z, c, :, 1536:2304].astype(F32), 0.02, 0.1)

        @pl.loop(0, 4)
        def _(c):
            for z in (2 * half, 2 * half + 1):
                rows = rows_of(192 * z + 16 * c)
                update((DW, DM, DS), rows, FA[z, 4 + c, :, 768:1536].astype(F32), 0.02, 0.1)

        back_rows(((dw_o, DW), (dm_o, DM), (ds_o, DS)), 384 * half, 384)

    wait(load_q)
    low = lanes(16) < 64

    def spread_heads(groups):
        out = []
        for t in range(3):
            for i in range(3):
                for pair in range(2):
                    halves = []
                    for odd in range(2):
                        group = groups[2 * pair + odd]
                        if t == 0:
                            u, at = group[3 + i // 2], i % 2
                        else:
                            u, at = group[i], t - 1
                        halves.append(u if at == odd else pltpu.roll(u, 64, 1))
                    out.append(jnp.where(low, halves[0], halves[1]))
        return jnp.concatenate(out, 1)

    def cut(value):
        value = value.astype(F32)
        return [value[:, 128 * j : 128 * j + 128] for j in range(value.shape[1] // 128)]

    @pl.loop(0, 8)
    def _(c):
        groups = [cut(QA[z, c]) for z in range(4)]
        update((QW, QM, QS), rows_of(16 * c), spread_heads(groups), 0.03, 0.1)

    back_rows(((qw_o, QW), (qm_o, QM), (qs_o, QS)), 0, 128)
    wait(load_q2)

    @pl.loop(0, 4)
    def _(c):
        groups = [cut(QB[c, z, :, 0:384]) + cut(QB[4 + c, z, :, 0:256]) for z in range(4)]
        update((QW, QM, QS), rows_of(128 + 16 * c), spread_heads(groups), 0.03, 0.1)

    back_rows(((qw_o, QW), (qm_o, QM), (qs_o, QS)), 128, 64)

    notes = [QB[4:8, z, :, 256:384].astype(F32).reshape(64, 128) for z in range(4)]
    total = (notes[0] + notes[1]) + (notes[2] + notes[3])

    def line(values, row):
        return jnp.concatenate([values[6 * row + j : 6 * row + j + 1, :] for j in range(6)], 1)

    linear = [line(n, 4) for n in notes]
    heads = []
    for at in (lambda i: 384 + 64 * i, lambda i: 128 * i, lambda i: 128 * i + 64):
        heads.append(
            jnp.concatenate([linear[z][:, at(i) : at(i) + 64] for i in range(3) for z in range(4)], 1)
        )
    hidden = [line(n, 5) for n in notes]
    wide = [
        jnp.concatenate([hidden[z][:, 192 * i : 192 * i + 192] for z in range(4)], 1) for i in range(4)
    ]
    ends = line(total, 6)
    lines = [line(total, i) for i in range(4)] + heads + [ends] + wide + [ends]
    for i, gradient in enumerate(lines):
        row = slice(i, i + 1)
        update((VW, VM, VS), row, gradient, 0.2, 0.0)
    leave(((VW, vw_o), (VM, vm_o), (VS, vs_o)))
    wait(leaving)


def step(spot, small, parts, vectors, weights):
    anywhere = pl.BlockSpec(memory_space=pl.ANY)
    outs = [jax.ShapeDtypeStruct((128, 768), LOW), jax.ShapeDtypeStruct((128, 768), F32)]
    operands = [*small, *parts, *vectors, *weights]
    outs += [jax.ShapeDtypeStruct(v.shape, F32) for v in [*vectors, *weights]]
    return pl.pallas_call(
        step_kernel,
        out_shape=outs,
        in_specs=[pl.BlockSpec(memory_space=pltpu.SMEM)] + [anywhere] * len(operands),
        out_specs=[anywhere] * len(outs),
        scratch_shapes=[pltpu.VMEM(v.shape, v.dtype) for v in operands]
        + [pltpu.VMEM(o.shape, o.dtype) for o in outs[:2]]
        + [pltpu.SemaphoreType.DMA((40,)), pltpu.SemaphoreType.DMA((40,))],
        compiler_params=pltpu.CompilerParams(vmem_limit_bytes=VMEM_LIMIT),
    )(spot, *operands)


def norm_back(incoming, normed, inv_scale, gain_row):
    scaled = incoming * gain_row
    return inv_scale * (
        scaled
        - jnp.mean(scaled, -1, keepdims=True)
        - normed * jnp.mean(scaled * normed, -1, keepdims=True)
    )


def adamw(weight, moment, second, gradient, step_rate, decay_rate):
    moment_new = beta_first * moment + (1.0 - beta_first) * gradient
    second_new = beta_second * second + ((1.0 - beta_second) * gradient) * gradient
    size = jnp.sqrt(second_new * (1.0 / (1.0 - beta_second**STEP))) + adam_eps
    change = moment_new * (step_rate / (1.0 - beta_first**STEP)) / size
    return (weight * (1.0 - step_rate * decay_rate) - change, moment_new, second_new)


def dot(a, b):
    return jnp.dot(a, b, preferred_element_type=F32)


def dot_rows(a, b):
    return lax.dot_general(a, b, (((1,), (1,)), ((), ())), preferred_element_type=F32)


def dot_down(a, b):
    return lax.dot_general(a, b, (((0,), (0,)), ((), ())), preferred_element_type=F32)


def body(
    tokens,
    cotangent,
    positions,
    vectors,
    vectors_moment,
    vectors_second,
    qkv_weight,
    qkv_moment,
    qkv_second,
    dense_weight,
    dense_moment,
    dense_second,
    up_weight,
    up_moment,
    up_second,
    down_weight,
    down_moment,
    down_second,
):
    fs = lax.axis_index("fsdp")
    ors, irs, fa, qa, qb = layer(
        positions, tokens[0], cotangent[0], qkv_weight, up_weight, down_weight, dense_weight, vectors
    )
    block_out, input_grad, *new = step(
        fs.reshape(1).astype(jnp.int32),
        (tokens[0], cotangent[0], ors, irs),
        (fa, qa, qb),
        (vectors, vectors_moment, vectors_second),
        (
            qkv_weight,
            qkv_moment,
            qkv_second,
            dense_weight,
            dense_moment,
            dense_second,
            up_weight,
            up_moment,
            up_second,
            down_weight,
            down_moment,
            down_second,
        ),
    )
    return (block_out[None], input_grad[None], *new)


def solution(mesh):
    split = P("fsdp", None)
    act = P("fsdp", "ctx", None)
    return jax.shard_map(
        body,
        mesh=mesh,
        in_specs=(act, act, split, P(), P(), P()) + (split,) * 12,
        out_specs=(act, act, P(), P(), P()) + (split,) * 12,
        check_vma=False,
    )
```

```python
import jax
import jax.numpy as jnp
from jax import lax
from jax.experimental import pallas as pl
from jax.experimental.pallas import tpu as pltpu
from jax.sharding import PartitionSpec as P

HEADS = 12
ROT = 16
STEP = 10
MESH = pl.DeviceIdType.MESH
F32 = jnp.float32
LOW = jnp.bfloat16
VMEM_LIMIT = 56 * 1024 * 1024

masked = -1e30
norm_eps = 1e-05
adam_eps = 1e-08
beta_first = 0.9
beta_second = 0.95
log2e = 1.4426950408889634


def ctx_of(y, xl, z):
    return (lax.rem(y, 4) * 2 + lax.rem(xl, 2)) * 4 + lax.rem(z, 4)


def place():
    ctx = lax.axis_index("ctx")
    fs = lax.axis_index("fsdp")
    c = lax.div(ctx, 4)
    return ctx, fs, lax.div(c, 2), lax.rem(c, 2), lax.rem(ctx, 4)


def greet(devices):
    barrier = pltpu.get_barrier_semaphore()
    for device in devices:
        pl.semaphore_signal(barrier, inc=1, device_id=device, device_id_type=MESH)
    pl.semaphore_wait(barrier, len(devices))


class Wire:
    def __init__(self, send_sem, recv_sem, local_sem):
        self.send_sem, self.recv_sem, self.local_sem = send_sem, recv_sem, local_sem
        self.sent, self.kept, self.local, self.count = [], [], 0, 0

    def send(self, src, dst, device):
        at = self.count
        self.count += 1
        copy = pltpu.make_async_remote_copy(
            src_ref=src,
            dst_ref=dst,
            send_sem=self.send_sem.at[at],
            recv_sem=self.recv_sem.at[at],
            device_id=device,
            device_id_type=MESH,
        )
        copy.start()
        self.sent.append(copy)
        return copy

    def left(self, *copies):
        for copy in copies:
            copy.wait_send()
        self.sent = [s for s in self.sent if not any(s is c for c in copies)]

    def keep(self, src, dst):
        copy = pltpu.make_async_copy(src, dst, self.local_sem.at[self.local])
        self.local += 1
        copy.start()
        self.kept.append(copy)
        return copy

    def finish(self):
        for copy in self.sent:
            copy.wait_send()
        for copy in self.kept:
            copy.wait()


def eight_peers(y, xl, z, fs):
    return [
        (ctx_of(lax.rem(y + 1, 4), xl, z), fs),
        (ctx_of(lax.rem(y + 3, 4), xl, z), fs),
        (ctx_of(y, 1 - xl, z), fs),
    ]


def erf(x):
    x = jnp.clip(x, -3.832506856900711, 3.832506856900711)
    s = x * x
    top = jnp.full_like(x, 0.00022905065861350646)
    for k in (0.0034082910107109506, 0.050955695062380861, 0.18520832239976145, 1.128379143519084):
        top = top * s + k
    low = jnp.full_like(x, -1.1791602954361697e-7)
    for k in (0.000023547966471313185, 0.0010179625278914885, 0.014070470171167667, 0.11098505178285362, 0.49746925110067538, 1.0):
        low = low * s + k
    return x * top / low


def lanes(rows, width=128):
    return lax.broadcasted_iota(jnp.int32, (rows, width), 1)


def turn(u, cos_wide, sin_wide):
    lane = lanes(u.shape[0])
    up = pltpu.roll(u, 120, 1) * jnp.where(lane < 8, -sin_wide, 0.0)
    down = pltpu.roll(u, 8, 1) * jnp.where(lane < 8, 0.0, sin_wide)
    return u * cos_wide + up + down


def angle_lanes(start, rows):
    lane = lanes(rows)
    row = lax.broadcasted_iota(jnp.int32, (rows, 128), 0)
    spot = row & 63
    for i, first in enumerate(start):
        spot = spot + jnp.where((row >> 6) == i, first, 0)
    power = (lane & 7).astype(F32) * (2.0 / ROT)
    frequency = jnp.where(lane < ROT, jnp.exp(power * -9.210340371976184), 0.0)
    angle = spot.astype(F32) * frequency
    return jnp.cos(angle), jnp.sin(angle)


class Spread:
    def __init__(self, wire, piece, out, where):
        self.wire, self.piece, self.out, self.w = wire, piece, out, where

    def around(self, slab, halves):
        w, wire = self.w, self.wire
        me = slab(w.c)
        a, b = wire.send(me, me, w.north), wire.send(me, me, w.south)
        x = wire.send(me, me, w.side)
        yield
        x.wait_recv()
        mate = slab(w.c_mate)
        p1, p2 = wire.send(mate, mate, w.north), wire.send(mate, mate, w.south)
        a.wait_recv()
        part = halves(slab(w.c_south), 0)
        h1 = wire.send(part, part, w.north)
        b.wait_recv()
        part = halves(slab(w.c_north), 1)
        h2 = wire.send(part, part, w.south)
        yield
        h1.wait_recv()
        h2.wait_recv()
        far = slab(w.c_far)
        last = wire.send(far, far, w.side)
        yield
        for copy in (p1, p2, last):
            copy.wait_recv()

    def eight_first(self):
        w, wire, out = self.w, self.wire, self.out
        width = out.shape[-1]
        cut = (width // 128 + 1) // 2 * 128
        ends = (pl.ds(0, cut), pl.ds(cut, width - cut))
        own = wire.keep(self.piece, out.at[w.z, w.c])
        own.wait()
        wire.kept = [k for k in wire.kept if k is not own]
        for _ in self.around(lambda c: out.at[w.z, c], lambda r, h: r.at[:, ends[h]]):
            yield
        mine = out.at[w.z]
        a, b = wire.send(mine, mine, w.up), wire.send(mine, mine, w.down)
        yield
        a.wait_recv()
        part = out.at[w.zm, pl.ds(0, 4)]
        h1 = wire.send(part, part, w.up)
        b.wait_recv()
        part = out.at[w.zp, pl.ds(4, 4)]
        h2 = wire.send(part, part, w.down)
        yield
        h1.wait_recv()
        h2.wait_recv()

    def ring_first(self):
        w, wire, out = self.w, self.wire, self.out
        own = wire.keep(self.piece, out.at[w.c, w.z])
        copies = [wire.send(self.piece, out.at[w.c, w.z], d) for d in (w.opposite, w.up, w.down)]
        yield
        own.wait()
        wire.kept = [k for k in wire.kept if k is not own]
        for copy in copies:
            copy.wait_recv()
        for _ in self.around(lambda c: out.at[c], lambda r, h: r.at[pl.ds(2 * h, 2)]):
            yield


class Where:
    def __init__(self):
        ctx, fs, y, xl, z = place()
        self.ctx, self.fs, self.y, self.xl, self.z = ctx, fs, y, xl, z
        self.core, self.xh = lax.rem(fs, 2), lax.div(fs, 2)
        yp, ym, yo = lax.rem(y + 1, 4), lax.rem(y + 3, 4), lax.rem(y + 2, 4)
        self.zp, self.zm, self.zo = lax.rem(z + 1, 4), lax.rem(z + 3, 4), lax.rem(z + 2, 4)
        self.c, self.c_mate = y * 2 + xl, y * 2 + 1 - xl
        self.c_north, self.c_south, self.c_far = yp * 2 + xl, ym * 2 + xl, yo * 2 + xl
        self.c_north_mate, self.c_south_mate = yp * 2 + 1 - xl, ym * 2 + 1 - xl
        self.c_far_mate = yo * 2 + 1 - xl
        self.north, self.south, self.side = eight_peers(y, xl, z, fs)
        self.up, self.down = (ctx_of(y, xl, self.zp), fs), (ctx_of(y, xl, self.zm), fs)
        self.opposite = (ctx_of(y, xl, self.zo), fs)
        self.twin = (ctx, fs + 1 - 2 * self.core)
        self.near = (ctx_of(y, 1 - xl, z), lax.rem(fs + 2, 4))
        self.plane = []
        for dh in (1, 0):
            for dy in (2, 1, 3, 0):
                for dx in (1, 0):
                    if dh or dy or dx:
                        hh = lax.rem(self.xh + dh, 2)
                        c = lax.rem(y + dy, 4) * 2 + lax.rem(xl + dx, 2)
                        self.plane.append((hh, c, (c * 4 + z, hh * 2 + self.core)))
        self.row = []
        for dh, dx in ((1, 0), (1, 1), (0, 1)):
            hh, xx = lax.rem(self.xh + dh, 2), lax.rem(xl + dx, 2)
            self.row.append((hh, xx, ((y * 2 + xx) * 4 + z, hh * 2 + self.core)))
        self.column = [(yy, (ctx_of(yy, xl, z), fs)) for yy in (yo, yp, ym)]
        self.eight = [(c, device) for hh, c, device in self.plane[8:]]


def layer_kernel(
    places, tok, cot, wqkv, wup, wdown, wdense, vec,
    or_o, ir_o, fa_o, qa_o, qb_o,
    X, G, WQ, WU, WD, WE, sq, su, sd, se, LA, LB, N, R, CS, bias,
    KVA, QGA, EC, GE, GH, SL, GU, GD, IB, SU,
    FT, FQ, FY, FX, FR, FPS,
    KP, QP0, LL, LT, raw, gap, TOP, SUM, MIX, ACC, DKV, OUT,
    F1, MA, MB, H1, H2, MF, NF, SF,
    AT, OPB, IPB, GL, GQ, VS, EP, ET, EQ, EY, EX, ER, QP, QT, QB, QR, QPS_A, QPS_B,
    ssem, rsem, lsem, wsem,
):
    w = Where()
    wire = Wire(ssem, rsem, lsem)
    ctx, fs, y, xl, z, core = w.ctx, w.fs, w.y, w.xl, w.z, w.core
    zp, zm, zo, up, down, twin, near = w.zp, w.zm, w.zo, w.up, w.down, w.twin, w.near
    other = lax.rem(fs + 2, 4)
    parity = lax.rem(z, 2)

    load_x = pltpu.make_async_copy(tok, X.at[z], wsem.at[0])
    load_x.start()
    loads_q = []
    for t in range(3):
        for i in range(3):
            at = pl.multiple_of(t * 768 + 256 * i + 128 * lax.div(z, 2), 128)
            loads_q.append(
                pltpu.make_async_copy(
                    wqkv.at[:, pl.ds(at, 128)], sq.at[:, pl.ds((3 * t + i) * 128, 128)], wsem.at[1 + 3 * t + i]
                )
            )
    for copy in loads_q:
        copy.start()
    load_g = pltpu.make_async_copy(cot, G.at[z], wsem.at[10])
    load_g.start()
    spare = jnp.minimum(lax.rem(z + fs, 4), 2)
    load_e = pltpu.make_async_copy(wdense.at[pl.ds(pl.multiple_of(spare * 64, 64), 64)], se, wsem.at[11])
    load_e.start()
    loads_u = []
    for i in range(4):
        at = pl.multiple_of(768 * i + 192 * z - 64 * parity, 128)
        loads_u.append(
            pltpu.make_async_copy(wup.at[:, pl.ds(at, 256)], su.at[:, pl.ds(256 * i, 256)], wsem.at[12 + i])
        )
    for copy in loads_u:
        copy.start()
    load_d = pltpu.make_async_copy(wdown.at[pl.ds(pl.multiple_of(z * 192, 64), 192)], sd, wsem.at[16])
    load_d.start()

    greet([up, down, w.opposite, twin] + [device for _, _, device in w.plane])

    load_x.wait()
    x_up, x_down = wire.send(X.at[z], X.at[z], up), wire.send(X.at[z], X.at[z], down)
    for copy in loads_q:
        copy.wait()

    def piece(stage, at, odd):
        return stage[:, 128 * at + 64 * odd : 128 * at + 64 * odd + 64]

    for odd in range(2):

        @pl.when(parity == odd)
        def _():
            parts = []
            for i in range(3):
                parts += [piece(sq, 3 + i, odd), piece(sq, 6 + i, odd)]
            parts += [piece(sq, i, odd) for i in range(3)] + [jnp.zeros((192, 64), F32)]
            WQ[fs] = jnp.concatenate(parts, 1).astype(LOW)

    q_near = wire.send(WQ.at[fs], WQ.at[fs], near)
    q_twin = wire.send(WQ.at[fs], WQ.at[fs], twin)
    first = lax.div(ctx, 4) * 512
    CS[0], CS[1] = angle_lanes([places[0, first + 64 * i] for i in range(8)], 512)

    def low_block(start):
        block = places[0, start] >> 6
        return block < 32, jnp.where(block < 32, block, 63 - block)

    runs = [low_block(first + 128 * i) for i in range(4)]
    row = lax.broadcasted_iota(jnp.int32, (128, 128), 0)
    for b in range(2):
        spot = jnp.where(row < 64, runs[2 * b][1], runs[2 * b + 1][1])
        QP0[b] = spot * 64 + (row & 63)
        QP0[2 + b] = (63 - spot) * 64 + (row & 63)
    lane = lax.broadcasted_iota(jnp.int32, (8, 256), 1)
    line = lax.broadcasted_iota(jnp.int32, (8, 256), 0)
    for c in range(8):
        spot = jnp.zeros((8, 256), jnp.int32)
        for i in range(4):
            spot = jnp.where((lane >> 6) == i, low_block(512 * c + 128 * i)[1], spot)
        KP[c] = jnp.where(line == 0, spot, 63 - spot) * 64 + (lane & 63)

    gain_a, shift_a, gain_b, shift_b = (vec[i : i + 1, :] for i in range(4))

    def norms(zz):
        rows = pl.ds(pl.multiple_of(128 * zz, 128), 128)
        x = X[zz].astype(F32)
        centered = x - jnp.mean(x, -1, keepdims=True)
        inv = lax.rsqrt(jnp.mean(centered * centered, -1, keepdims=True) + norm_eps)
        normed = centered * inv
        N[rows, :] = normed
        R[rows, :] = jnp.broadcast_to(inv, (128, 128))
        LA[rows, :] = (normed * gain_a + shift_a).astype(LOW)
        LB[rows, :] = (normed * gain_b + shift_b).astype(LOW)

    norms(z)
    load_e.wait()
    WE[fs] = se[...].astype(LOW)
    for copy in loads_u:
        copy.wait()
    for odd in range(2):

        @pl.when(parity == odd)
        def _():
            parts = [su[:, 256 * i + 64 * odd : 256 * i + 64 * odd + 192] for i in range(4)]
            WU[fs] = jnp.concatenate(parts, 1).astype(LOW)

    load_d.wait()
    WD[fs] = sd[...].astype(LOW)
    load_g.wait()

    for zz in range(4):

        @pl.when(z == zz)
        def _():
            def head(row, i):
                return vec[row : row + 1, 64 * (zz + 4 * i) : 64 * (zz + 4 * i) + 64]

            parts = []
            for i in range(3):
                parts += [head(5, i), head(6, i)]
            parts += [head(4, i) for i in range(3)] + [jnp.zeros((1, 64), F32)]
            bias[0:1, 0:640] = jnp.concatenate(parts, 1)
            bias[1:2, :] = jnp.concatenate(
                [vec[8 + i : 9 + i, 192 * zz : 192 * zz + 192] for i in range(4)], 1
            )

    def relay(slab, from_down, from_up):
        from_down.wait_recv()
        part = slab.at[zm, pl.ds(0, 64)]
        a = wire.send(part, part, up)
        from_up.wait_recv()
        part = slab.at[zp, pl.ds(64, 64)]
        return [a, wire.send(part, part, down)]

    def forward(slab, copy):
        copy.wait_recv()
        return wire.send(slab.at[other], slab.at[other], twin)

    wire.left(x_up, x_down)
    g_up, g_down = wire.send(G.at[z], G.at[z], up), wire.send(G.at[z], G.at[z], down)
    x_far = relay(X, x_up, x_down)
    norms(zm)
    norms(zp)
    wire.left(q_near)
    e_near, e_twin = wire.send(WE.at[fs], WE.at[fs], near), wire.send(WE.at[fs], WE.at[fs], twin)
    u_near, u_twin = wire.send(WU.at[fs], WU.at[fs], near), wire.send(WU.at[fs], WU.at[fs], twin)
    q_far = forward(WQ, q_near)
    for copy in x_far:
        copy.wait_recv()
    norms(zo)
    g_far = relay(G, g_up, g_down)
    q_twin.wait_recv()
    q_far.wait_recv()
    low256 = lanes(256) < 64

    def arrange(value, i):
        a, b = value[:64], value[64:]
        return jnp.where(runs[i][0], a, b), jnp.where(runs[i][0], b, a)

    for t in range(2):
        rows = slice(256 * t, 256 * t + 256)
        linear = dot(LA[rows, :], WQ[...].reshape(768, 640)) + bias[0:1, 0:640]
        cos_wide, sin_wide = CS[0, rows, :], CS[1, rows, :]
        ab, last = linear[:, 384:512], linear[:, 512:640]
        for h, u in enumerate((ab, pltpu.roll(ab, 64, 1), last)):
            keys = turn(linear[:, 128 * h : 128 * h + 128], cos_wide, sin_wide)
            asks = jnp.where(low256, turn(u, cos_wide, sin_wide), 0.0)
            for i in (2 * t, 2 * t + 1):
                part = slice(128 * (i - 2 * t), 128 * (i - 2 * t) + 128)
                for half, value in enumerate(arrange(keys[part], i)):
                    at = 256 * half + 64 * i
                    KVA[w.c, h, at : at + 64, :] = value.astype(LOW)
                for half, value in enumerate(arrange(asks[part], i)):
                    at = 256 * half + 64 * i
                    QGA[at : at + 64, 128 * h : 128 * h + 128] = value.astype(LOW)

    spread = Spread(wire, None, None, w)

    def gather(h):
        return spread.around(lambda c: KVA.at[c, h], lambda r, half: r.at[pl.ds(256 * half, 256)])

    kv = [gather(h) for h in range(3)]
    next(kv[0])
    next(kv[2])
    e_far = forward(WE, e_near)
    for copy in g_far + [e_twin, e_far]:
        copy.wait_recv()
    EC[192:, :] = jnp.zeros((64, 768), LOW)
    for i in range(3):
        EC[64 * i : 64 * i + 64, :] = WE[i + jnp.where(i >= 3 - z, 1, 0)]
    for t in range(2):
        grad = dot_rows(G[pl.ds(2 * t, 2)].reshape(256, 768), EC[...])
        ab, last = grad[:, :128], grad[:, 128:]
        for h, u in enumerate((pltpu.roll(ab, 64, 1), ab, pltpu.roll(last, 64, 1))):
            for i in (2 * t, 2 * t + 1):
                part = slice(128 * (i - 2 * t), 128 * (i - 2 * t) + 128)
                for half, value in enumerate(arrange(u[part], i)):
                    at = slice(256 * half + 64 * i, 256 * half + 64 * i + 64)
                    col = slice(128 * h, 128 * h + 128)
                    QGA[at, col] = jnp.where(low256[:64], QGA[at, col], value.astype(LOW))

    wire.left(u_near)
    d_near, d_twin = wire.send(WD.at[fs], WD.at[fs], near), wire.send(WD.at[fs], WD.at[fs], twin)
    u_far = forward(WU, u_near)
    for copy in (u_twin, u_far):
        copy.wait_recv()

    def feed_up(t):
        rows = pl.ds(256 * t, 256)
        hidden = dot(LB[rows, :], WU[...].reshape(768, 768)) + bias[1:2, :]
        half = 0.5 + 0.5 * erf(hidden * 0.7071067811865476)
        GE[rows, :] = (hidden * half).astype(LOW)
        SL[rows, :] = half + hidden * (jnp.exp(hidden * hidden * -0.5) * 0.3989422804014327)

    down_parts = ((GD, 1, 0, 64, 64, 768), (GD, 1, 64, 128, 0, 1536))
    up_parts = ((GU, 0, 0, 128, 0, 0), (GU, 0, 128, 64, 0, 768))

    def exchange(slab, k):
        copies = []
        for h in range(2):
            at = pl.multiple_of(192 * (2 * h + 1 - core), 64)
            copies.append(wire.send(slab.at[pl.ds(at, 192)], FT.at[k, h], twin))
        return copies

    def add_pair(copies, parts):
        for copy in copies:
            copy.wait_recv()
        for slab, k, row, size, to, col in parts:
            for h in range(2):
                at = pl.multiple_of(192 * (2 * h + core) + row, 64)
                for r in range(0, size, 16):
                    total = slab[pl.ds(pl.multiple_of(at + r, 16), 16), :].astype(F32) + FT[
                        k, h, row + r : row + r + 16, :
                    ].astype(F32)
                    FQ[(to + r) // 32, h, (to + r) // 16 % 2, :, col : col + 768] = total.astype(LOW)

    feed_up(0)
    next(kv[0])
    feed_up(1)
    next(kv[1])
    d_far = forward(WD, d_near)
    for copy in (d_twin, d_far):
        copy.wait_recv()
    for t in range(2):
        rows = pl.ds(256 * t, 256)
        grad = G[2 * t : 2 * t + 2].reshape(256, 768)
        GH[rows, :] = (dot_rows(grad, WD[...].reshape(768, 768)) * SL[rows, :]).astype(LOW)
    next(kv[0])

    @pl.loop(0, 3)
    def _(j):
        at = pl.ds(pl.multiple_of(256 * j, 256), 256)
        GD[at, :] = dot_down(GE[:, at], G[...].reshape(512, 768)).astype(LOW)

    paired_down = exchange(GD, 1)
    next(kv[2])

    @pl.loop(0, 3)
    def _(j):
        at = pl.ds(pl.multiple_of(256 * j, 256), 256)
        GU[at, :] = dot_down(LB[:, at], GH[...]).astype(LOW)

    paired_up = exchange(GU, 0)
    next(kv[1])

    low = lanes(512) < 64
    same = (
        lax.broadcasted_iota(jnp.int32, (256, 256), 0) == lax.broadcasted_iota(jnp.int32, (256, 256), 1)
    )
    same = jnp.where(same, 1.0, 0.0).astype(LOW)
    deep = lax.broadcasted_iota(jnp.int32, (128, 256), 0) < 64

    meets = ((0,), (0,), (0, 1), (0, 1))
    spots = {}
    for b in range(4):
        for side in meets[b]:
            spots[b, side] = len(spots)

    def keys_of(c, h, side):
        return KVA[c, h, 256 * side : 256 * side + 256, :]

    def twice(value):
        return jnp.concatenate([value, value], 1)

    def score(h):
        for b in range(4):
            part = QGA[128 * b : 128 * b + 128, 128 * h : 128 * h + 128]
            none = jnp.zeros_like(part)
            pile = jnp.concatenate(
                [jnp.where(low256[:128], part, none), jnp.where(low256[:128], none, part)], 0
            )
            LL[b] = pile
            LT[b] = dot_rows(same[:128, :128], pile).astype(LOW)
        TOP[...] = jnp.full_like(TOP, masked)

        @pl.loop(0, 8)
        def _(c):
            for b in range(4):
                top = TOP[b]
                for side in meets[b]:
                    pair = dot_rows(LL[b], keys_of(c, h, side))
                    scores = pair[:128]
                    if b < 2 or side:
                        seen = KP[c, side : side + 1, :] <= twice(QP0[b])
                        scores = jnp.where(seen, scores, masked)
                    raw[c, spots[b, side]] = scores
                    gap[c, spots[b, side]] = pair[128:]
                    top = jnp.maximum(top, jnp.maximum(scores[:, :128], scores[:, 128:]))
                TOP[b] = top

    def weigh():
        for b in range(4):
            TOP[b] = jnp.broadcast_to(jnp.max(TOP[b], -1, keepdims=True), (128, 128))
        SUM[...] = jnp.zeros_like(SUM)
        MIX[...] = jnp.zeros_like(MIX)

        @pl.loop(0, 8)
        def _(c):
            for b in range(4):
                total, blend = SUM[b], MIX[b]
                for side in meets[b]:
                    i = spots[b, side]
                    e = jnp.exp((raw[c, i] - twice(TOP[b])) * 0.125)
                    raw[c, i] = e
                    mix = e * gap[c, i]
                    total = total + (e[:, :128] + e[:, 128:])
                    blend = blend + (mix[:, :128] + mix[:, 128:])
                SUM[b] = total
                MIX[b] = blend

    def settle(h):
        for b in range(4):
            inverse = 1.0 / jnp.sum(SUM[b], -1, keepdims=True)
            shared = jnp.sum(MIX[b], -1, keepdims=True) * inverse
            SUM[b] = jnp.broadcast_to(inverse, (128, 128))
            MIX[b] = jnp.broadcast_to(shared, (128, 128))
        ACC[...] = jnp.zeros_like(ACC)

        @pl.loop(0, 8)
        def _(c):
            grown = [None, None]
            for b in range(4):
                total = ACC[b]
                for side in meets[b]:
                    i = spots[b, side]
                    probs = raw[c, i] * twice(SUM[b])
                    slope = probs * (gap[c, i] - twice(MIX[b]))
                    pile = jnp.concatenate([slope.astype(LOW), probs.astype(LOW)], 0)
                    total = total + dot(pile, keys_of(c, h, side))
                    part = dot(LT[b], pile)
                    grown[side] = part if grown[side] is None else grown[side] + part
                ACC[b] = total
            for side, g in enumerate(grown):
                g = jnp.where(deep, g * 0.125, g).astype(LOW)
                DKV[c, h, 256 * side : 256 * side + 256, :] = dot_rows(same, g).astype(LOW)

        done = [jnp.where(low256[:128], ACC[b, :128] * 0.125, ACC[b, 128:]) for b in range(4)]
        for i in range(4):
            at = slice(64 * (i % 2), 64 * (i % 2) + 64)
            a, b = done[i // 2][at], done[2 + i // 2][at]
            at = slice(128 * h, 128 * h + 128)
            OUT[128 * i : 128 * i + 64, at] = jnp.where(runs[i][0], a, b)
            OUT[128 * i + 64 : 128 * i + 128, at] = jnp.where(runs[i][0], b, a)

    def tree(h):
        t1 = wire.send(DKV.at[w.c_far_mate, h], F1.at[h], w.side)
        t2 = wire.send(DKV.at[w.c_north_mate, h], MA.at[h], w.north)
        t3 = wire.send(DKV.at[w.c_south_mate, h], MB.at[h], w.south)
        yield
        t1.wait_recv()
        DKV[w.c_far, h] = (DKV[w.c_far, h].astype(F32) + F1[h].astype(F32)).astype(LOW)
        t4 = wire.send(DKV.at[w.c_far, h, pl.ds(0, 256)], H1.at[h], w.south)
        t5 = wire.send(DKV.at[w.c_far, h, pl.ds(256, 256)], H2.at[h], w.north)
        t2.wait_recv()
        t3.wait_recv()
        total = DKV[w.c_mate, h].astype(F32) + MA[h].astype(F32) + MB[h].astype(F32)
        DKV[w.c_mate, h] = total.astype(LOW)
        t6 = wire.send(DKV.at[w.c_mate, h], MF.at[h], w.side)
        yield
        t4.wait_recv()
        total = DKV[w.c_south, h, 0:256, :].astype(F32) + H1[h].astype(F32)
        DKV[w.c_south, h, 0:256, :] = total.astype(LOW)
        t7 = wire.send(DKV.at[w.c_south, h], NF.at[h], w.south)
        t5.wait_recv()
        total = DKV[w.c_north, h, 256:512, :].astype(F32) + H2[h].astype(F32)
        DKV[w.c_north, h, 256:512, :] = total.astype(LOW)
        t8 = wire.send(DKV.at[w.c_north, h], SF.at[h], w.north)
        yield
        for copy in (t6, t7, t8):
            copy.wait_recv()

    def add_up(parts):
        total = parts[0].astype(F32)
        for part in parts[1:]:
            total = total + part.astype(F32)
        return total.astype(LOW)

    def ladder(packet, fy, fx, fr, out):
        copies = [wire.send(packet.at[yy], fy.at[y], device) for yy, device in w.column]
        fy[y] = packet[y]
        yield
        for copy in copies:
            copy.wait_recv()
        for h in range(2):
            for i in range(2):
                fx[h, i] = add_up([fy[j, h, i] for j in range(4)])
        me = w.xh * 2 + xl
        copies = [wire.send(fx.at[hh, xx], fr.at[me], device) for hh, xx, device in w.row]
        fr[me] = fx[w.xh, xl]
        yield
        for copy in copies:
            copy.wait_recv()
        out(add_up([fr[j] for j in range(4)]))

    def drain(steps):
        for _ in steps:
            pass

    def keep_piece(total):
        FPS[...] = total

    def keep_dense(total):
        QPS_B[:, 384:768] = total

    def arrived(copies):
        for copy in copies:
            copy.wait_recv()

    def arrived(copies):
        for copy in copies:
            copy.wait_recv()

    fl = ladder(FQ, FY, FX, FR, keep_piece)
    fa = Spread(wire, FPS, fa_o, w).eight_first()
    trees = [tree(h) for h in range(3)]
    drain(kv[0])
    score(0)
    add_pair(paired_down, down_parts)
    add_pair(paired_up, up_parts)
    next(fl)
    weigh()
    next(kv[1])
    settle(0)
    next(kv[2])
    drain(kv[1])
    score(1)
    next(trees[0])
    weigh()
    next(fl)
    settle(1)
    next(trees[0])
    drain(fl)
    next(fa)
    drain(kv[2])
    score(2)
    next(fa)
    weigh()
    next(trees[1])
    next(fa)
    settle(2)
    next(trees[2])
    next(fa)

    o0, o1, o2 = (OUT[:, 128 * i : 128 * i + 128] for i in range(3))
    AT[:, :128] = jnp.where(low, pltpu.roll(o0, 64, 1), o1).astype(LOW)
    AT[:, 128:] = jnp.where(low, pltpu.roll(o2, 64, 1), 0.0).astype(LOW)
    ge = dot_down(AT[...], G[...].reshape(512, 768))
    for i in range(4):
        empty = 3 - z
        after = ge[64 * i - 64 : 64 * i] if i else ge[0:64]
        before = ge[64 * i : 64 * i + 64] if i < 3 else ge[128:192]
        slot = jnp.where(i > empty, after, before)
        slot = jnp.where(i == empty, 0.0, slot).astype(LOW)
        EP[i, 0:64, :] = slot[:, :384]
        EP[i, 64:128, :] = slot[:, 384:]
    paired_e = [wire.send(EP.at[2 * h + 1 - core], ET.at[h], twin) for h in range(2)]
    next(trees[1])
    next(trees[0])
    SU[...] = jnp.zeros_like(SU)
    for t in range(2):
        rows = pl.ds(256 * t, 256)
        back = GH[rows, :]
        grad_ln = dot_rows(back, WU[...].reshape(768, 768))
        normed = N[rows, :]
        SU[0:1, :] += jnp.sum(grad_ln * normed, 0, keepdims=True)
        SU[1:2, :] += jnp.sum(grad_ln, 0, keepdims=True)
        SU[2:3, :] += jnp.sum(back.astype(F32), 0, keepdims=True)
        IB[rows, :] = norm_back(grad_ln, normed, R[rows, 0:1], gain_b)
    next(trees[2])
    next(trees[1])
    arrived(paired_e)
    for h in range(2):
        for c in range(8):
            at = slice(16 * c, 16 * c + 16)
            EQ[c // 2, h, c % 2] = add_up([EP[2 * h + core, at, :], ET[h, at, :]])
    el = ladder(EQ, EY, EX, ER, keep_dense)
    next(el)
    for i in range(4):
        rows = slice(128 * i, 128 * i + 128)
        total = dot(GE[rows, :], WD[...].reshape(768, 768)) + dot(AT[rows, :], EC[...])
        OPB[i] = total.astype(LOW)
    ring = ((zo, w.opposite), (zp, up), (zm, down))
    o_sent = [wire.send(OPB.at[zz], or_o.at[z], device) for zz, device in ring]
    wire.keep(OPB.at[z], or_o.at[z])
    next(trees[2])

    cos_wide, sin_wide = CS[0], -CS[1]
    u0, u1, u2 = (turn(u, cos_wide, sin_wide) for u in (o0, o1, o2))
    GL[:, 384:512] = jnp.where(low, u0, pltpu.roll(u1, 64, 1)).astype(LOW)
    GL[:, 512:640] = jnp.where(low, u2, 0.0).astype(LOW)

    def own_sum(h):
        drain(trees[h])
        total = DKV[w.c, h].astype(F32) + MF[h].astype(F32) + NF[h].astype(F32) + SF[h].astype(F32)
        for i in range(4):
            a, b = total[64 * i : 64 * i + 64], total[256 + 64 * i : 320 + 64 * i]
            rows = slice(128 * i, 128 * i + 128)
            value = jnp.concatenate([jnp.where(runs[i][0], a, b), jnp.where(runs[i][0], b, a)], 0)
            value = turn(value, CS[0, rows, :], -CS[1, rows, :])
            GL[rows, 128 * h : 128 * h + 128] = value.astype(LOW)

    def project(cols):
        for t in range(2):
            rows = slice(256 * t, 256 * t + 256)
            yield rows, dot_rows(GL[rows, cols], WQ[:, :, cols].reshape(768, -1))

    def weight_part(cols):
        @pl.loop(0, 3)
        def _(j):
            at = pl.ds(pl.multiple_of(256 * j, 256), 256)
            GQ[at, cols] = dot_down(LA[:, at], GL[:, cols]).astype(LOW)

    own_sum(0)
    own_sum(1)
    for rows, value in project(slice(0, 256)):
        SL[rows, :] = value
    for rows, value in project(slice(384, 640)):
        SL[rows, :] = SL[rows, :] + value
    weight_part(slice(0, 256))
    weight_part(slice(384, 640))
    VS[...] = jnp.zeros_like(VS)

    def note(row, values):
        for j in range(values.shape[1] // 128):
            VS[6 * row + j : 6 * row + j + 1, :] = values[:, 128 * j : 128 * j + 128]

    note(2, SU[0:1, :])
    note(3, SU[1:2, :])
    note(5, SU[2:3, :])
    note(6, jnp.sum(G[z].astype(F32), 0, keepdims=True))
    next(el)
    own_sum(2)
    dots = jnp.zeros((1, 768), F32)
    plain = jnp.zeros((1, 768), F32)
    for rows, value in project(slice(256, 384)):
        grad_ln = SL[rows, :] + value
        SL[rows, :] = grad_ln
        dots = dots + jnp.sum(grad_ln * N[rows, :], 0, keepdims=True)
        plain = plain + jnp.sum(grad_ln, 0, keepdims=True)
    note(0, dots)
    note(1, plain)
    note(4, jnp.sum(GL[...].astype(F32), 0, keepdims=True))
    weight_part(slice(256, 384))
    for i in range(4):
        QP[i, :, 0:640] = GQ[192 * i : 192 * i + 128, :]
        QP[i, 0:64, 640:1024] = GQ[192 * i + 128 : 192 * i + 192, 0:384]
        QP[i, 64:128, 640:896] = GQ[192 * i + 128 : 192 * i + 192, 384:640]
        QP[i, 64:128, 896:1024] = VS[...].astype(LOW)
    paired_q = [wire.send(QP.at[2 * h + 1 - core], QT.at[h], twin) for h in range(2)]
    next(fa)
    drain(el)
    arrived(paired_q)
    for h in range(2):
        for c in range(8):
            at = slice(16 * c, 16 * c + 16)
            QB[h, c] = add_up([QP[2 * h + core, at, :], QT[h, at, :]])
    me = w.xh * 8 + w.c
    q_plane = [wire.send(QB.at[hh, c], QR.at[me], device) for hh, c, device in w.plane]
    QR[me] = QB[w.xh, w.c]
    for t in range(4):
        rows = slice(128 * t, 128 * t + 128)
        total = norm_back(SL[rows, :], N[rows, :], R[rows, 0:1], gain_a) + IB[rows, :]
        IPB[t] = total.astype(LOW)
    i_sent = [wire.send(IPB.at[zz], ir_o.at[z], device) for zz, device in ring]
    wire.keep(IPB.at[z], ir_o.at[z])
    for copy in q_plane:
        copy.wait_recv()
    total = add_up([QR[j] for j in range(16)])
    QPS_A[...] = total[:, :640]
    QPS_B[:, :384] = total[:, 640:]
    qa, qb = Spread(wire, QPS_A, qa_o, w).eight_first(), Spread(wire, QPS_B, qb_o, w).ring_first()
    for steps in (qb, qa, qb, qa, qb, qa, qb, qa, qa):
        next(steps)
    for steps in (fa, qb, qa):
        drain(steps)
    for copy in o_sent + i_sent:
        copy.wait_recv()
    wire.finish()


def layer(places, tok, cot, wqkv, wup, wdown, wdense, vec):
    outs = [
        ((4, 128, 768), LOW),
        ((4, 128, 768), LOW),
        ((4, 8, 16, 2304), LOW),
        ((4, 8, 16, 640), LOW),
        ((8, 4, 16, 768), LOW),
    ]
    scratch = [
        *[((4, 128, 768), LOW)] * 2,
        ((4, 192, 640), LOW),
        *[((4, 192, 768), LOW)] * 2,
        ((4, 64, 768), LOW),
        ((192, 1152), F32),
        ((192, 1024), F32),
        ((192, 768), F32),
        ((64, 768), F32),
        *[((512, 768), LOW)] * 2,
        ((512, 768), F32),
        ((512, 128), F32),
        ((2, 512, 128), F32),
        ((8, 768), F32),
        ((8, 3, 512, 128), LOW),
        ((512, 384), LOW),
        ((256, 768), LOW),
        *[((512, 768), LOW)] * 2,
        ((512, 768), F32),
        *[((768, 768), LOW)] * 2,
        ((512, 768), F32),
        ((8, 768), F32),
        ((2, 2, 192, 768), LOW),
        ((4, 2, 2, 16, 2304), LOW),
        ((4, 2, 2, 16, 2304), LOW),
        ((2, 2, 16, 2304), LOW),
        ((4, 16, 2304), LOW),
        ((16, 2304), LOW),
        ((8, 8, 256), jnp.int32),
        ((4, 128, 128), jnp.int32),
        ((4, 256, 128), LOW),
        ((4, 128, 256), LOW),
        *[((8, 6, 128, 256), F32)] * 2,
        *[((4, 128, 128), F32)] * 3,
        ((4, 256, 128), F32),
        ((8, 3, 512, 128), LOW),
        ((512, 384), F32),
        *[((3, 512, 128), LOW)] * 3,
        *[((3, 256, 128), LOW)] * 2,
        *[((3, 512, 128), LOW)] * 3,
        ((512, 256), LOW),
        *[((4, 128, 768), LOW)] * 2,
        ((512, 640), LOW),
        ((768, 640), LOW),
        ((64, 128), F32),
        ((4, 128, 384), LOW),
        ((2, 128, 384), LOW),
        ((4, 2, 2, 16, 384), LOW),
        ((4, 2, 2, 16, 384), LOW),
        ((2, 2, 16, 384), LOW),
        ((4, 16, 384), LOW),
        ((4, 128, 1024), LOW),
        ((2, 128, 1024), LOW),
        ((2, 8, 16, 1024), LOW),
        ((16, 16, 1024), LOW),
        ((16, 640), LOW),
        ((16, 768), LOW),
    ]
    anywhere = pl.BlockSpec(memory_space=pl.ANY)
    sends = 168
    return pl.pallas_call(
        layer_kernel,
        out_shape=[jax.ShapeDtypeStruct(s, d) for s, d in outs],
        in_specs=[pl.BlockSpec(memory_space=pltpu.SMEM)]
        + [anywhere] * 6
        + [pl.BlockSpec(memory_space=pltpu.VMEM)],
        out_specs=[anywhere] * len(outs),
        scratch_shapes=[pltpu.VMEM(s, d) for s, d in scratch]
        + [
            pltpu.SemaphoreType.DMA((sends,)),
            pltpu.SemaphoreType.DMA((sends,)),
            pltpu.SemaphoreType.DMA((16,)),
            pltpu.SemaphoreType.DMA((17,)),
        ],
        compiler_params=pltpu.CompilerParams(
            collective_id=0, has_side_effects=True, vmem_limit_bytes=60 * 1024 * 1024
        ),
    )(places, tok, cot, wqkv, wup, wdown, wdense, vec)


def step_kernel(
    spot, tok, cot, ors, irs, fa, qa, qb, vec, vec_m, vec_s,
    qw, qm, qs, ew, em, es, uw, um, us, dw, dm, ds,
    blk_o, inp_o, vw_o, vm_o, vs_o,
    qw_o, qm_o, qs_o, ew_o, em_o, es_o, uw_o, um_o, us_o, dw_o, dm_o, ds_o,
    TO, CO, OR, IR, FA, QA, QB, VW, VM, VS, QW, QM, QS, EW, EM, ES, UW, UM, US, DW, DM, DS,
    BL, IN, isem, osem,
):
    count = [0, 0]

    def start(src, dst, sem, which):
        copy = pltpu.make_async_copy(src, dst, sem.at[count[which]])
        count[which] += 1
        copy.start()
        return copy

    def arrive(pairs):
        return [start(a, b, isem, 0) for a, b in pairs]

    def cut_rows(pairs, at, size):
        return [(a.at[pl.ds(at, size)], b.at[pl.ds(at, size)]) for a, b in pairs]

    up, down = ((uw, UW), (um, UM), (us, US)), ((dw, DW), (dm, DM), (ds, DS))
    dense, qkv = ((ew, EW), (em, EM), (es, ES)), ((qw, QW), (qm, QM), (qs, QS))
    load_v = arrive(((vec, VW), (vec_m, VM), (vec_s, VS)))
    load_e = arrive(((qb, QB),) + dense)
    load_small = arrive(((tok, TO), (cot, CO), (ors, OR), (irs, IR)))
    load_u1 = arrive(((fa, FA), *cut_rows(up, 0, 128)))
    load_u2 = arrive(cut_rows(up, 128, 64))
    load_d1 = arrive(cut_rows(down, 0, 384))
    load_d2 = arrive(cut_rows(down, 384, 384))
    load_q = arrive(((qa, QA),) + tuple(cut_rows(qkv, 0, 128)))
    load_q2 = arrive(cut_rows(qkv, 128, 64))
    leaving = []

    def leave(pairs):
        leaving.extend(start(a, b, osem, 1) for a, b in pairs)

    def back_rows(pairs, at, size):
        leave((b.at[pl.ds(at, size)], a.at[pl.ds(at, size)]) for a, b in pairs)

    def wait(copies):
        for copy in copies:
            copy.wait()

    def update(slabs, rows, gradient, rate, decay):
        new = adamw(slabs[0][rows, :], slabs[1][rows, :], slabs[2][rows, :], gradient, rate, decay)
        for slab, value in zip(slabs, new):
            slab[rows, :] = value

    def rows_of(start_at, size=16):
        return pl.ds(pl.multiple_of(start_at, 16), size)

    def spread_up(parts):
        parts = [p.astype(F32) for p in parts]
        return jnp.concatenate([parts[z][:, 192 * i : 192 * i + 192] for i in range(4) for z in range(4)], 1)

    wait(load_v)
    wait(load_e)

    @pl.loop(0, 4)
    def _(c):
        for o in range(3):
            z = lax.rem(o + 4 - spot[0], 4)
            gradient = jnp.concatenate([QB[c, z, :, 384:768], QB[4 + c, z, :, 384:768]], 1).astype(F32)
            update((EW, EM, ES), rows_of(64 * o + 16 * c), gradient, 0.1, 0.1)

    leave(((EW, ew_o), (EM, em_o), (ES, es_o)))
    wait(load_small)
    BL[...] = (
        TO[...].astype(F32) + jnp.sum(OR[...].astype(F32), 0) + VW[7:8, :] + VW[12:13, :]
    ).astype(LOW)
    IN[...] = CO[...].astype(F32) + jnp.sum(IR[...].astype(F32), 0)
    leave(((BL, blk_o), (IN, inp_o)))
    wait(load_u1)

    @pl.loop(0, 8)
    def _(c):
        update((UW, UM, US), rows_of(16 * c), spread_up([FA[z, c, :, 0:768] for z in range(4)]), 0.03, 0.1)

    back_rows(((uw_o, UW), (um_o, UM), (us_o, US)), 0, 128)
    wait(load_u2)

    @pl.loop(0, 4)
    def _(c):
        gradient = spread_up([FA[z, c, :, 768:1536] for z in range(4)])
        update((UW, UM, US), rows_of(128 + 16 * c), gradient, 0.03, 0.1)

    back_rows(((uw_o, UW), (um_o, UM), (us_o, US)), 128, 64)

    for half, load in enumerate((load_d1, load_d2)):
        wait(load)

        @pl.loop(0, 8)
        def _(c):
            for z in (2 * half, 2 * half + 1):
                rows = rows_of(192 * z + 64 + 16 * c)
                update((DW, DM, DS), rows, FA[z, c, :, 1536:2304].astype(F32), 0.02, 0.1)

        @pl.loop(0, 4)
        def _(c):
            for z in (2 * half, 2 * half + 1):
                rows = rows_of(192 * z + 16 * c)
                update((DW, DM, DS), rows, FA[z, 4 + c, :, 768:1536].astype(F32), 0.02, 0.1)

        back_rows(((dw_o, DW), (dm_o, DM), (ds_o, DS)), 384 * half, 384)

    wait(load_q)
    low = lanes(16) < 64

    def spread_heads(groups):
        out = []
        for t in range(3):
            for i in range(3):
                for pair in range(2):
                    halves = []
                    for odd in range(2):
                        group = groups[2 * pair + odd]
                        if t == 0:
                            u, at = group[3 + i // 2], i % 2
                        else:
                            u, at = group[i], t - 1
                        halves.append(u if at == odd else pltpu.roll(u, 64, 1))
                    out.append(jnp.where(low, halves[0], halves[1]))
        return jnp.concatenate(out, 1)

    def cut(value):
        value = value.astype(F32)
        return [value[:, 128 * j : 128 * j + 128] for j in range(value.shape[1] // 128)]

    @pl.loop(0, 8)
    def _(c):
        groups = [cut(QA[z, c]) for z in range(4)]
        update((QW, QM, QS), rows_of(16 * c), spread_heads(groups), 0.03, 0.1)

    back_rows(((qw_o, QW), (qm_o, QM), (qs_o, QS)), 0, 128)
    wait(load_q2)

    @pl.loop(0, 4)
    def _(c):
        groups = [cut(QB[c, z, :, 0:384]) + cut(QB[4 + c, z, :, 0:256]) for z in range(4)]
        update((QW, QM, QS), rows_of(128 + 16 * c), spread_heads(groups), 0.03, 0.1)

    back_rows(((qw_o, QW), (qm_o, QM), (qs_o, QS)), 128, 64)

    notes = [QB[4:8, z, :, 256:384].astype(F32).reshape(64, 128) for z in range(4)]
    total = (notes[0] + notes[1]) + (notes[2] + notes[3])

    def line(values, row):
        return jnp.concatenate([values[6 * row + j : 6 * row + j + 1, :] for j in range(6)], 1)

    linear = [line(n, 4) for n in notes]
    heads = []
    for at in (lambda i: 384 + 64 * i, lambda i: 128 * i, lambda i: 128 * i + 64):
        heads.append(
            jnp.concatenate([linear[z][:, at(i) : at(i) + 64] for i in range(3) for z in range(4)], 1)
        )
    hidden = [line(n, 5) for n in notes]
    wide = [
        jnp.concatenate([hidden[z][:, 192 * i : 192 * i + 192] for z in range(4)], 1) for i in range(4)
    ]
    ends = line(total, 6)
    lines = [line(total, i) for i in range(4)] + heads + [ends] + wide + [ends]
    for i, gradient in enumerate(lines):
        row = slice(i, i + 1)
        update((VW, VM, VS), row, gradient, 0.2, 0.0)
    leave(((VW, vw_o), (VM, vm_o), (VS, vs_o)))
    wait(leaving)


def step(spot, small, parts, vectors, weights):
    anywhere = pl.BlockSpec(memory_space=pl.ANY)
    outs = [jax.ShapeDtypeStruct((128, 768), LOW), jax.ShapeDtypeStruct((128, 768), F32)]
    operands = [*small, *parts, *vectors, *weights]
    outs += [jax.ShapeDtypeStruct(v.shape, F32) for v in [*vectors, *weights]]
    return pl.pallas_call(
        step_kernel,
        out_shape=outs,
        in_specs=[pl.BlockSpec(memory_space=pltpu.SMEM)] + [anywhere] * len(operands),
        out_specs=[anywhere] * len(outs),
        scratch_shapes=[pltpu.VMEM(v.shape, v.dtype) for v in operands]
        + [pltpu.VMEM(o.shape, o.dtype) for o in outs[:2]]
        + [pltpu.SemaphoreType.DMA((40,)), pltpu.SemaphoreType.DMA((40,))],
        compiler_params=pltpu.CompilerParams(vmem_limit_bytes=VMEM_LIMIT),
    )(spot, *operands)


def norm_back(incoming, normed, inv_scale, gain_row):
    scaled = incoming * gain_row
    return inv_scale * (
        scaled
        - jnp.mean(scaled, -1, keepdims=True)
        - normed * jnp.mean(scaled * normed, -1, keepdims=True)
    )


def adamw(weight, moment, second, gradient, step_rate, decay_rate):
    moment_new = beta_first * moment + (1.0 - beta_first) * gradient
    second_new = beta_second * second + ((1.0 - beta_second) * gradient) * gradient
    size = jnp.sqrt(second_new * (1.0 / (1.0 - beta_second**STEP))) + adam_eps
    change = moment_new * (step_rate / (1.0 - beta_first**STEP)) / size
    return (weight * (1.0 - step_rate * decay_rate) - change, moment_new, second_new)


def dot(a, b):
    return jnp.dot(a, b, preferred_element_type=F32)


def dot_rows(a, b):
    return lax.dot_general(a, b, (((1,), (1,)), ((), ())), preferred_element_type=F32)


def dot_down(a, b):
    return lax.dot_general(a, b, (((0,), (0,)), ((), ())), preferred_element_type=F32)


def body(
    tokens,
    cotangent,
    positions,
    vectors,
    vectors_moment,
    vectors_second,
    qkv_weight,
    qkv_moment,
    qkv_second,
    dense_weight,
    dense_moment,
    dense_second,
    up_weight,
    up_moment,
    up_second,
    down_weight,
    down_moment,
    down_second,
):
    fs = lax.axis_index("fsdp")
    ors, irs, fa, qa, qb = layer(
        positions, tokens[0], cotangent[0], qkv_weight, up_weight, down_weight, dense_weight, vectors
    )
    block_out, input_grad, *new = step(
        fs.reshape(1).astype(jnp.int32),
        (tokens[0], cotangent[0], ors, irs),
        (fa, qa, qb),
        (vectors, vectors_moment, vectors_second),
        (
            qkv_weight,
            qkv_moment,
            qkv_second,
            dense_weight,
            dense_moment,
            dense_second,
            up_weight,
            up_moment,
            up_second,
            down_weight,
            down_moment,
            down_second,
        ),
    )
    return (block_out[None], input_grad[None], *new)


def solution(mesh):
    split = P("fsdp", None)
    act = P("fsdp", "ctx", None)
    return jax.shard_map(
        body,
        mesh=mesh,
        in_specs=(act, act, split, P(), P(), P()) + (split,) * 12,
        out_specs=(act, act, P(), P(), P()) + (split,) * 12,
        check_vma=False,
    )
```

```python
import jax
import jax.numpy as jnp
from jax import lax
from jax.experimental import pallas as pl
from jax.experimental.pallas import tpu as pltpu
from jax.sharding import PartitionSpec as P

HEADS = 12
ROT = 16
STEP = 10
MESH = pl.DeviceIdType.MESH
F32 = jnp.float32
LOW = jnp.bfloat16
VMEM_LIMIT = 56 * 1024 * 1024

masked = -1e30
norm_eps = 1e-05
adam_eps = 1e-08
beta_first = 0.9
beta_second = 0.95
log2e = 1.4426950408889634


def ctx_of(y, xl, z):
    return (lax.rem(y, 4) * 2 + lax.rem(xl, 2)) * 4 + lax.rem(z, 4)


def place():
    ctx = lax.axis_index("ctx")
    fs = lax.axis_index("fsdp")
    c = lax.div(ctx, 4)
    return ctx, fs, lax.div(c, 2), lax.rem(c, 2), lax.rem(ctx, 4)


def greet(devices):
    barrier = pltpu.get_barrier_semaphore()
    for device in devices:
        pl.semaphore_signal(barrier, inc=1, device_id=device, device_id_type=MESH)
    pl.semaphore_wait(barrier, len(devices))


class Wire:
    def __init__(self, send_sem, recv_sem, local_sem):
        self.send_sem, self.recv_sem, self.local_sem = send_sem, recv_sem, local_sem
        self.sent, self.kept, self.local, self.count = [], [], 0, 0

    def send(self, src, dst, device):
        at = self.count
        self.count += 1
        copy = pltpu.make_async_remote_copy(
            src_ref=src,
            dst_ref=dst,
            send_sem=self.send_sem.at[at],
            recv_sem=self.recv_sem.at[at],
            device_id=device,
            device_id_type=MESH,
        )
        copy.start()
        self.sent.append(copy)
        return copy

    def left(self, *copies):
        for copy in copies:
            copy.wait_send()
        self.sent = [s for s in self.sent if not any(s is c for c in copies)]

    def keep(self, src, dst):
        copy = pltpu.make_async_copy(src, dst, self.local_sem.at[self.local])
        self.local += 1
        copy.start()
        self.kept.append(copy)
        return copy

    def finish(self):
        for copy in self.sent:
            copy.wait_send()
        for copy in self.kept:
            copy.wait()


def eight_peers(y, xl, z, fs):
    return [
        (ctx_of(lax.rem(y + 1, 4), xl, z), fs),
        (ctx_of(lax.rem(y + 3, 4), xl, z), fs),
        (ctx_of(y, 1 - xl, z), fs),
    ]


def erf(x):
    x = jnp.clip(x, -3.832506856900711, 3.832506856900711)
    s = x * x
    top = jnp.full_like(x, 0.00022905065861350646)
    for k in (0.0034082910107109506, 0.050955695062380861, 0.18520832239976145, 1.128379143519084):
        top = top * s + k
    low = jnp.full_like(x, -1.1791602954361697e-7)
    for k in (0.000023547966471313185, 0.0010179625278914885, 0.014070470171167667, 0.11098505178285362, 0.49746925110067538, 1.0):
        low = low * s + k
    return x * top / low


def lanes(rows, width=128):
    return lax.broadcasted_iota(jnp.int32, (rows, width), 1)


def turn(u, cos_wide, sin_wide):
    lane = lanes(u.shape[0])
    up = pltpu.roll(u, 120, 1) * jnp.where(lane < 8, -sin_wide, 0.0)
    down = pltpu.roll(u, 8, 1) * jnp.where(lane < 8, 0.0, sin_wide)
    return u * cos_wide + up + down


def angle_lanes(start, rows):
    lane = lanes(rows)
    row = lax.broadcasted_iota(jnp.int32, (rows, 128), 0)
    spot = row & 63
    for i, first in enumerate(start):
        spot = spot + jnp.where((row >> 6) == i, first, 0)
    power = (lane & 7).astype(F32) * (2.0 / ROT)
    frequency = jnp.where(lane < ROT, jnp.exp(power * -9.210340371976184), 0.0)
    angle = spot.astype(F32) * frequency
    return jnp.cos(angle), jnp.sin(angle)


class Spread:
    def __init__(self, wire, piece, out, where):
        self.wire, self.piece, self.out, self.w = wire, piece, out, where

    def around(self, slab, halves):
        w, wire = self.w, self.wire
        me = slab(w.c)
        a, b = wire.send(me, me, w.north), wire.send(me, me, w.south)
        x = wire.send(me, me, w.side)
        yield
        x.wait_recv()
        mate = slab(w.c_mate)
        p1, p2 = wire.send(mate, mate, w.north), wire.send(mate, mate, w.south)
        a.wait_recv()
        part = halves(slab(w.c_south), 0)
        h1 = wire.send(part, part, w.north)
        b.wait_recv()
        part = halves(slab(w.c_north), 1)
        h2 = wire.send(part, part, w.south)
        yield
        h1.wait_recv()
        h2.wait_recv()
        far = slab(w.c_far)
        last = wire.send(far, far, w.side)
        yield
        for copy in (p1, p2, last):
            copy.wait_recv()

    def eight_first(self):
        w, wire, out = self.w, self.wire, self.out
        width = out.shape[-1]
        cut = (width // 128 + 1) // 2 * 128
        ends = (pl.ds(0, cut), pl.ds(cut, width - cut))
        own = wire.keep(self.piece, out.at[w.z, w.c])
        own.wait()
        wire.kept = [k for k in wire.kept if k is not own]
        for _ in self.around(lambda c: out.at[w.z, c], lambda r, h: r.at[:, ends[h]]):
            yield
        mine = out.at[w.z]
        a, b = wire.send(mine, mine, w.up), wire.send(mine, mine, w.down)
        yield
        a.wait_recv()
        part = out.at[w.zm, pl.ds(0, 4)]
        h1 = wire.send(part, part, w.up)
        b.wait_recv()
        part = out.at[w.zp, pl.ds(4, 4)]
        h2 = wire.send(part, part, w.down)
        yield
        h1.wait_recv()
        h2.wait_recv()

    def ring_first(self):
        w, wire, out = self.w, self.wire, self.out
        own = wire.keep(self.piece, out.at[w.c, w.z])
        copies = [wire.send(self.piece, out.at[w.c, w.z], d) for d in (w.opposite, w.up, w.down)]
        yield
        own.wait()
        wire.kept = [k for k in wire.kept if k is not own]
        for copy in copies:
            copy.wait_recv()
        for _ in self.around(lambda c: out.at[c], lambda r, h: r.at[pl.ds(2 * h, 2)]):
            yield


class Where:
    def __init__(self):
        ctx, fs, y, xl, z = place()
        self.ctx, self.fs, self.y, self.xl, self.z = ctx, fs, y, xl, z
        self.core, self.xh = lax.rem(fs, 2), lax.div(fs, 2)
        yp, ym, yo = lax.rem(y + 1, 4), lax.rem(y + 3, 4), lax.rem(y + 2, 4)
        self.zp, self.zm, self.zo = lax.rem(z + 1, 4), lax.rem(z + 3, 4), lax.rem(z + 2, 4)
        self.c, self.c_mate = y * 2 + xl, y * 2 + 1 - xl
        self.c_north, self.c_south, self.c_far = yp * 2 + xl, ym * 2 + xl, yo * 2 + xl
        self.c_north_mate, self.c_south_mate = yp * 2 + 1 - xl, ym * 2 + 1 - xl
        self.c_far_mate = yo * 2 + 1 - xl
        self.north, self.south, self.side = eight_peers(y, xl, z, fs)
        self.up, self.down = (ctx_of(y, xl, self.zp), fs), (ctx_of(y, xl, self.zm), fs)
        self.opposite = (ctx_of(y, xl, self.zo), fs)
        self.twin = (ctx, fs + 1 - 2 * self.core)
        self.near = (ctx_of(y, 1 - xl, z), lax.rem(fs + 2, 4))
        self.plane = []
        for dh in (1, 0):
            for dy in (2, 1, 3, 0):
                for dx in (1, 0):
                    if dh or dy or dx:
                        hh = lax.rem(self.xh + dh, 2)
                        c = lax.rem(y + dy, 4) * 2 + lax.rem(xl + dx, 2)
                        self.plane.append((hh, c, (c * 4 + z, hh * 2 + self.core)))
        self.row = []
        for dh, dx in ((1, 0), (1, 1), (0, 1)):
            hh, xx = lax.rem(self.xh + dh, 2), lax.rem(xl + dx, 2)
            self.row.append((hh, xx, ((y * 2 + xx) * 4 + z, hh * 2 + self.core)))
        self.column = [(yy, (ctx_of(yy, xl, z), fs)) for yy in (yo, yp, ym)]
        self.eight = [(c, device) for hh, c, device in self.plane[8:]]


def layer_kernel(
    places, tok, cot, wqkv, wup, wdown, wdense, vec,
    or_o, ir_o, fa_o, qa_o, qb_o,
    X, G, WQ, WU, WD, WE, sq, su, sd, se, LA, LB, N, R, CS, bias,
    KVA, QGA, EC, GE, GH, SL, GU, GD, IB, SU,
    FT, FQ, FY, FX, FR, FPS,
    KP, QP0, LL, LT, raw, gap, TOPS, TOP, SUM, MIX, ACC, DKV, OUT,
    F1, MA, MB, H1, H2, MF, NF, SF,
    AT, OPB, IPB, GL, GQ, VS, EP, ET, EQ, EY, EX, ER, QP, QT, QB, QR, QPS_A, QPS_B,
    ssem, rsem, lsem, wsem,
):
    w = Where()
    wire = Wire(ssem, rsem, lsem)
    ctx, fs, y, xl, z, core = w.ctx, w.fs, w.y, w.xl, w.z, w.core
    zp, zm, zo, up, down, twin, near = w.zp, w.zm, w.zo, w.up, w.down, w.twin, w.near
    other = lax.rem(fs + 2, 4)
    parity = lax.rem(z, 2)

    load_x = pltpu.make_async_copy(tok, X.at[z], wsem.at[0])
    load_x.start()
    loads_q = []
    for t in range(3):
        for i in range(3):
            at = pl.multiple_of(t * 768 + 256 * i + 128 * lax.div(z, 2), 128)
            loads_q.append(
                pltpu.make_async_copy(
                    wqkv.at[:, pl.ds(at, 128)], sq.at[:, pl.ds((3 * t + i) * 128, 128)], wsem.at[1 + 3 * t + i]
                )
            )
    for copy in loads_q:
        copy.start()
    load_g = pltpu.make_async_copy(cot, G.at[z], wsem.at[10])
    load_g.start()
    spare = jnp.minimum(lax.rem(z + fs, 4), 2)
    load_e = pltpu.make_async_copy(wdense.at[pl.ds(pl.multiple_of(spare * 64, 64), 64)], se, wsem.at[11])
    load_e.start()
    loads_u = []
    for i in range(4):
        at = pl.multiple_of(768 * i + 192 * z - 64 * parity, 128)
        loads_u.append(
            pltpu.make_async_copy(wup.at[:, pl.ds(at, 256)], su.at[:, pl.ds(256 * i, 256)], wsem.at[12 + i])
        )
    for copy in loads_u:
        copy.start()
    load_d = pltpu.make_async_copy(wdown.at[pl.ds(pl.multiple_of(z * 192, 64), 192)], sd, wsem.at[16])
    load_d.start()

    greet([up, down, w.opposite, twin] + [device for _, _, device in w.plane])

    load_x.wait()
    x_up, x_down = wire.send(X.at[z], X.at[z], up), wire.send(X.at[z], X.at[z], down)
    for copy in loads_q:
        copy.wait()

    def piece(stage, at, odd):
        return stage[:, 128 * at + 64 * odd : 128 * at + 64 * odd + 64]

    for odd in range(2):

        @pl.when(parity == odd)
        def _():
            parts = []
            for i in range(3):
                parts += [piece(sq, 3 + i, odd), piece(sq, 6 + i, odd)]
            parts += [piece(sq, i, odd) for i in range(3)] + [jnp.zeros((192, 64), F32)]
            WQ[fs] = jnp.concatenate(parts, 1).astype(LOW)

    q_near = wire.send(WQ.at[fs], WQ.at[fs], near)
    q_twin = wire.send(WQ.at[fs], WQ.at[fs], twin)
    first = lax.div(ctx, 4) * 512
    CS[0], CS[1] = angle_lanes([places[0, first + 64 * i] for i in range(8)], 512)

    def low_block(start):
        block = places[0, start] >> 6
        return block < 32, jnp.where(block < 32, block, 63 - block)

    runs = [low_block(first + 128 * i) for i in range(4)]
    row = lax.broadcasted_iota(jnp.int32, (128, 128), 0)
    for b in range(2):
        spot = jnp.where(row < 64, runs[2 * b][1], runs[2 * b + 1][1])
        QP0[b] = spot * 64 + (row & 63)
        QP0[2 + b] = (63 - spot) * 64 + (row & 63)
    lane = lax.broadcasted_iota(jnp.int32, (8, 256), 1)
    line = lax.broadcasted_iota(jnp.int32, (8, 256), 0)
    for c in range(8):
        spot = jnp.zeros((8, 256), jnp.int32)
        for i in range(4):
            spot = jnp.where((lane >> 6) == i, low_block(512 * c + 128 * i)[1], spot)
        KP[c] = jnp.where(line == 0, spot, 63 - spot) * 64 + (lane & 63)

    gain_a, shift_a, gain_b, shift_b = (vec[i : i + 1, :] for i in range(4))

    def norms(zz):
        rows = pl.ds(pl.multiple_of(128 * zz, 128), 128)
        x = X[zz].astype(F32)
        centered = x - jnp.mean(x, -1, keepdims=True)
        inv = lax.rsqrt(jnp.mean(centered * centered, -1, keepdims=True) + norm_eps)
        normed = centered * inv
        N[rows, :] = normed
        R[rows, :] = jnp.broadcast_to(inv, (128, 128))
        LA[rows, :] = (normed * gain_a + shift_a).astype(LOW)
        LB[rows, :] = (normed * gain_b + shift_b).astype(LOW)

    norms(z)
    load_e.wait()
    WE[fs] = se[...].astype(LOW)
    for copy in loads_u:
        copy.wait()
    for odd in range(2):

        @pl.when(parity == odd)
        def _():
            parts = [su[:, 256 * i + 64 * odd : 256 * i + 64 * odd + 192] for i in range(4)]
            WU[fs] = jnp.concatenate(parts, 1).astype(LOW)

    load_d.wait()
    WD[fs] = sd[...].astype(LOW)
    load_g.wait()

    for zz in range(4):

        @pl.when(z == zz)
        def _():
            def head(row, i):
                return vec[row : row + 1, 64 * (zz + 4 * i) : 64 * (zz + 4 * i) + 64]

            parts = []
            for i in range(3):
                parts += [head(5, i), head(6, i)]
            parts += [head(4, i) for i in range(3)] + [jnp.zeros((1, 64), F32)]
            bias[0:1, 0:640] = jnp.concatenate(parts, 1)
            bias[1:2, :] = jnp.concatenate(
                [vec[8 + i : 9 + i, 192 * zz : 192 * zz + 192] for i in range(4)], 1
            )

    def relay(slab, from_down, from_up):
        from_down.wait_recv()
        part = slab.at[zm, pl.ds(0, 64)]
        a = wire.send(part, part, up)
        from_up.wait_recv()
        part = slab.at[zp, pl.ds(64, 64)]
        return [a, wire.send(part, part, down)]

    def forward(slab, copy):
        copy.wait_recv()
        return wire.send(slab.at[other], slab.at[other], twin)

    wire.left(x_up, x_down)
    g_up, g_down = wire.send(G.at[z], G.at[z], up), wire.send(G.at[z], G.at[z], down)
    x_far = relay(X, x_up, x_down)
    norms(zm)
    norms(zp)
    wire.left(q_near)
    e_near, e_twin = wire.send(WE.at[fs], WE.at[fs], near), wire.send(WE.at[fs], WE.at[fs], twin)
    u_near, u_twin = wire.send(WU.at[fs], WU.at[fs], near), wire.send(WU.at[fs], WU.at[fs], twin)
    q_far = forward(WQ, q_near)
    for copy in x_far:
        copy.wait_recv()
    norms(zo)
    g_far = relay(G, g_up, g_down)
    q_twin.wait_recv()
    q_far.wait_recv()
    low256 = lanes(256) < 64

    def arrange(value, i):
        a, b = value[:64], value[64:]
        return jnp.where(runs[i][0], a, b), jnp.where(runs[i][0], b, a)

    for t in range(2):
        rows = slice(256 * t, 256 * t + 256)
        linear = dot(LA[rows, :], WQ[...].reshape(768, 640)) + bias[0:1, 0:640]
        cos_wide, sin_wide = CS[0, rows, :], CS[1, rows, :]
        ab, last = linear[:, 384:512], linear[:, 512:640]
        for h, u in enumerate((ab, pltpu.roll(ab, 64, 1), last)):
            keys = turn(linear[:, 128 * h : 128 * h + 128], cos_wide, sin_wide)
            asks = jnp.where(low256, turn(u, cos_wide, sin_wide), 0.0)
            for i in (2 * t, 2 * t + 1):
                part = slice(128 * (i - 2 * t), 128 * (i - 2 * t) + 128)
                for half, value in enumerate(arrange(keys[part], i)):
                    at = 256 * half + 64 * i
                    KVA[w.c, h, at : at + 64, :] = value.astype(LOW)
                for half, value in enumerate(arrange(asks[part], i)):
                    at = 256 * half + 64 * i
                    QGA[at : at + 64, 128 * h : 128 * h + 128] = value.astype(LOW)

    spread = Spread(wire, None, None, w)

    def gather(h):
        return spread.around(lambda c: KVA.at[c, h], lambda r, half: r.at[pl.ds(256 * half, 256)])

    kv = [gather(h) for h in range(3)]
    next(kv[0])
    next(kv[2])
    e_far = forward(WE, e_near)
    for copy in g_far + [e_twin, e_far]:
        copy.wait_recv()
    EC[192:, :] = jnp.zeros((64, 768), LOW)
    for i in range(3):
        EC[64 * i : 64 * i + 64, :] = WE[i + jnp.where(i >= 3 - z, 1, 0)]
    for t in range(2):
        grad = dot_rows(G[pl.ds(2 * t, 2)].reshape(256, 768), EC[...])
        ab, last = grad[:, :128], grad[:, 128:]
        for h, u in enumerate((pltpu.roll(ab, 64, 1), ab, pltpu.roll(last, 64, 1))):
            for i in (2 * t, 2 * t + 1):
                part = slice(128 * (i - 2 * t), 128 * (i - 2 * t) + 128)
                for half, value in enumerate(arrange(u[part], i)):
                    at = slice(256 * half + 64 * i, 256 * half + 64 * i + 64)
                    col = slice(128 * h, 128 * h + 128)
                    QGA[at, col] = jnp.where(low256[:64], QGA[at, col], value.astype(LOW))

    next(kv[1])
    wire.left(u_near)
    d_near, d_twin = wire.send(WD.at[fs], WD.at[fs], near), wire.send(WD.at[fs], WD.at[fs], twin)
    u_far = forward(WU, u_near)
    for copy in (u_twin, u_far):
        copy.wait_recv()

    def feed_up(t):
        rows = pl.ds(256 * t, 256)
        hidden = dot(LB[rows, :], WU[...].reshape(768, 768)) + bias[1:2, :]
        half = 0.5 + 0.5 * erf(hidden * 0.7071067811865476)
        GE[rows, :] = (hidden * half).astype(LOW)
        SL[rows, :] = half + hidden * (jnp.exp(hidden * hidden * -0.5) * 0.3989422804014327)

    down_parts = ((GD, 1, 0, 64, 64, 768), (GD, 1, 64, 128, 0, 1536))
    up_parts = ((GU, 0, 0, 128, 0, 0), (GU, 0, 128, 64, 0, 768))

    def exchange(slab, k):
        copies = []
        for h in range(2):
            at = pl.multiple_of(192 * (2 * h + 1 - core), 64)
            copies.append(wire.send(slab.at[pl.ds(at, 192)], FT.at[k, h], twin))
        return copies

    def add_pair(copies, parts):
        for copy in copies:
            copy.wait_recv()
        for slab, k, row, size, to, col in parts:
            for h in range(2):
                at = pl.multiple_of(192 * (2 * h + core) + row, 64)
                for r in range(0, size, 16):
                    total = slab[pl.ds(pl.multiple_of(at + r, 16), 16), :].astype(F32) + FT[
                        k, h, row + r : row + r + 16, :
                    ].astype(F32)
                    FQ[(to + r) // 32, h, (to + r) // 16 % 2, :, col : col + 768] = total.astype(LOW)

    feed_up(0)
    next(kv[0])
    feed_up(1)
    d_far = forward(WD, d_near)
    for copy in (d_twin, d_far):
        copy.wait_recv()
    for t in range(2):
        rows = pl.ds(256 * t, 256)
        grad = G[2 * t : 2 * t + 2].reshape(256, 768)
        GH[rows, :] = (dot_rows(grad, WD[...].reshape(768, 768)) * SL[rows, :]).astype(LOW)
    next(kv[0])

    @pl.loop(0, 3)
    def _(j):
        at = pl.ds(pl.multiple_of(256 * j, 256), 256)
        GD[at, :] = dot_down(GE[:, at], G[...].reshape(512, 768)).astype(LOW)

    paired_down = exchange(GD, 1)
    next(kv[2])

    @pl.loop(0, 3)
    def _(j):
        at = pl.ds(pl.multiple_of(256 * j, 256), 256)
        GU[at, :] = dot_down(LB[:, at], GH[...]).astype(LOW)

    paired_up = exchange(GU, 0)
    next(kv[1])

    low = lanes(512) < 64
    same = (
        lax.broadcasted_iota(jnp.int32, (256, 256), 0) == lax.broadcasted_iota(jnp.int32, (256, 256), 1)
    )
    same = jnp.where(same, 1.0, 0.0).astype(LOW)
    deep = lax.broadcasted_iota(jnp.int32, (128, 256), 0) < 64

    meets = ((0,), (0,), (0, 1), (0, 1))
    spots = {}
    for b in range(4):
        for side in meets[b]:
            spots[b, side] = len(spots)

    def keys_of(c, h, side):
        return KVA[c, h, 256 * side : 256 * side + 256, :]

    def twice(value):
        return jnp.concatenate([value, value], 1)

    def begin(h):
        for b in range(4):
            part = QGA[128 * b : 128 * b + 128, 128 * h : 128 * h + 128]
            none = jnp.zeros_like(part)
            pile = jnp.concatenate(
                [jnp.where(low256[:128], part, none), jnp.where(low256[:128], none, part)], 0
            )
            LL[b] = pile
            LT[b] = dot_rows(same[:128, :128], pile).astype(LOW)
        TOP[...] = jnp.full_like(TOP, masked)
        SUM[...] = jnp.zeros_like(SUM)
        MIX[...] = jnp.zeros_like(MIX)
        ACC[...] = jnp.zeros_like(ACC)

    def score(h, shards):
        @pl.loop(*shards)
        def _(c):
            for b in range(4):
                old = TOP[b]
                top = old
                met = []
                for side in meets[b]:
                    pair = dot_rows(LL[b], keys_of(c, h, side))
                    scores = pair[:128]
                    if b < 2 or side:
                        seen = KP[c, side : side + 1, :] <= twice(QP0[b])
                        scores = jnp.where(seen, scores, masked)
                    gap[c, spots[b, side]] = pair[128:]
                    top = jnp.maximum(top, jnp.maximum(scores[:, :128], scores[:, 128:]))
                    met.append((spots[b, side], scores, pair[128:]))
                fade = jnp.exp((old - top) * 0.125)
                total, blend = SUM[b] * fade, MIX[b] * fade
                for i, scores, grads in met:
                    e = jnp.exp((scores - twice(top)) * 0.125)
                    raw[c, i] = e
                    mix = e * grads
                    total = total + (e[:, :128] + e[:, 128:])
                    blend = blend + (mix[:, :128] + mix[:, 128:])
                TOP[b] = top
                TOPS[c, b] = top
                SUM[b] = total
                MIX[b] = blend

    def weigh():
        for b in range(4):
            top = jnp.max(TOP[b], -1, keepdims=True)
            fade = jnp.exp((TOP[b] - top) * 0.125)
            inverse = 1.0 / jnp.sum(SUM[b] * fade, -1, keepdims=True)
            shared = jnp.sum(MIX[b] * fade, -1, keepdims=True) * inverse
            TOP[b] = jnp.broadcast_to(top, (128, 128))
            SUM[b] = jnp.broadcast_to(inverse, (128, 128))
            MIX[b] = jnp.broadcast_to(shared, (128, 128))

    def settle(h, shards):
        @pl.loop(*shards)
        def _(c):
            grown = [None, None]
            for b in range(4):
                total = ACC[b]
                share = twice(jnp.exp((TOPS[c, b] - TOP[b]) * 0.125) * SUM[b])
                for side in meets[b]:
                    i = spots[b, side]
                    probs = raw[c, i] * share
                    slope = probs * (gap[c, i] - twice(MIX[b]))
                    pile = jnp.concatenate([slope.astype(LOW), probs.astype(LOW)], 0)
                    total = total + dot(pile, keys_of(c, h, side))
                    part = dot(LT[b], pile)
                    grown[side] = part if grown[side] is None else grown[side] + part
                ACC[b] = total
            for side, g in enumerate(grown):
                g = jnp.where(deep, g * 0.125, g).astype(LOW)
                DKV[c, h, 256 * side : 256 * side + 256, :] = dot_rows(same, g).astype(LOW)

    def finish(h):
        done = [jnp.where(low256[:128], ACC[b, :128] * 0.125, ACC[b, 128:]) for b in range(4)]
        for i in range(4):
            at = slice(64 * (i % 2), 64 * (i % 2) + 64)
            a, b = done[i // 2][at], done[2 + i // 2][at]
            at = slice(128 * h, 128 * h + 128)
            OUT[128 * i : 128 * i + 64, at] = jnp.where(runs[i][0], a, b)
            OUT[128 * i + 64 : 128 * i + 128, at] = jnp.where(runs[i][0], b, a)

    def tree(h):
        t1 = wire.send(DKV.at[w.c_far_mate, h], F1.at[h], w.side)
        t2 = wire.send(DKV.at[w.c_north_mate, h], MA.at[h], w.north)
        t3 = wire.send(DKV.at[w.c_south_mate, h], MB.at[h], w.south)
        yield
        t1.wait_recv()
        DKV[w.c_far, h] = (DKV[w.c_far, h].astype(F32) + F1[h].astype(F32)).astype(LOW)
        t4 = wire.send(DKV.at[w.c_far, h, pl.ds(0, 256)], H1.at[h], w.south)
        t5 = wire.send(DKV.at[w.c_far, h, pl.ds(256, 256)], H2.at[h], w.north)
        t2.wait_recv()
        t3.wait_recv()
        total = DKV[w.c_mate, h].astype(F32) + MA[h].astype(F32) + MB[h].astype(F32)
        DKV[w.c_mate, h] = total.astype(LOW)
        t6 = wire.send(DKV.at[w.c_mate, h], MF.at[h], w.side)
        yield
        t4.wait_recv()
        total = DKV[w.c_south, h, 0:256, :].astype(F32) + H1[h].astype(F32)
        DKV[w.c_south, h, 0:256, :] = total.astype(LOW)
        t7 = wire.send(DKV.at[w.c_south, h], NF.at[h], w.south)
        t5.wait_recv()
        total = DKV[w.c_north, h, 256:512, :].astype(F32) + H2[h].astype(F32)
        DKV[w.c_north, h, 256:512, :] = total.astype(LOW)
        t8 = wire.send(DKV.at[w.c_north, h], SF.at[h], w.north)
        yield
        for copy in (t6, t7, t8):
            copy.wait_recv()

    def add_up(parts):
        total = parts[0].astype(F32)
        for part in parts[1:]:
            total = total + part.astype(F32)
        return total.astype(LOW)

    def ladder(packet, fy, fx, fr, out):
        copies = [wire.send(packet.at[yy], fy.at[y], device) for yy, device in w.column]
        fy[y] = packet[y]
        yield
        for copy in copies:
            copy.wait_recv()
        for h in range(2):
            for i in range(2):
                fx[h, i] = add_up([fy[j, h, i] for j in range(4)])
        me = w.xh * 2 + xl
        copies = [wire.send(fx.at[hh, xx], fr.at[me], device) for hh, xx, device in w.row]
        fr[me] = fx[w.xh, xl]
        yield
        for copy in copies:
            copy.wait_recv()
        out(add_up([fr[j] for j in range(4)]))

    def drain(steps):
        for _ in steps:
            pass

    def keep_piece(total):
        FPS[...] = total

    def keep_dense(total):
        QPS_B[:, 384:768] = total

    def arrived(copies):
        for copy in copies:
            copy.wait_recv()

    def arrived(copies):
        for copy in copies:
            copy.wait_recv()

    fl = ladder(FQ, FY, FX, FR, keep_piece)
    fa = Spread(wire, FPS, fa_o, w).eight_first()
    trees = [tree(h) for h in range(3)]
    early, late = (0, 4), (4, 8)
    drain(kv[0])
    begin(0)
    score(0, early)
    score(0, late)
    next(kv[1])
    add_pair(paired_down, down_parts)
    add_pair(paired_up, up_parts)
    next(fl)
    weigh()
    settle(0, early)
    settle(0, late)
    finish(0)
    drain(kv[1])
    begin(1)
    score(1, early)
    next(kv[2])
    score(1, late)
    next(trees[0])
    weigh()
    settle(1, early)
    next(fl)
    settle(1, late)
    finish(1)
    next(trees[0])
    drain(fl)
    next(fa)
    drain(kv[2])
    begin(2)
    score(2, early)
    next(trees[1])
    next(fa)
    score(2, late)
    next(trees[0])
    next(fa)
    weigh()
    settle(2, early)
    next(trees[1])
    next(fa)
    settle(2, late)
    next(trees[2])
    finish(2)

    o0, o1, o2 = (OUT[:, 128 * i : 128 * i + 128] for i in range(3))
    AT[:, :128] = jnp.where(low, pltpu.roll(o0, 64, 1), o1).astype(LOW)
    AT[:, 128:] = jnp.where(low, pltpu.roll(o2, 64, 1), 0.0).astype(LOW)
    ge = dot_down(AT[...], G[...].reshape(512, 768))
    for i in range(4):
        empty = 3 - z
        after = ge[64 * i - 64 : 64 * i] if i else ge[0:64]
        before = ge[64 * i : 64 * i + 64] if i < 3 else ge[128:192]
        slot = jnp.where(i > empty, after, before)
        slot = jnp.where(i == empty, 0.0, slot).astype(LOW)
        EP[i, 0:64, :] = slot[:, :384]
        EP[i, 64:128, :] = slot[:, 384:]
    paired_e = [wire.send(EP.at[2 * h + 1 - core], ET.at[h], twin) for h in range(2)]
    next(trees[1])
    SU[...] = jnp.zeros_like(SU)
    for t in range(2):
        rows = pl.ds(256 * t, 256)
        back = GH[rows, :]
        grad_ln = dot_rows(back, WU[...].reshape(768, 768))
        normed = N[rows, :]
        SU[0:1, :] += jnp.sum(grad_ln * normed, 0, keepdims=True)
        SU[1:2, :] += jnp.sum(grad_ln, 0, keepdims=True)
        SU[2:3, :] += jnp.sum(back.astype(F32), 0, keepdims=True)
        IB[rows, :] = norm_back(grad_ln, normed, R[rows, 0:1], gain_b)
    next(trees[2])
    arrived(paired_e)
    for h in range(2):
        for c in range(8):
            at = slice(16 * c, 16 * c + 16)
            EQ[c // 2, h, c % 2] = add_up([EP[2 * h + core, at, :], ET[h, at, :]])
    el = ladder(EQ, EY, EX, ER, keep_dense)
    next(el)
    for i in range(4):
        rows = slice(128 * i, 128 * i + 128)
        total = dot(GE[rows, :], WD[...].reshape(768, 768)) + dot(AT[rows, :], EC[...])
        OPB[i] = total.astype(LOW)
    ring = ((zo, w.opposite), (zp, up), (zm, down))
    o_sent = [wire.send(OPB.at[zz], or_o.at[z], device) for zz, device in ring]
    wire.keep(OPB.at[z], or_o.at[z])
    next(trees[2])

    cos_wide, sin_wide = CS[0], -CS[1]
    u0, u1, u2 = (turn(u, cos_wide, sin_wide) for u in (o0, o1, o2))
    GL[:, 384:512] = jnp.where(low, u0, pltpu.roll(u1, 64, 1)).astype(LOW)
    GL[:, 512:640] = jnp.where(low, u2, 0.0).astype(LOW)

    def own_sum(h):
        drain(trees[h])
        total = DKV[w.c, h].astype(F32) + MF[h].astype(F32) + NF[h].astype(F32) + SF[h].astype(F32)
        for i in range(4):
            a, b = total[64 * i : 64 * i + 64], total[256 + 64 * i : 320 + 64 * i]
            rows = slice(128 * i, 128 * i + 128)
            value = jnp.concatenate([jnp.where(runs[i][0], a, b), jnp.where(runs[i][0], b, a)], 0)
            value = turn(value, CS[0, rows, :], -CS[1, rows, :])
            GL[rows, 128 * h : 128 * h + 128] = value.astype(LOW)

    def project(cols):
        for t in range(2):
            rows = slice(256 * t, 256 * t + 256)
            yield rows, dot_rows(GL[rows, cols], WQ[:, :, cols].reshape(768, -1))

    def weight_part(cols):
        @pl.loop(0, 3)
        def _(j):
            at = pl.ds(pl.multiple_of(256 * j, 256), 256)
            GQ[at, cols] = dot_down(LA[:, at], GL[:, cols]).astype(LOW)

    own_sum(0)
    own_sum(1)
    for rows, value in project(slice(0, 256)):
        SL[rows, :] = value
    for rows, value in project(slice(384, 640)):
        SL[rows, :] = SL[rows, :] + value
    weight_part(slice(0, 256))
    weight_part(slice(384, 640))
    VS[...] = jnp.zeros_like(VS)

    def note(row, values):
        for j in range(values.shape[1] // 128):
            VS[6 * row + j : 6 * row + j + 1, :] = values[:, 128 * j : 128 * j + 128]

    note(2, SU[0:1, :])
    note(3, SU[1:2, :])
    note(5, SU[2:3, :])
    note(6, jnp.sum(G[z].astype(F32), 0, keepdims=True))
    next(el)
    own_sum(2)
    dots = jnp.zeros((1, 768), F32)
    plain = jnp.zeros((1, 768), F32)
    for rows, value in project(slice(256, 384)):
        grad_ln = SL[rows, :] + value
        SL[rows, :] = grad_ln
        dots = dots + jnp.sum(grad_ln * N[rows, :], 0, keepdims=True)
        plain = plain + jnp.sum(grad_ln, 0, keepdims=True)
    note(0, dots)
    note(1, plain)
    note(4, jnp.sum(GL[...].astype(F32), 0, keepdims=True))
    weight_part(slice(256, 384))
    for i in range(4):
        QP[i, :, 0:640] = GQ[192 * i : 192 * i + 128, :]
        QP[i, 0:64, 640:1024] = GQ[192 * i + 128 : 192 * i + 192, 0:384]
        QP[i, 64:128, 640:896] = GQ[192 * i + 128 : 192 * i + 192, 384:640]
        QP[i, 64:128, 896:1024] = VS[...].astype(LOW)
    paired_q = [wire.send(QP.at[2 * h + 1 - core], QT.at[h], twin) for h in range(2)]
    next(fa)
    drain(el)
    arrived(paired_q)
    for h in range(2):
        for c in range(8):
            at = slice(16 * c, 16 * c + 16)
            QB[h, c] = add_up([QP[2 * h + core, at, :], QT[h, at, :]])
    me = w.xh * 8 + w.c
    q_plane = [wire.send(QB.at[hh, c], QR.at[me], device) for hh, c, device in w.plane]
    QR[me] = QB[w.xh, w.c]
    for t in range(4):
        rows = slice(128 * t, 128 * t + 128)
        total = norm_back(SL[rows, :], N[rows, :], R[rows, 0:1], gain_a) + IB[rows, :]
        IPB[t] = total.astype(LOW)
    i_sent = [wire.send(IPB.at[zz], ir_o.at[z], device) for zz, device in ring]
    wire.keep(IPB.at[z], ir_o.at[z])
    for copy in q_plane:
        copy.wait_recv()
    total = add_up([QR[j] for j in range(16)])
    QPS_A[...] = total[:, :640]
    QPS_B[:, :384] = total[:, 640:]
    first_a = [wire.send(QPS_A, qa_o.at[z, w.c], device) for _, device in w.eight]
    first_b = [wire.send(QPS_B, qb_o.at[w.c, z], device) for _, device in ring]
    own = wire.keep(QPS_B, qb_o.at[w.c, z]), wire.keep(QPS_A, qa_o.at[z, w.c])
    for copy in own:
        copy.wait()
    wire.kept = [k for k in wire.kept if not any(k is o for o in own)]
    arrived(first_b)
    last_b = [wire.send(qb_o.at[w.c], qb_o.at[w.c], device) for _, device in w.eight]
    arrived(first_a)
    last_a = [wire.send(qa_o.at[z], qa_o.at[z], device) for _, device in ring]
    drain(fa)
    arrived(last_b + last_a)
    for copy in o_sent + i_sent:
        copy.wait_recv()
    wire.finish()


def layer(places, tok, cot, wqkv, wup, wdown, wdense, vec):
    outs = [
        ((4, 128, 768), LOW),
        ((4, 128, 768), LOW),
        ((4, 8, 16, 2304), LOW),
        ((4, 8, 16, 640), LOW),
        ((8, 4, 16, 768), LOW),
    ]
    scratch = [
        *[((4, 128, 768), LOW)] * 2,
        ((4, 192, 640), LOW),
        *[((4, 192, 768), LOW)] * 2,
        ((4, 64, 768), LOW),
        ((192, 1152), F32),
        ((192, 1024), F32),
        ((192, 768), F32),
        ((64, 768), F32),
        *[((512, 768), LOW)] * 2,
        ((512, 768), F32),
        ((512, 128), F32),
        ((2, 512, 128), F32),
        ((8, 768), F32),
        ((8, 3, 512, 128), LOW),
        ((512, 384), LOW),
        ((256, 768), LOW),
        *[((512, 768), LOW)] * 2,
        ((512, 768), F32),
        *[((768, 768), LOW)] * 2,
        ((512, 768), F32),
        ((8, 768), F32),
        ((2, 2, 192, 768), LOW),
        ((4, 2, 2, 16, 2304), LOW),
        ((4, 2, 2, 16, 2304), LOW),
        ((2, 2, 16, 2304), LOW),
        ((4, 16, 2304), LOW),
        ((16, 2304), LOW),
        ((8, 8, 256), jnp.int32),
        ((4, 128, 128), jnp.int32),
        ((4, 256, 128), LOW),
        ((4, 128, 256), LOW),
        *[((8, 6, 128, 256), F32)] * 2,
        ((8, 4, 128, 128), F32),
        *[((4, 128, 128), F32)] * 3,
        ((4, 256, 128), F32),
        ((8, 3, 512, 128), LOW),
        ((512, 384), F32),
        *[((3, 512, 128), LOW)] * 3,
        *[((3, 256, 128), LOW)] * 2,
        *[((3, 512, 128), LOW)] * 3,
        ((512, 256), LOW),
        *[((4, 128, 768), LOW)] * 2,
        ((512, 640), LOW),
        ((768, 640), LOW),
        ((64, 128), F32),
        ((4, 128, 384), LOW),
        ((2, 128, 384), LOW),
        ((4, 2, 2, 16, 384), LOW),
        ((4, 2, 2, 16, 384), LOW),
        ((2, 2, 16, 384), LOW),
        ((4, 16, 384), LOW),
        ((4, 128, 1024), LOW),
        ((2, 128, 1024), LOW),
        ((2, 8, 16, 1024), LOW),
        ((16, 16, 1024), LOW),
        ((16, 640), LOW),
        ((16, 768), LOW),
    ]
    anywhere = pl.BlockSpec(memory_space=pl.ANY)
    sends = 168
    return pl.pallas_call(
        layer_kernel,
        out_shape=[jax.ShapeDtypeStruct(s, d) for s, d in outs],
        in_specs=[pl.BlockSpec(memory_space=pltpu.SMEM)]
        + [anywhere] * 6
        + [pl.BlockSpec(memory_space=pltpu.VMEM)],
        out_specs=[anywhere] * len(outs),
        scratch_shapes=[pltpu.VMEM(s, d) for s, d in scratch]
        + [
            pltpu.SemaphoreType.DMA((sends,)),
            pltpu.SemaphoreType.DMA((sends,)),
            pltpu.SemaphoreType.DMA((16,)),
            pltpu.SemaphoreType.DMA((17,)),
        ],
        compiler_params=pltpu.CompilerParams(
            collective_id=0, has_side_effects=True, vmem_limit_bytes=60 * 1024 * 1024
        ),
    )(places, tok, cot, wqkv, wup, wdown, wdense, vec)


def step_kernel(
    spot, tok, cot, ors, irs, fa, qa, qb, vec, vec_m, vec_s,
    qw, qm, qs, ew, em, es, uw, um, us, dw, dm, ds,
    blk_o, inp_o, vw_o, vm_o, vs_o,
    qw_o, qm_o, qs_o, ew_o, em_o, es_o, uw_o, um_o, us_o, dw_o, dm_o, ds_o,
    TO, CO, OR, IR, FA, QA, QB, VW, VM, VS, QW, QM, QS, EW, EM, ES, UW, UM, US, DW, DM, DS,
    BL, IN, isem, osem,
):
    count = [0, 0]

    def start(src, dst, sem, which):
        copy = pltpu.make_async_copy(src, dst, sem.at[count[which]])
        count[which] += 1
        copy.start()
        return copy

    def arrive(pairs):
        return [start(a, b, isem, 0) for a, b in pairs]

    def cut_rows(pairs, at, size):
        return [(a.at[pl.ds(at, size)], b.at[pl.ds(at, size)]) for a, b in pairs]

    up, down = ((uw, UW), (um, UM), (us, US)), ((dw, DW), (dm, DM), (ds, DS))
    dense, qkv = ((ew, EW), (em, EM), (es, ES)), ((qw, QW), (qm, QM), (qs, QS))
    load_v = arrive(((vec, VW), (vec_m, VM), (vec_s, VS)))
    load_e = arrive(((qb, QB),) + dense)
    load_small = arrive(((tok, TO), (cot, CO), (ors, OR), (irs, IR)))
    load_u1 = arrive(((fa, FA), *cut_rows(up, 0, 128)))
    load_u2 = arrive(cut_rows(up, 128, 64))
    load_d1 = arrive(cut_rows(down, 0, 384))
    load_d2 = arrive(cut_rows(down, 384, 384))
    load_q = arrive(((qa, QA),) + tuple(cut_rows(qkv, 0, 128)))
    load_q2 = arrive(cut_rows(qkv, 128, 64))
    leaving = []

    def leave(pairs):
        leaving.extend(start(a, b, osem, 1) for a, b in pairs)

    def back_rows(pairs, at, size):
        leave((b.at[pl.ds(at, size)], a.at[pl.ds(at, size)]) for a, b in pairs)

    def wait(copies):
        for copy in copies:
            copy.wait()

    def update(slabs, rows, gradient, rate, decay):
        new = adamw(slabs[0][rows, :], slabs[1][rows, :], slabs[2][rows, :], gradient, rate, decay)
        for slab, value in zip(slabs, new):
            slab[rows, :] = value

    def rows_of(start_at, size=16):
        return pl.ds(pl.multiple_of(start_at, 16), size)

    def spread_up(parts):
        parts = [p.astype(F32) for p in parts]
        return jnp.concatenate([parts[z][:, 192 * i : 192 * i + 192] for i in range(4) for z in range(4)], 1)

    wait(load_v)
    wait(load_e)

    @pl.loop(0, 4)
    def _(c):
        for o in range(3):
            z = lax.rem(o + 4 - spot[0], 4)
            gradient = jnp.concatenate([QB[c, z, :, 384:768], QB[4 + c, z, :, 384:768]], 1).astype(F32)
            update((EW, EM, ES), rows_of(64 * o + 16 * c), gradient, 0.1, 0.1)

    leave(((EW, ew_o), (EM, em_o), (ES, es_o)))
    wait(load_small)
    BL[...] = (
        TO[...].astype(F32) + jnp.sum(OR[...].astype(F32), 0) + VW[7:8, :] + VW[12:13, :]
    ).astype(LOW)
    IN[...] = CO[...].astype(F32) + jnp.sum(IR[...].astype(F32), 0)
    leave(((BL, blk_o), (IN, inp_o)))
    wait(load_u1)

    @pl.loop(0, 8)
    def _(c):
        update((UW, UM, US), rows_of(16 * c), spread_up([FA[z, c, :, 0:768] for z in range(4)]), 0.03, 0.1)

    back_rows(((uw_o, UW), (um_o, UM), (us_o, US)), 0, 128)
    wait(load_u2)

    @pl.loop(0, 4)
    def _(c):
        gradient = spread_up([FA[z, c, :, 768:1536] for z in range(4)])
        update((UW, UM, US), rows_of(128 + 16 * c), gradient, 0.03, 0.1)

    back_rows(((uw_o, UW), (um_o, UM), (us_o, US)), 128, 64)

    for half, load in enumerate((load_d1, load_d2)):
        wait(load)

        @pl.loop(0, 8)
        def _(c):
            for z in (2 * half, 2 * half + 1):
                rows = rows_of(192 * z + 64 + 16 * c)
                update((DW, DM, DS), rows, FA[z, c, :, 1536:2304].astype(F32), 0.02, 0.1)

        @pl.loop(0, 4)
        def _(c):
            for z in (2 * half, 2 * half + 1):
                rows = rows_of(192 * z + 16 * c)
                update((DW, DM, DS), rows, FA[z, 4 + c, :, 768:1536].astype(F32), 0.02, 0.1)

        back_rows(((dw_o, DW), (dm_o, DM), (ds_o, DS)), 384 * half, 384)

    wait(load_q)
    low = lanes(16) < 64

    def spread_heads(groups):
        out = []
        for t in range(3):
            for i in range(3):
                for pair in range(2):
                    halves = []
                    for odd in range(2):
                        group = groups[2 * pair + odd]
                        if t == 0:
                            u, at = group[3 + i // 2], i % 2
                        else:
                            u, at = group[i], t - 1
                        halves.append(u if at == odd else pltpu.roll(u, 64, 1))
                    out.append(jnp.where(low, halves[0], halves[1]))
        return jnp.concatenate(out, 1)

    def cut(value):
        value = value.astype(F32)
        return [value[:, 128 * j : 128 * j + 128] for j in range(value.shape[1] // 128)]

    @pl.loop(0, 8)
    def _(c):
        groups = [cut(QA[z, c]) for z in range(4)]
        update((QW, QM, QS), rows_of(16 * c), spread_heads(groups), 0.03, 0.1)

    back_rows(((qw_o, QW), (qm_o, QM), (qs_o, QS)), 0, 128)
    wait(load_q2)

    @pl.loop(0, 4)
    def _(c):
        groups = [cut(QB[c, z, :, 0:384]) + cut(QB[4 + c, z, :, 0:256]) for z in range(4)]
        update((QW, QM, QS), rows_of(128 + 16 * c), spread_heads(groups), 0.03, 0.1)

    back_rows(((qw_o, QW), (qm_o, QM), (qs_o, QS)), 128, 64)

    notes = [QB[4:8, z, :, 256:384].astype(F32).reshape(64, 128) for z in range(4)]
    total = (notes[0] + notes[1]) + (notes[2] + notes[3])

    def line(values, row):
        return jnp.concatenate([values[6 * row + j : 6 * row + j + 1, :] for j in range(6)], 1)

    linear = [line(n, 4) for n in notes]
    heads = []
    for at in (lambda i: 384 + 64 * i, lambda i: 128 * i, lambda i: 128 * i + 64):
        heads.append(
            jnp.concatenate([linear[z][:, at(i) : at(i) + 64] for i in range(3) for z in range(4)], 1)
        )
    hidden = [line(n, 5) for n in notes]
    wide = [
        jnp.concatenate([hidden[z][:, 192 * i : 192 * i + 192] for z in range(4)], 1) for i in range(4)
    ]
    ends = line(total, 6)
    lines = [line(total, i) for i in range(4)] + heads + [ends] + wide + [ends]
    for i, gradient in enumerate(lines):
        row = slice(i, i + 1)
        update((VW, VM, VS), row, gradient, 0.2, 0.0)
    leave(((VW, vw_o), (VM, vm_o), (VS, vs_o)))
    wait(leaving)


def step(spot, small, parts, vectors, weights):
    anywhere = pl.BlockSpec(memory_space=pl.ANY)
    outs = [jax.ShapeDtypeStruct((128, 768), LOW), jax.ShapeDtypeStruct((128, 768), F32)]
    operands = [*small, *parts, *vectors, *weights]
    outs += [jax.ShapeDtypeStruct(v.shape, F32) for v in [*vectors, *weights]]
    return pl.pallas_call(
        step_kernel,
        out_shape=outs,
        in_specs=[pl.BlockSpec(memory_space=pltpu.SMEM)] + [anywhere] * len(operands),
        out_specs=[anywhere] * len(outs),
        scratch_shapes=[pltpu.VMEM(v.shape, v.dtype) for v in operands]
        + [pltpu.VMEM(o.shape, o.dtype) for o in outs[:2]]
        + [pltpu.SemaphoreType.DMA((40,)), pltpu.SemaphoreType.DMA((40,))],
        compiler_params=pltpu.CompilerParams(vmem_limit_bytes=VMEM_LIMIT),
    )(spot, *operands)


def norm_back(incoming, normed, inv_scale, gain_row):
    scaled = incoming * gain_row
    return inv_scale * (
        scaled
        - jnp.mean(scaled, -1, keepdims=True)
        - normed * jnp.mean(scaled * normed, -1, keepdims=True)
    )


def adamw(weight, moment, second, gradient, step_rate, decay_rate):
    moment_new = beta_first * moment + (1.0 - beta_first) * gradient
    second_new = beta_second * second + ((1.0 - beta_second) * gradient) * gradient
    size = jnp.sqrt(second_new * (1.0 / (1.0 - beta_second**STEP))) + adam_eps
    change = moment_new * (step_rate / (1.0 - beta_first**STEP)) / size
    return (weight * (1.0 - step_rate * decay_rate) - change, moment_new, second_new)


def dot(a, b):
    return jnp.dot(a, b, preferred_element_type=F32)


def dot_rows(a, b):
    return lax.dot_general(a, b, (((1,), (1,)), ((), ())), preferred_element_type=F32)


def dot_down(a, b):
    return lax.dot_general(a, b, (((0,), (0,)), ((), ())), preferred_element_type=F32)


def body(
    tokens,
    cotangent,
    positions,
    vectors,
    vectors_moment,
    vectors_second,
    qkv_weight,
    qkv_moment,
    qkv_second,
    dense_weight,
    dense_moment,
    dense_second,
    up_weight,
    up_moment,
    up_second,
    down_weight,
    down_moment,
    down_second,
):
    fs = lax.axis_index("fsdp")
    ors, irs, fa, qa, qb = layer(
        positions, tokens[0], cotangent[0], qkv_weight, up_weight, down_weight, dense_weight, vectors
    )
    block_out, input_grad, *new = step(
        fs.reshape(1).astype(jnp.int32),
        (tokens[0], cotangent[0], ors, irs),
        (fa, qa, qb),
        (vectors, vectors_moment, vectors_second),
        (
            qkv_weight,
            qkv_moment,
            qkv_second,
            dense_weight,
            dense_moment,
            dense_second,
            up_weight,
            up_moment,
            up_second,
            down_weight,
            down_moment,
            down_second,
        ),
    )
    return (block_out[None], input_grad[None], *new)


def solution(mesh):
    split = P("fsdp", None)
    act = P("fsdp", "ctx", None)
    return jax.shard_map(
        body,
        mesh=mesh,
        in_specs=(act, act, split, P(), P(), P()) + (split,) * 12,
        out_specs=(act, act, P(), P(), P()) + (split,) * 12,
        check_vma=False,
    )
```

```python
import jax
import jax.numpy as jnp
from jax import lax
from jax.experimental import pallas as pl
from jax.experimental.pallas import tpu as pltpu
from jax.sharding import PartitionSpec as P

HEADS = 12
ROT = 16
STEP = 10
MESH = pl.DeviceIdType.MESH
F32 = jnp.float32
LOW = jnp.bfloat16
VMEM_LIMIT = 56 * 1024 * 1024

masked = -1e30
norm_eps = 1e-05
adam_eps = 1e-08
beta_first = 0.9
beta_second = 0.95
log2e = 1.4426950408889634


def ctx_of(y, xl, z):
    return (lax.rem(y, 4) * 2 + lax.rem(xl, 2)) * 4 + lax.rem(z, 4)


def place():
    ctx = lax.axis_index("ctx")
    fs = lax.axis_index("fsdp")
    c = lax.div(ctx, 4)
    return ctx, fs, lax.div(c, 2), lax.rem(c, 2), lax.rem(ctx, 4)


def greet(devices):
    barrier = pltpu.get_barrier_semaphore()
    for device in devices:
        pl.semaphore_signal(barrier, inc=1, device_id=device, device_id_type=MESH)
    pl.semaphore_wait(barrier, len(devices))


class Wire:
    def __init__(self, send_sem, recv_sem, local_sem):
        self.send_sem, self.recv_sem, self.local_sem = send_sem, recv_sem, local_sem
        self.sent, self.kept, self.local, self.count = [], [], 0, 0

    def send(self, src, dst, device):
        at = self.count
        self.count += 1
        copy = pltpu.make_async_remote_copy(
            src_ref=src,
            dst_ref=dst,
            send_sem=self.send_sem.at[at],
            recv_sem=self.recv_sem.at[at],
            device_id=device,
            device_id_type=MESH,
        )
        copy.start()
        self.sent.append(copy)
        return copy

    def left(self, *copies):
        for copy in copies:
            copy.wait_send()
        self.sent = [s for s in self.sent if not any(s is c for c in copies)]

    def keep(self, src, dst):
        copy = pltpu.make_async_copy(src, dst, self.local_sem.at[self.local])
        self.local += 1
        copy.start()
        self.kept.append(copy)
        return copy

    def finish(self):
        for copy in self.sent:
            copy.wait_send()
        for copy in self.kept:
            copy.wait()


def eight_peers(y, xl, z, fs):
    return [
        (ctx_of(lax.rem(y + 1, 4), xl, z), fs),
        (ctx_of(lax.rem(y + 3, 4), xl, z), fs),
        (ctx_of(y, 1 - xl, z), fs),
    ]


def erf(x):
    x = jnp.clip(x, -3.832506856900711, 3.832506856900711)
    s = x * x
    top = jnp.full_like(x, 0.00022905065861350646)
    for k in (0.0034082910107109506, 0.050955695062380861, 0.18520832239976145, 1.128379143519084):
        top = top * s + k
    low = jnp.full_like(x, -1.1791602954361697e-7)
    for k in (0.000023547966471313185, 0.0010179625278914885, 0.014070470171167667, 0.11098505178285362, 0.49746925110067538, 1.0):
        low = low * s + k
    return x * top / low


def lanes(rows, width=128):
    return lax.broadcasted_iota(jnp.int32, (rows, width), 1)


def turn(u, cos_wide, sin_wide):
    lane = lanes(u.shape[0])
    up = pltpu.roll(u, 120, 1) * jnp.where(lane < 8, -sin_wide, 0.0)
    down = pltpu.roll(u, 8, 1) * jnp.where(lane < 8, 0.0, sin_wide)
    return u * cos_wide + up + down


def angle_lanes(start, rows):
    lane = lanes(rows)
    row = lax.broadcasted_iota(jnp.int32, (rows, 128), 0)
    spot = row & 63
    for i, first in enumerate(start):
        spot = spot + jnp.where((row >> 6) == i, first, 0)
    power = (lane & 7).astype(F32) * (2.0 / ROT)
    frequency = jnp.where(lane < ROT, jnp.exp(power * -9.210340371976184), 0.0)
    angle = spot.astype(F32) * frequency
    return jnp.cos(angle), jnp.sin(angle)


class Spread:
    def __init__(self, wire, piece, out, where):
        self.wire, self.piece, self.out, self.w = wire, piece, out, where

    def around(self, slab, halves):
        w, wire = self.w, self.wire
        me = slab(w.c)
        a, b = wire.send(me, me, w.north), wire.send(me, me, w.south)
        x = wire.send(me, me, w.side)
        yield
        x.wait_recv()
        mate = slab(w.c_mate)
        p1, p2 = wire.send(mate, mate, w.north), wire.send(mate, mate, w.south)
        a.wait_recv()
        part = halves(slab(w.c_south), 0)
        h1 = wire.send(part, part, w.north)
        b.wait_recv()
        part = halves(slab(w.c_north), 1)
        h2 = wire.send(part, part, w.south)
        yield
        h1.wait_recv()
        h2.wait_recv()
        far = slab(w.c_far)
        last = wire.send(far, far, w.side)
        yield
        for copy in (p1, p2, last):
            copy.wait_recv()

    def eight_first(self):
        w, wire, out = self.w, self.wire, self.out
        width = out.shape[-1]
        cut = (width // 128 + 1) // 2 * 128
        ends = (pl.ds(0, cut), pl.ds(cut, width - cut))
        own = wire.keep(self.piece, out.at[w.z, w.c])
        own.wait()
        wire.kept = [k for k in wire.kept if k is not own]
        for _ in self.around(lambda c: out.at[w.z, c], lambda r, h: r.at[:, ends[h]]):
            yield
        mine = out.at[w.z]
        a, b = wire.send(mine, mine, w.up), wire.send(mine, mine, w.down)
        yield
        a.wait_recv()
        part = out.at[w.zm, pl.ds(0, 4)]
        h1 = wire.send(part, part, w.up)
        b.wait_recv()
        part = out.at[w.zp, pl.ds(4, 4)]
        h2 = wire.send(part, part, w.down)
        yield
        h1.wait_recv()
        h2.wait_recv()

    def ring_first(self):
        w, wire, out = self.w, self.wire, self.out
        own = wire.keep(self.piece, out.at[w.c, w.z])
        copies = [wire.send(self.piece, out.at[w.c, w.z], d) for d in (w.opposite, w.up, w.down)]
        yield
        own.wait()
        wire.kept = [k for k in wire.kept if k is not own]
        for copy in copies:
            copy.wait_recv()
        for _ in self.around(lambda c: out.at[c], lambda r, h: r.at[pl.ds(2 * h, 2)]):
            yield


class Where:
    def __init__(self):
        ctx, fs, y, xl, z = place()
        self.ctx, self.fs, self.y, self.xl, self.z = ctx, fs, y, xl, z
        self.core, self.xh = lax.rem(fs, 2), lax.div(fs, 2)
        yp, ym, yo = lax.rem(y + 1, 4), lax.rem(y + 3, 4), lax.rem(y + 2, 4)
        self.zp, self.zm, self.zo = lax.rem(z + 1, 4), lax.rem(z + 3, 4), lax.rem(z + 2, 4)
        self.c, self.c_mate = y * 2 + xl, y * 2 + 1 - xl
        self.c_north, self.c_south, self.c_far = yp * 2 + xl, ym * 2 + xl, yo * 2 + xl
        self.c_north_mate, self.c_south_mate = yp * 2 + 1 - xl, ym * 2 + 1 - xl
        self.c_far_mate = yo * 2 + 1 - xl
        self.north, self.south, self.side = eight_peers(y, xl, z, fs)
        self.up, self.down = (ctx_of(y, xl, self.zp), fs), (ctx_of(y, xl, self.zm), fs)
        self.opposite = (ctx_of(y, xl, self.zo), fs)
        self.twin = (ctx, fs + 1 - 2 * self.core)
        self.near = (ctx_of(y, 1 - xl, z), lax.rem(fs + 2, 4))
        self.plane = []
        for dh in (1, 0):
            for dy in (2, 1, 3, 0):
                for dx in (1, 0):
                    if dh or dy or dx:
                        hh = lax.rem(self.xh + dh, 2)
                        c = lax.rem(y + dy, 4) * 2 + lax.rem(xl + dx, 2)
                        self.plane.append((hh, c, (c * 4 + z, hh * 2 + self.core)))
        self.row = []
        for dh, dx in ((1, 0), (1, 1), (0, 1)):
            hh, xx = lax.rem(self.xh + dh, 2), lax.rem(xl + dx, 2)
            self.row.append((hh, xx, ((y * 2 + xx) * 4 + z, hh * 2 + self.core)))
        self.column = [(yy, (ctx_of(yy, xl, z), fs)) for yy in (yo, yp, ym)]
        self.eight = [(c, device) for hh, c, device in self.plane[8:]]


def layer_kernel(
    places, tok, cot, wqkv, wup, wdown, wdense, vec,
    or_o, ir_o, fa_o, qa_o, qb_o,
    X, G, WQ, WU, WD, WE, sq, su, sd, se, LA, LB, N, R, CS, bias,
    KVA, QGA, EC, GE, GH, SL, GU, GD, IB, SU,
    FT, FQ, FY, FX, FR, FPS,
    KP, QP0, LL, LT, raw, gap, TOPS, TOP, SUM, MIX, ACC, DKV, OUT,
    F1, MA, MB, H1, H2, MF, NF, SF,
    AT, OPB, IPB, GL, GQ, VS, EP, ET, EQ, EY, EX, ER, QP, QT, QB, QR, QPS_A, QPS_B,
    ssem, rsem, lsem, wsem,
):
    w = Where()
    wire = Wire(ssem, rsem, lsem)
    ctx, fs, y, xl, z, core = w.ctx, w.fs, w.y, w.xl, w.z, w.core
    zp, zm, zo, up, down, twin, near = w.zp, w.zm, w.zo, w.up, w.down, w.twin, w.near
    other = lax.rem(fs + 2, 4)
    parity = lax.rem(z, 2)

    load_x = pltpu.make_async_copy(tok, X.at[z], wsem.at[0])
    load_x.start()
    loads_q = []
    for t in range(3):
        for i in range(3):
            at = pl.multiple_of(t * 768 + 256 * i + 128 * lax.div(z, 2), 128)
            loads_q.append(
                pltpu.make_async_copy(
                    wqkv.at[:, pl.ds(at, 128)], sq.at[:, pl.ds((3 * t + i) * 128, 128)], wsem.at[1 + 3 * t + i]
                )
            )
    for copy in loads_q:
        copy.start()
    load_g = pltpu.make_async_copy(cot, G.at[z], wsem.at[10])
    load_g.start()
    spare = jnp.minimum(lax.rem(z + fs, 4), 2)
    load_e = pltpu.make_async_copy(wdense.at[pl.ds(pl.multiple_of(spare * 64, 64), 64)], se, wsem.at[11])
    load_e.start()
    loads_u = []
    for i in range(4):
        at = pl.multiple_of(768 * i + 192 * z - 64 * parity, 128)
        loads_u.append(
            pltpu.make_async_copy(wup.at[:, pl.ds(at, 256)], su.at[:, pl.ds(256 * i, 256)], wsem.at[12 + i])
        )
    for copy in loads_u:
        copy.start()
    load_d = pltpu.make_async_copy(wdown.at[pl.ds(pl.multiple_of(z * 192, 64), 192)], sd, wsem.at[16])
    load_d.start()

    greet([up, down, w.opposite, twin] + [device for _, _, device in w.plane])

    load_x.wait()
    x_up, x_down = wire.send(X.at[z], X.at[z], up), wire.send(X.at[z], X.at[z], down)
    for copy in loads_q:
        copy.wait()

    def piece(stage, at, odd):
        return stage[:, 128 * at + 64 * odd : 128 * at + 64 * odd + 64]

    for odd in range(2):

        @pl.when(parity == odd)
        def _():
            parts = []
            for i in range(3):
                parts += [piece(sq, 3 + i, odd), piece(sq, 6 + i, odd)]
            parts += [piece(sq, i, odd) for i in range(3)] + [jnp.zeros((192, 64), F32)]
            WQ[fs] = jnp.concatenate(parts, 1).astype(LOW)

    q_near = wire.send(WQ.at[fs], WQ.at[fs], near)
    q_twin = wire.send(WQ.at[fs], WQ.at[fs], twin)
    first = lax.div(ctx, 4) * 512
    CS[0], CS[1] = angle_lanes([places[0, first + 64 * i] for i in range(8)], 512)

    def low_block(start):
        block = places[0, start] >> 6
        return block < 32, jnp.where(block < 32, block, 63 - block)

    runs = [low_block(first + 128 * i) for i in range(4)]
    row = lax.broadcasted_iota(jnp.int32, (128, 128), 0)
    for b in range(2):
        spot = jnp.where(row < 64, runs[2 * b][1], runs[2 * b + 1][1])
        QP0[b] = spot * 64 + (row & 63)
        QP0[2 + b] = (63 - spot) * 64 + (row & 63)
    lane = lax.broadcasted_iota(jnp.int32, (8, 256), 1)
    line = lax.broadcasted_iota(jnp.int32, (8, 256), 0)
    for c in range(8):
        spot = jnp.zeros((8, 256), jnp.int32)
        for i in range(4):
            spot = jnp.where((lane >> 6) == i, low_block(512 * c + 128 * i)[1], spot)
        KP[c] = jnp.where(line == 0, spot, 63 - spot) * 64 + (lane & 63)

    gain_a, shift_a, gain_b, shift_b = (vec[i : i + 1, :] for i in range(4))

    def norms(zz):
        rows = pl.ds(pl.multiple_of(128 * zz, 128), 128)
        x = X[zz].astype(F32)
        centered = x - jnp.mean(x, -1, keepdims=True)
        inv = lax.rsqrt(jnp.mean(centered * centered, -1, keepdims=True) + norm_eps)
        normed = centered * inv
        N[rows, :] = normed
        R[rows, :] = jnp.broadcast_to(inv, (128, 128))
        LA[rows, :] = (normed * gain_a + shift_a).astype(LOW)
        LB[rows, :] = (normed * gain_b + shift_b).astype(LOW)

    norms(z)
    load_e.wait()
    WE[fs] = se[...].astype(LOW)
    for copy in loads_u:
        copy.wait()
    for odd in range(2):

        @pl.when(parity == odd)
        def _():
            parts = [su[:, 256 * i + 64 * odd : 256 * i + 64 * odd + 192] for i in range(4)]
            WU[fs] = jnp.concatenate(parts, 1).astype(LOW)

    load_d.wait()
    WD[fs] = sd[...].astype(LOW)
    load_g.wait()

    for zz in range(4):

        @pl.when(z == zz)
        def _():
            def head(row, i):
                return vec[row : row + 1, 64 * (zz + 4 * i) : 64 * (zz + 4 * i) + 64]

            parts = []
            for i in range(3):
                parts += [head(5, i), head(6, i)]
            parts += [head(4, i) for i in range(3)] + [jnp.zeros((1, 64), F32)]
            bias[0:1, 0:640] = jnp.concatenate(parts, 1)
            bias[1:2, :] = jnp.concatenate(
                [vec[8 + i : 9 + i, 192 * zz : 192 * zz + 192] for i in range(4)], 1
            )

    def relay(slab, from_down, from_up):
        from_down.wait_recv()
        part = slab.at[zm, pl.ds(0, 64)]
        a = wire.send(part, part, up)
        from_up.wait_recv()
        part = slab.at[zp, pl.ds(64, 64)]
        return [a, wire.send(part, part, down)]

    def forward(slab, copy):
        copy.wait_recv()
        return wire.send(slab.at[other], slab.at[other], twin)

    wire.left(x_up, x_down)
    g_up, g_down = wire.send(G.at[z], G.at[z], up), wire.send(G.at[z], G.at[z], down)
    x_far = relay(X, x_up, x_down)
    norms(zm)
    norms(zp)
    wire.left(q_near)
    e_near, e_twin = wire.send(WE.at[fs], WE.at[fs], near), wire.send(WE.at[fs], WE.at[fs], twin)
    u_near, u_twin = wire.send(WU.at[fs], WU.at[fs], near), wire.send(WU.at[fs], WU.at[fs], twin)
    q_far = forward(WQ, q_near)
    for copy in x_far:
        copy.wait_recv()
    norms(zo)
    g_far = relay(G, g_up, g_down)
    q_twin.wait_recv()
    q_far.wait_recv()
    low256 = lanes(256) < 64

    def arrange(value, i):
        a, b = value[:64], value[64:]
        return jnp.where(runs[i][0], a, b), jnp.where(runs[i][0], b, a)

    for t in range(2):
        rows = slice(256 * t, 256 * t + 256)
        linear = dot(LA[rows, :], WQ[...].reshape(768, 640)) + bias[0:1, 0:640]
        cos_wide, sin_wide = CS[0, rows, :], CS[1, rows, :]
        ab, last = linear[:, 384:512], linear[:, 512:640]
        for h, u in enumerate((ab, pltpu.roll(ab, 64, 1), last)):
            keys = turn(linear[:, 128 * h : 128 * h + 128], cos_wide, sin_wide)
            asks = jnp.where(low256, turn(u, cos_wide, sin_wide), 0.0)
            for i in (2 * t, 2 * t + 1):
                part = slice(128 * (i - 2 * t), 128 * (i - 2 * t) + 128)
                for half, value in enumerate(arrange(keys[part], i)):
                    at = 256 * half + 64 * i
                    KVA[w.c, h, at : at + 64, :] = value.astype(LOW)
                for half, value in enumerate(arrange(asks[part], i)):
                    at = 256 * half + 64 * i
                    QGA[at : at + 64, 128 * h : 128 * h + 128] = value.astype(LOW)

    spread = Spread(wire, None, None, w)

    def gather(h):
        return spread.around(lambda c: KVA.at[c, h], lambda r, half: r.at[pl.ds(256 * half, 256)])

    kv = [gather(h) for h in range(3)]
    next(kv[0])
    next(kv[2])
    e_far = forward(WE, e_near)
    for copy in g_far + [e_twin, e_far]:
        copy.wait_recv()
    EC[192:, :] = jnp.zeros((64, 768), LOW)
    for i in range(3):
        EC[64 * i : 64 * i + 64, :] = WE[i + jnp.where(i >= 3 - z, 1, 0)]
    for t in range(2):
        grad = dot_rows(G[pl.ds(2 * t, 2)].reshape(256, 768), EC[...])
        ab, last = grad[:, :128], grad[:, 128:]
        for h, u in enumerate((pltpu.roll(ab, 64, 1), ab, pltpu.roll(last, 64, 1))):
            for i in (2 * t, 2 * t + 1):
                part = slice(128 * (i - 2 * t), 128 * (i - 2 * t) + 128)
                for half, value in enumerate(arrange(u[part], i)):
                    at = slice(256 * half + 64 * i, 256 * half + 64 * i + 64)
                    col = slice(128 * h, 128 * h + 128)
                    QGA[at, col] = jnp.where(low256[:64], QGA[at, col], value.astype(LOW))

    next(kv[1])
    wire.left(u_near)
    d_near, d_twin = wire.send(WD.at[fs], WD.at[fs], near), wire.send(WD.at[fs], WD.at[fs], twin)
    u_far = forward(WU, u_near)
    for copy in (u_twin, u_far):
        copy.wait_recv()

    def feed_up(t):
        rows = pl.ds(256 * t, 256)
        hidden = dot(LB[rows, :], WU[...].reshape(768, 768)) + bias[1:2, :]
        half = 0.5 + 0.5 * erf(hidden * 0.7071067811865476)
        GE[rows, :] = (hidden * half).astype(LOW)
        SL[rows, :] = half + hidden * (jnp.exp(hidden * hidden * -0.5) * 0.3989422804014327)

    down_parts = ((GD, 1, 0, 64, 64, 768), (GD, 1, 64, 128, 0, 1536))
    up_parts = ((GU, 0, 0, 128, 0, 0), (GU, 0, 128, 64, 0, 768))

    def exchange(slab, k):
        copies = []
        for h in range(2):
            at = pl.multiple_of(192 * (2 * h + 1 - core), 64)
            copies.append(wire.send(slab.at[pl.ds(at, 192)], FT.at[k, h], twin))
        return copies

    def add_pair(copies, parts):
        for copy in copies:
            copy.wait_recv()
        for slab, k, row, size, to, col in parts:
            for h in range(2):
                at = pl.multiple_of(192 * (2 * h + core) + row, 64)
                for r in range(0, size, 16):
                    total = slab[pl.ds(pl.multiple_of(at + r, 16), 16), :].astype(F32) + FT[
                        k, h, row + r : row + r + 16, :
                    ].astype(F32)
                    FQ[(to + r) // 32, h, (to + r) // 16 % 2, :, col : col + 768] = total.astype(LOW)

    feed_up(0)
    next(kv[0])
    feed_up(1)
    d_far = forward(WD, d_near)
    for copy in (d_twin, d_far):
        copy.wait_recv()
    for t in range(2):
        rows = pl.ds(256 * t, 256)
        grad = G[2 * t : 2 * t + 2].reshape(256, 768)
        GH[rows, :] = (dot_rows(grad, WD[...].reshape(768, 768)) * SL[rows, :]).astype(LOW)
    next(kv[0])

    @pl.loop(0, 3)
    def _(j):
        at = pl.ds(pl.multiple_of(256 * j, 256), 256)
        GD[at, :] = dot_down(GE[:, at], G[...].reshape(512, 768)).astype(LOW)

    paired_down = exchange(GD, 1)
    next(kv[2])

    @pl.loop(0, 3)
    def _(j):
        at = pl.ds(pl.multiple_of(256 * j, 256), 256)
        GU[at, :] = dot_down(LB[:, at], GH[...]).astype(LOW)

    paired_up = exchange(GU, 0)
    next(kv[1])

    low = lanes(512) < 64
    same = (
        lax.broadcasted_iota(jnp.int32, (256, 256), 0) == lax.broadcasted_iota(jnp.int32, (256, 256), 1)
    )
    same = jnp.where(same, 1.0, 0.0).astype(LOW)
    deep = lax.broadcasted_iota(jnp.int32, (128, 256), 0) < 64

    meets = ((0,), (0,), (0, 1), (0, 1))
    spots = {}
    for b in range(4):
        for side in meets[b]:
            spots[b, side] = len(spots)

    def keys_of(c, h, side):
        return KVA[c, h, 256 * side : 256 * side + 256, :]

    def twice(value):
        return jnp.concatenate([value, value], 1)

    def begin(h):
        for b in range(4):
            part = QGA[128 * b : 128 * b + 128, 128 * h : 128 * h + 128]
            none = jnp.zeros_like(part)
            pile = jnp.concatenate(
                [jnp.where(low256[:128], part, none), jnp.where(low256[:128], none, part)], 0
            )
            LL[b] = pile
            LT[b] = dot_rows(same[:128, :128], pile).astype(LOW)
        TOP[...] = jnp.full_like(TOP, masked)
        SUM[...] = jnp.zeros_like(SUM)
        MIX[...] = jnp.zeros_like(MIX)
        ACC[...] = jnp.zeros_like(ACC)

    def score(h, shards):
        @pl.loop(*shards)
        def _(c):
            for b in range(4):
                old = TOP[b]
                top = old
                met = []
                for side in meets[b]:
                    pair = dot_rows(LL[b], keys_of(c, h, side))
                    scores = pair[:128]
                    if b < 2 or side:
                        seen = KP[c, side : side + 1, :] <= twice(QP0[b])
                        scores = jnp.where(seen, scores, masked)
                    gap[c, spots[b, side]] = pair[128:]
                    top = jnp.maximum(top, jnp.maximum(scores[:, :128], scores[:, 128:]))
                    met.append((spots[b, side], scores, pair[128:]))
                fade = jnp.exp((old - top) * 0.125)
                total, blend = SUM[b] * fade, MIX[b] * fade
                for i, scores, grads in met:
                    e = jnp.exp((scores - twice(top)) * 0.125)
                    raw[c, i] = e
                    mix = e * grads
                    total = total + (e[:, :128] + e[:, 128:])
                    blend = blend + (mix[:, :128] + mix[:, 128:])
                TOP[b] = top
                TOPS[c, b] = top
                SUM[b] = total
                MIX[b] = blend

    def weigh():
        for b in range(4):
            top = jnp.max(TOP[b], -1, keepdims=True)
            fade = jnp.exp((TOP[b] - top) * 0.125)
            inverse = 1.0 / jnp.sum(SUM[b] * fade, -1, keepdims=True)
            shared = jnp.sum(MIX[b] * fade, -1, keepdims=True) * inverse
            TOP[b] = jnp.broadcast_to(top, (128, 128))
            SUM[b] = jnp.broadcast_to(inverse, (128, 128))
            MIX[b] = jnp.broadcast_to(shared, (128, 128))

    def settle(h, shards):
        @pl.loop(*shards)
        def _(c):
            grown = [None, None]
            for b in range(4):
                total = ACC[b]
                share = twice(jnp.exp((TOPS[c, b] - TOP[b]) * 0.125) * SUM[b])
                for side in meets[b]:
                    i = spots[b, side]
                    probs = raw[c, i] * share
                    slope = probs * (gap[c, i] - twice(MIX[b]))
                    pile = jnp.concatenate([slope.astype(LOW), probs.astype(LOW)], 0)
                    total = total + dot(pile, keys_of(c, h, side))
                    part = dot(LT[b], pile)
                    grown[side] = part if grown[side] is None else grown[side] + part
                ACC[b] = total
            for side, g in enumerate(grown):
                g = jnp.where(deep, g * 0.125, g).astype(LOW)
                DKV[c, h, 256 * side : 256 * side + 256, :] = dot_rows(same, g).astype(LOW)

    def finish(h):
        done = [jnp.where(low256[:128], ACC[b, :128] * 0.125, ACC[b, 128:]) for b in range(4)]
        for i in range(4):
            at = slice(64 * (i % 2), 64 * (i % 2) + 64)
            a, b = done[i // 2][at], done[2 + i // 2][at]
            at = slice(128 * h, 128 * h + 128)
            OUT[128 * i : 128 * i + 64, at] = jnp.where(runs[i][0], a, b)
            OUT[128 * i + 64 : 128 * i + 128, at] = jnp.where(runs[i][0], b, a)

    def tree(h):
        t1 = wire.send(DKV.at[w.c_far_mate, h], F1.at[h], w.side)
        t2 = wire.send(DKV.at[w.c_north_mate, h], MA.at[h], w.north)
        t3 = wire.send(DKV.at[w.c_south_mate, h], MB.at[h], w.south)
        yield
        t1.wait_recv()
        DKV[w.c_far, h] = (DKV[w.c_far, h].astype(F32) + F1[h].astype(F32)).astype(LOW)
        t4 = wire.send(DKV.at[w.c_far, h, pl.ds(0, 256)], H1.at[h], w.south)
        t5 = wire.send(DKV.at[w.c_far, h, pl.ds(256, 256)], H2.at[h], w.north)
        t2.wait_recv()
        t3.wait_recv()
        total = DKV[w.c_mate, h].astype(F32) + MA[h].astype(F32) + MB[h].astype(F32)
        DKV[w.c_mate, h] = total.astype(LOW)
        t6 = wire.send(DKV.at[w.c_mate, h], MF.at[h], w.side)
        yield
        t4.wait_recv()
        total = DKV[w.c_south, h, 0:256, :].astype(F32) + H1[h].astype(F32)
        DKV[w.c_south, h, 0:256, :] = total.astype(LOW)
        t7 = wire.send(DKV.at[w.c_south, h], NF.at[h], w.south)
        t5.wait_recv()
        total = DKV[w.c_north, h, 256:512, :].astype(F32) + H2[h].astype(F32)
        DKV[w.c_north, h, 256:512, :] = total.astype(LOW)
        t8 = wire.send(DKV.at[w.c_north, h], SF.at[h], w.north)
        yield
        for copy in (t6, t7, t8):
            copy.wait_recv()

    def add_up(parts):
        total = parts[0].astype(F32)
        for part in parts[1:]:
            total = total + part.astype(F32)
        return total.astype(LOW)

    def ladder(packet, fy, fx, fr, out):
        copies = [wire.send(packet.at[yy], fy.at[y], device) for yy, device in w.column]
        fy[y] = packet[y]
        yield
        for copy in copies:
            copy.wait_recv()
        for h in range(2):
            for i in range(2):
                fx[h, i] = add_up([fy[j, h, i] for j in range(4)])
        me = w.xh * 2 + xl
        copies = [wire.send(fx.at[hh, xx], fr.at[me], device) for hh, xx, device in w.row]
        fr[me] = fx[w.xh, xl]
        yield
        for copy in copies:
            copy.wait_recv()
        out(add_up([fr[j] for j in range(4)]))

    def drain(steps):
        for _ in steps:
            pass

    def keep_piece(total):
        FPS[...] = total

    def keep_dense(total):
        QPS_B[:, 384:768] = total

    def arrived(copies):
        for copy in copies:
            copy.wait_recv()

    def arrived(copies):
        for copy in copies:
            copy.wait_recv()

    fl = ladder(FQ, FY, FX, FR, keep_piece)
    fa = Spread(wire, FPS, fa_o, w).eight_first()
    trees = [tree(h) for h in range(3)]
    early, late = (0, 4), (4, 8)
    drain(kv[0])
    begin(0)
    score(0, early)
    score(0, late)
    next(kv[1])
    add_pair(paired_down, down_parts)
    add_pair(paired_up, up_parts)
    next(fl)
    weigh()
    settle(0, early)
    settle(0, late)
    finish(0)
    drain(kv[1])
    begin(1)
    score(1, early)
    next(kv[2])
    score(1, late)
    next(trees[0])
    weigh()
    settle(1, early)
    next(fl)
    settle(1, late)
    finish(1)
    next(trees[0])
    drain(fl)
    next(fa)
    drain(kv[2])
    begin(2)
    score(2, early)
    next(trees[1])
    next(fa)
    score(2, late)
    next(trees[0])
    next(fa)
    weigh()
    settle(2, early)
    next(trees[1])
    next(fa)
    settle(2, late)
    next(trees[2])
    finish(2)

    o0, o1, o2 = (OUT[:, 128 * i : 128 * i + 128] for i in range(3))
    AT[:, :128] = jnp.where(low, pltpu.roll(o0, 64, 1), o1).astype(LOW)
    AT[:, 128:] = jnp.where(low, pltpu.roll(o2, 64, 1), 0.0).astype(LOW)
    ge = dot_down(AT[...], G[...].reshape(512, 768))
    for i in range(4):
        empty = 3 - z
        after = ge[64 * i - 64 : 64 * i] if i else ge[0:64]
        before = ge[64 * i : 64 * i + 64] if i < 3 else ge[128:192]
        slot = jnp.where(i > empty, after, before)
        slot = jnp.where(i == empty, 0.0, slot).astype(LOW)
        EP[i, 0:64, :] = slot[:, :384]
        EP[i, 64:128, :] = slot[:, 384:]
    paired_e = [wire.send(EP.at[2 * h + 1 - core], ET.at[h], twin) for h in range(2)]
    next(trees[1])
    SU[...] = jnp.zeros_like(SU)
    for t in range(2):
        rows = pl.ds(256 * t, 256)
        back = GH[rows, :]
        grad_ln = dot_rows(back, WU[...].reshape(768, 768))
        normed = N[rows, :]
        SU[0:1, :] += jnp.sum(grad_ln * normed, 0, keepdims=True)
        SU[1:2, :] += jnp.sum(grad_ln, 0, keepdims=True)
        SU[2:3, :] += jnp.sum(back.astype(F32), 0, keepdims=True)
        IB[rows, :] = norm_back(grad_ln, normed, R[rows, 0:1], gain_b)
    next(trees[2])
    arrived(paired_e)
    for h in range(2):
        for c in range(8):
            at = slice(16 * c, 16 * c + 16)
            EQ[c // 2, h, c % 2] = add_up([EP[2 * h + core, at, :], ET[h, at, :]])
    el = ladder(EQ, EY, EX, ER, keep_dense)
    next(el)
    for i in range(4):
        rows = slice(128 * i, 128 * i + 128)
        total = dot(GE[rows, :], WD[...].reshape(768, 768)) + dot(AT[rows, :], EC[...])
        OPB[i] = total.astype(LOW)
    ring = ((zo, w.opposite), (zp, up), (zm, down))
    o_sent = [wire.send(OPB.at[zz], or_o.at[z], device) for zz, device in ring]
    wire.keep(OPB.at[z], or_o.at[z])
    next(trees[2])

    cos_wide, sin_wide = CS[0], -CS[1]
    u0, u1, u2 = (turn(u, cos_wide, sin_wide) for u in (o0, o1, o2))
    GL[:, 384:512] = jnp.where(low, u0, pltpu.roll(u1, 64, 1)).astype(LOW)
    GL[:, 512:640] = jnp.where(low, u2, 0.0).astype(LOW)

    def own_sum(h):
        drain(trees[h])
        total = DKV[w.c, h].astype(F32) + MF[h].astype(F32) + NF[h].astype(F32) + SF[h].astype(F32)
        for i in range(4):
            a, b = total[64 * i : 64 * i + 64], total[256 + 64 * i : 320 + 64 * i]
            rows = slice(128 * i, 128 * i + 128)
            value = jnp.concatenate([jnp.where(runs[i][0], a, b), jnp.where(runs[i][0], b, a)], 0)
            value = turn(value, CS[0, rows, :], -CS[1, rows, :])
            GL[rows, 128 * h : 128 * h + 128] = value.astype(LOW)

    def project(cols):
        for t in range(2):
            rows = slice(256 * t, 256 * t + 256)
            yield rows, dot_rows(GL[rows, cols], WQ[:, :, cols].reshape(768, -1))

    def weight_part(cols):
        @pl.loop(0, 3)
        def _(j):
            at = pl.ds(pl.multiple_of(256 * j, 256), 256)
            GQ[at, cols] = dot_down(LA[:, at], GL[:, cols]).astype(LOW)

    own_sum(0)
    own_sum(1)
    for rows, value in project(slice(0, 256)):
        SL[rows, :] = value
    for rows, value in project(slice(384, 640)):
        SL[rows, :] = SL[rows, :] + value
    weight_part(slice(0, 256))
    weight_part(slice(384, 640))
    VS[...] = jnp.zeros_like(VS)

    def note(row, values):
        for j in range(values.shape[1] // 128):
            VS[6 * row + j : 6 * row + j + 1, :] = values[:, 128 * j : 128 * j + 128]

    note(2, SU[0:1, :])
    note(3, SU[1:2, :])
    note(5, SU[2:3, :])
    note(6, jnp.sum(G[z].astype(F32), 0, keepdims=True))
    next(el)
    own_sum(2)
    dots = jnp.zeros((1, 768), F32)
    plain = jnp.zeros((1, 768), F32)
    for rows, value in project(slice(256, 384)):
        grad_ln = SL[rows, :] + value
        SL[rows, :] = grad_ln
        dots = dots + jnp.sum(grad_ln * N[rows, :], 0, keepdims=True)
        plain = plain + jnp.sum(grad_ln, 0, keepdims=True)
    note(0, dots)
    note(1, plain)
    note(4, jnp.sum(GL[...].astype(F32), 0, keepdims=True))
    weight_part(slice(256, 384))
    for i in range(4):
        QP[i, :, 0:640] = GQ[192 * i : 192 * i + 128, :]
        QP[i, 0:64, 640:1024] = GQ[192 * i + 128 : 192 * i + 192, 0:384]
        QP[i, 64:128, 640:896] = GQ[192 * i + 128 : 192 * i + 192, 384:640]
        QP[i, 64:128, 896:1024] = VS[...].astype(LOW)
    paired_q = [wire.send(QP.at[2 * h + 1 - core], QT.at[h], twin) for h in range(2)]
    arrived(paired_q)
    for h in range(2):
        for c in range(8):
            at = slice(16 * c, 16 * c + 16)
            QB[h, c] = add_up([QP[2 * h + core, at, :], QT[h, at, :]])
    me = w.xh * 8 + w.c
    q_plane = [wire.send(QB.at[hh, c], QR.at[me], device) for hh, c, device in w.plane]
    QR[me] = QB[w.xh, w.c]
    for t in range(4):
        rows = slice(128 * t, 128 * t + 128)
        total = norm_back(SL[rows, :], N[rows, :], R[rows, 0:1], gain_a) + IB[rows, :]
        IPB[t] = total.astype(LOW)
    i_sent = [wire.send(IPB.at[zz], ir_o.at[z], device) for zz, device in ring]
    wire.keep(IPB.at[z], ir_o.at[z])
    next(fa)
    drain(el)
    for copy in q_plane:
        copy.wait_recv()
    total = add_up([QR[j] for j in range(16)])
    QPS_A[...] = total[:, :640]
    QPS_B[:, :384] = total[:, 640:]
    first_a = [wire.send(QPS_A, qa_o.at[z, w.c], device) for _, device in w.eight]
    first_b = [wire.send(QPS_B, qb_o.at[w.c, z], device) for _, device in ring]
    own = wire.keep(QPS_B, qb_o.at[w.c, z]), wire.keep(QPS_A, qa_o.at[z, w.c])
    for copy in own:
        copy.wait()
    wire.kept = [k for k in wire.kept if not any(k is o for o in own)]
    arrived(first_b)
    last_b = [wire.send(qb_o.at[w.c], qb_o.at[w.c], device) for _, device in w.eight]
    arrived(first_a)
    last_a = [wire.send(qa_o.at[z], qa_o.at[z], device) for _, device in ring]
    drain(fa)
    arrived(last_b + last_a)
    for copy in o_sent + i_sent:
        copy.wait_recv()
    wire.finish()


def layer(places, tok, cot, wqkv, wup, wdown, wdense, vec):
    outs = [
        ((4, 128, 768), LOW),
        ((4, 128, 768), LOW),
        ((4, 8, 16, 2304), LOW),
        ((4, 8, 16, 640), LOW),
        ((8, 4, 16, 768), LOW),
    ]
    scratch = [
        *[((4, 128, 768), LOW)] * 2,
        ((4, 192, 640), LOW),
        *[((4, 192, 768), LOW)] * 2,
        ((4, 64, 768), LOW),
        ((192, 1152), F32),
        ((192, 1024), F32),
        ((192, 768), F32),
        ((64, 768), F32),
        *[((512, 768), LOW)] * 2,
        ((512, 768), F32),
        ((512, 128), F32),
        ((2, 512, 128), F32),
        ((8, 768), F32),
        ((8, 3, 512, 128), LOW),
        ((512, 384), LOW),
        ((256, 768), LOW),
        *[((512, 768), LOW)] * 2,
        ((512, 768), F32),
        *[((768, 768), LOW)] * 2,
        ((512, 768), F32),
        ((8, 768), F32),
        ((2, 2, 192, 768), LOW),
        ((4, 2, 2, 16, 2304), LOW),
        ((4, 2, 2, 16, 2304), LOW),
        ((2, 2, 16, 2304), LOW),
        ((4, 16, 2304), LOW),
        ((16, 2304), LOW),
        ((8, 8, 256), jnp.int32),
        ((4, 128, 128), jnp.int32),
        ((4, 256, 128), LOW),
        ((4, 128, 256), LOW),
        *[((8, 6, 128, 256), F32)] * 2,
        ((8, 4, 128, 128), F32),
        *[((4, 128, 128), F32)] * 3,
        ((4, 256, 128), F32),
        ((8, 3, 512, 128), LOW),
        ((512, 384), F32),
        *[((3, 512, 128), LOW)] * 3,
        *[((3, 256, 128), LOW)] * 2,
        *[((3, 512, 128), LOW)] * 3,
        ((512, 256), LOW),
        *[((4, 128, 768), LOW)] * 2,
        ((512, 640), LOW),
        ((768, 640), LOW),
        ((64, 128), F32),
        ((4, 128, 384), LOW),
        ((2, 128, 384), LOW),
        ((4, 2, 2, 16, 384), LOW),
        ((4, 2, 2, 16, 384), LOW),
        ((2, 2, 16, 384), LOW),
        ((4, 16, 384), LOW),
        ((4, 128, 1024), LOW),
        ((2, 128, 1024), LOW),
        ((2, 8, 16, 1024), LOW),
        ((16, 16, 1024), LOW),
        ((16, 640), LOW),
        ((16, 768), LOW),
    ]
    anywhere = pl.BlockSpec(memory_space=pl.ANY)
    sends = 168
    return pl.pallas_call(
        layer_kernel,
        out_shape=[jax.ShapeDtypeStruct(s, d) for s, d in outs],
        in_specs=[pl.BlockSpec(memory_space=pltpu.SMEM)]
        + [anywhere] * 6
        + [pl.BlockSpec(memory_space=pltpu.VMEM)],
        out_specs=[anywhere] * len(outs),
        scratch_shapes=[pltpu.VMEM(s, d) for s, d in scratch]
        + [
            pltpu.SemaphoreType.DMA((sends,)),
            pltpu.SemaphoreType.DMA((sends,)),
            pltpu.SemaphoreType.DMA((16,)),
            pltpu.SemaphoreType.DMA((17,)),
        ],
        compiler_params=pltpu.CompilerParams(
            collective_id=0, has_side_effects=True, vmem_limit_bytes=60 * 1024 * 1024
        ),
    )(places, tok, cot, wqkv, wup, wdown, wdense, vec)


def step_kernel(
    spot, tok, cot, ors, irs, fa, qa, qb, vec, vec_m, vec_s,
    qw, qm, qs, ew, em, es, uw, um, us, dw, dm, ds,
    blk_o, inp_o, vw_o, vm_o, vs_o,
    qw_o, qm_o, qs_o, ew_o, em_o, es_o, uw_o, um_o, us_o, dw_o, dm_o, ds_o,
    TO, CO, OR, IR, FA, QA, QB, VW, VM, VS, QW, QM, QS, EW, EM, ES, UW, UM, US, DW, DM, DS,
    BL, IN, isem, osem,
):
    count = [0, 0]

    def start(src, dst, sem, which):
        copy = pltpu.make_async_copy(src, dst, sem.at[count[which]])
        count[which] += 1
        copy.start()
        return copy

    def arrive(pairs):
        return [start(a, b, isem, 0) for a, b in pairs]

    def cut_rows(pairs, at, size):
        return [(a.at[pl.ds(at, size)], b.at[pl.ds(at, size)]) for a, b in pairs]

    up, down = ((uw, UW), (um, UM), (us, US)), ((dw, DW), (dm, DM), (ds, DS))
    dense, qkv = ((ew, EW), (em, EM), (es, ES)), ((qw, QW), (qm, QM), (qs, QS))
    load_v = arrive(((vec, VW), (vec_m, VM), (vec_s, VS)))
    load_e = arrive(((qb, QB),) + dense)
    load_small = arrive(((tok, TO), (cot, CO), (ors, OR), (irs, IR)))
    load_u1 = arrive(((fa, FA), *cut_rows(up, 0, 128)))
    load_u2 = arrive(cut_rows(up, 128, 64))
    load_d1 = arrive(cut_rows(down, 0, 384))
    load_d2 = arrive(cut_rows(down, 384, 384))
    load_q = arrive(((qa, QA),) + tuple(cut_rows(qkv, 0, 128)))
    load_q2 = arrive(cut_rows(qkv, 128, 64))
    leaving = []

    def leave(pairs):
        leaving.extend(start(a, b, osem, 1) for a, b in pairs)

    def back_rows(pairs, at, size):
        leave((b.at[pl.ds(at, size)], a.at[pl.ds(at, size)]) for a, b in pairs)

    def wait(copies):
        for copy in copies:
            copy.wait()

    def update(slabs, rows, gradient, rate, decay):
        new = adamw(slabs[0][rows, :], slabs[1][rows, :], slabs[2][rows, :], gradient, rate, decay)
        for slab, value in zip(slabs, new):
            slab[rows, :] = value

    def rows_of(start_at, size=16):
        return pl.ds(pl.multiple_of(start_at, 16), size)

    def spread_up(parts):
        parts = [p.astype(F32) for p in parts]
        return jnp.concatenate([parts[z][:, 192 * i : 192 * i + 192] for i in range(4) for z in range(4)], 1)

    wait(load_v)
    wait(load_e)

    @pl.loop(0, 4)
    def _(c):
        for o in range(3):
            z = lax.rem(o + 4 - spot[0], 4)
            gradient = jnp.concatenate([QB[c, z, :, 384:768], QB[4 + c, z, :, 384:768]], 1).astype(F32)
            update((EW, EM, ES), rows_of(64 * o + 16 * c), gradient, 0.1, 0.1)

    leave(((EW, ew_o), (EM, em_o), (ES, es_o)))
    wait(load_small)
    BL[...] = (
        TO[...].astype(F32) + jnp.sum(OR[...].astype(F32), 0) + VW[7:8, :] + VW[12:13, :]
    ).astype(LOW)
    IN[...] = CO[...].astype(F32) + jnp.sum(IR[...].astype(F32), 0)
    leave(((BL, blk_o), (IN, inp_o)))
    wait(load_u1)

    @pl.loop(0, 8)
    def _(c):
        update((UW, UM, US), rows_of(16 * c), spread_up([FA[z, c, :, 0:768] for z in range(4)]), 0.03, 0.1)

    back_rows(((uw_o, UW), (um_o, UM), (us_o, US)), 0, 128)
    wait(load_u2)

    @pl.loop(0, 4)
    def _(c):
        gradient = spread_up([FA[z, c, :, 768:1536] for z in range(4)])
        update((UW, UM, US), rows_of(128 + 16 * c), gradient, 0.03, 0.1)

    back_rows(((uw_o, UW), (um_o, UM), (us_o, US)), 128, 64)

    for half, load in enumerate((load_d1, load_d2)):
        wait(load)

        @pl.loop(0, 8)
        def _(c):
            for z in (2 * half, 2 * half + 1):
                rows = rows_of(192 * z + 64 + 16 * c)
                update((DW, DM, DS), rows, FA[z, c, :, 1536:2304].astype(F32), 0.02, 0.1)

        @pl.loop(0, 4)
        def _(c):
            for z in (2 * half, 2 * half + 1):
                rows = rows_of(192 * z + 16 * c)
                update((DW, DM, DS), rows, FA[z, 4 + c, :, 768:1536].astype(F32), 0.02, 0.1)

        back_rows(((dw_o, DW), (dm_o, DM), (ds_o, DS)), 384 * half, 384)

    wait(load_q)
    low = lanes(16) < 64

    def spread_heads(groups):
        out = []
        for t in range(3):
            for i in range(3):
                for pair in range(2):
                    halves = []
                    for odd in range(2):
                        group = groups[2 * pair + odd]
                        if t == 0:
                            u, at = group[3 + i // 2], i % 2
                        else:
                            u, at = group[i], t - 1
                        halves.append(u if at == odd else pltpu.roll(u, 64, 1))
                    out.append(jnp.where(low, halves[0], halves[1]))
        return jnp.concatenate(out, 1)

    def cut(value):
        value = value.astype(F32)
        return [value[:, 128 * j : 128 * j + 128] for j in range(value.shape[1] // 128)]

    @pl.loop(0, 8)
    def _(c):
        groups = [cut(QA[z, c]) for z in range(4)]
        update((QW, QM, QS), rows_of(16 * c), spread_heads(groups), 0.03, 0.1)

    back_rows(((qw_o, QW), (qm_o, QM), (qs_o, QS)), 0, 128)
    wait(load_q2)

    @pl.loop(0, 4)
    def _(c):
        groups = [cut(QB[c, z, :, 0:384]) + cut(QB[4 + c, z, :, 0:256]) for z in range(4)]
        update((QW, QM, QS), rows_of(128 + 16 * c), spread_heads(groups), 0.03, 0.1)

    back_rows(((qw_o, QW), (qm_o, QM), (qs_o, QS)), 128, 64)

    notes = [QB[4:8, z, :, 256:384].astype(F32).reshape(64, 128) for z in range(4)]
    total = (notes[0] + notes[1]) + (notes[2] + notes[3])

    def line(values, row):
        return jnp.concatenate([values[6 * row + j : 6 * row + j + 1, :] for j in range(6)], 1)

    linear = [line(n, 4) for n in notes]
    heads = []
    for at in (lambda i: 384 + 64 * i, lambda i: 128 * i, lambda i: 128 * i + 64):
        heads.append(
            jnp.concatenate([linear[z][:, at(i) : at(i) + 64] for i in range(3) for z in range(4)], 1)
        )
    hidden = [line(n, 5) for n in notes]
    wide = [
        jnp.concatenate([hidden[z][:, 192 * i : 192 * i + 192] for z in range(4)], 1) for i in range(4)
    ]
    ends = line(total, 6)
    lines = [line(total, i) for i in range(4)] + heads + [ends] + wide + [ends]
    for i, gradient in enumerate(lines):
        row = slice(i, i + 1)
        update((VW, VM, VS), row, gradient, 0.2, 0.0)
    leave(((VW, vw_o), (VM, vm_o), (VS, vs_o)))
    wait(leaving)


def step(spot, small, parts, vectors, weights):
    anywhere = pl.BlockSpec(memory_space=pl.ANY)
    outs = [jax.ShapeDtypeStruct((128, 768), LOW), jax.ShapeDtypeStruct((128, 768), F32)]
    operands = [*small, *parts, *vectors, *weights]
    outs += [jax.ShapeDtypeStruct(v.shape, F32) for v in [*vectors, *weights]]
    return pl.pallas_call(
        step_kernel,
        out_shape=outs,
        in_specs=[pl.BlockSpec(memory_space=pltpu.SMEM)] + [anywhere] * len(operands),
        out_specs=[anywhere] * len(outs),
        scratch_shapes=[pltpu.VMEM(v.shape, v.dtype) for v in operands]
        + [pltpu.VMEM(o.shape, o.dtype) for o in outs[:2]]
        + [pltpu.SemaphoreType.DMA((40,)), pltpu.SemaphoreType.DMA((40,))],
        compiler_params=pltpu.CompilerParams(vmem_limit_bytes=VMEM_LIMIT),
    )(spot, *operands)


def norm_back(incoming, normed, inv_scale, gain_row):
    scaled = incoming * gain_row
    return inv_scale * (
        scaled
        - jnp.mean(scaled, -1, keepdims=True)
        - normed * jnp.mean(scaled * normed, -1, keepdims=True)
    )


def adamw(weight, moment, second, gradient, step_rate, decay_rate):
    moment_new = beta_first * moment + (1.0 - beta_first) * gradient
    second_new = beta_second * second + ((1.0 - beta_second) * gradient) * gradient
    size = jnp.sqrt(second_new * (1.0 / (1.0 - beta_second**STEP))) + adam_eps
    change = moment_new * (step_rate / (1.0 - beta_first**STEP)) / size
    return (weight * (1.0 - step_rate * decay_rate) - change, moment_new, second_new)


def dot(a, b):
    return jnp.dot(a, b, preferred_element_type=F32)


def dot_rows(a, b):
    return lax.dot_general(a, b, (((1,), (1,)), ((), ())), preferred_element_type=F32)


def dot_down(a, b):
    return lax.dot_general(a, b, (((0,), (0,)), ((), ())), preferred_element_type=F32)


def body(
    tokens,
    cotangent,
    positions,
    vectors,
    vectors_moment,
    vectors_second,
    qkv_weight,
    qkv_moment,
    qkv_second,
    dense_weight,
    dense_moment,
    dense_second,
    up_weight,
    up_moment,
    up_second,
    down_weight,
    down_moment,
    down_second,
):
    fs = lax.axis_index("fsdp")
    ors, irs, fa, qa, qb = layer(
        positions, tokens[0], cotangent[0], qkv_weight, up_weight, down_weight, dense_weight, vectors
    )
    block_out, input_grad, *new = step(
        fs.reshape(1).astype(jnp.int32),
        (tokens[0], cotangent[0], ors, irs),
        (fa, qa, qb),
        (vectors, vectors_moment, vectors_second),
        (
            qkv_weight,
            qkv_moment,
            qkv_second,
            dense_weight,
            dense_moment,
            dense_second,
            up_weight,
            up_moment,
            up_second,
            down_weight,
            down_moment,
            down_second,
        ),
    )
    return (block_out[None], input_grad[None], *new)


def solution(mesh):
    split = P("fsdp", None)
    act = P("fsdp", "ctx", None)
    return jax.shard_map(
        body,
        mesh=mesh,
        in_specs=(act, act, split, P(), P(), P()) + (split,) * 12,
        out_specs=(act, act, P(), P(), P()) + (split,) * 12,
        check_vma=False,
    )
```
